32 devices in a mesh: gz: 4 (over y, x), gx: 8 (over z, core).
Axes of the slice: x: 2, y: 2, z: 4, core: 2. Of those that a mesh axis runs over, the one named last changes fastest.
Arguments:
- populations: float32 [27, 8, 64, 128], P(None, 'gz', 'gx'), may hold values from 0 to 1, as said below
- rates: float32 [27], replicated, may hold values from 0.5 to 1.8
- grain_fraction: bfloat16 [16384, 128], P(('gz', 'gx')), may hold values from 0 to 0.3984375
- grain_velocity: bfloat16 [3, 16384], P(None, ('gz', 'gx')), may hold values from -0.29882812 to 0.29882812
- grain_dest: int32 [16384, 1], P(('gz', 'gx')), may hold values from 0 to 31; in each aligned block of 512 rows (0 to 511, 512 to 1023, ...) at most 32 rows name the same one
- grain_line: int32 [16384], P(('gz', 'gx')), may hold values from 0 to 15
Outputs:
- scaled: float32 [27, 8, 64, 128], P(None, 'gz', 'gx')
- grain_force: float32 [3, 16384], P(None, ('gz', 'gx'))
The draws below stay inside these ranges and needn't reach their ends.
Inputs may be any that keep to these rules, and one draw needn't show every extreme that they name: populations are positive. grain_dest is a linear index of gz+gx, gz slowest; among the rows of one device at most 32 name the same device, and exactly 32 do in some device's rows.
All inputs are finite; a program needn't handle non-finite values.
Results may differ from the reference program's by a relative error of at most 0.0003.
Values may be sent and summed in bfloat16 or wider, within the bound.
No kernel may reach another device: no remote copies, remote signals or barrier semaphores. Data moves between devices by JAX's collectives and lax.ppermute only.
A program may use at most 64 MiB of HBM per device.

```python
import math
import jax
import jax.numpy as jnp
import numpy as np
from jax import lax

CZ = 2
CX = 8
NY = 128
G_DEV = 512
STEPS = 2
NZ = 8
NX = 64
GRAINS = 16384
CAP = 32
N_GX = 8
DEVICES = 32


def lattice_columns():
    labels = np.arange(27)
    comp_z = (labels // 9 - 1).astype(np.float32)
    comp_x = (labels // 3 % 3 - 1).astype(np.float32)
    comp_y = (labels % 3 - 1).astype(np.float32)
    count = np.abs(labels // 9 - 1) + np.abs(labels // 3 % 3 - 1) + np.abs(labels % 3 - 1)
    weights = np.array([8.0 / 27, 2.0 / 27, 1.0 / 54, 1.0 / 216], dtype=np.float32)[count]
    return (comp_z, comp_x, comp_y, weights)


def draw_populations(key, part):
    key_density, key_speed, key_noise = jax.random.split(jax.random.fold_in(key, 11), 3)
    comp_z, comp_x, comp_y, weights = lattice_columns()
    grid = (NZ, NX, NY)
    density = 1.0 + jnp.clip(0.03 * jax.random.normal(key_density, grid, jnp.float32), -0.1, 0.1)
    speed = jnp.clip(0.06 * jax.random.normal(key_speed, (3,) + grid, jnp.float32), -0.15, 0.15)
    noise = jax.random.uniform(key_noise, (27,) + grid, jnp.float32, -0.2, 0.2)
    along = jnp.asarray(comp_z)[:, None, None, None] * speed[0][None] + jnp.asarray(comp_x)[:, None, None, None] * speed[1][None] + jnp.asarray(comp_y)[:, None, None, None] * speed[2][None]
    square = jnp.sum(speed * speed, axis=0)
    equil = jnp.asarray(weights)[:, None, None, None] * density[None] * (1.0 + 3.0 * along + 4.5 * along * along - 1.5 * square[None])
    return equil * (1.0 + noise)


def set_ends(values, key, low, largest):
    longest = values.shape.index(max(values.shape))
    spots = []
    for shift in (0, 1):
        where = [jax.random.randint(jax.random.fold_in(key, axis), (), 0, length) for axis, length in enumerate(values.shape)]
        where[longest] = (where[longest] + shift) % values.shape[longest]
        spots.append(tuple(where))
    return values.at[spots[0]].set(low).at[spots[1]].set(largest)


def levels(stream_key, shape, cuts, least, top_value):
    def one(dim, parts):
        heights = jax.random.uniform(jax.random.fold_in(jax.random.fold_in(stream_key, 6), dim), (parts,), jnp.float32, least / len(cuts), top_value / len(cuts))
        return jnp.repeat(jnp.exp(heights), shape[dim] // parts).reshape((-1,) + (1,) * (len(shape) - dim - 1))

    level = one(*cuts[0])
    for cut in cuts[1:]:
        level = level * one(*cut)
    return level


def assign_block(stream_key, own, number, rows, number_of, top, bound, skew):
    sequence = jax.random.permutation(stream_key, number_of)
    crowded, common = load_shares(number_of, rows * top, bound, skew, True), load_shares(number_of, rows * top, bound, skew, False)
    places = jnp.arange(number_of)

    def named(lengths, rotation):
        used = int((lengths > 0).sum())
        fixed = max(1, used // 4)
        shifted = fixed + (places - fixed + rotation * (used - fixed)) % max(1, number_of - fixed)
        return jnp.zeros((number_of,), jnp.int32).at[sequence[jnp.where(places < fixed, places, shifted)]].set(jnp.asarray(lengths, jnp.int32))

    lengths = jnp.where(number % 4 == 0, named(crowded, number // 4), named(common, number - number // 4 - 1))
    mixed = jax.random.permutation(jax.random.fold_in(own, 3), number_of)
    source_of, receiver = mixed[0:number_of // 2 * 2:2], mixed[1:number_of // 2 * 2:2]
    room = jnp.minimum(lengths[source_of] - 1, bound - lengths[receiver]) // 2
    room = jnp.where((source_of == sequence[0]) | (receiver == sequence[0]) | (lengths[receiver] == 0), 0, jnp.maximum(room, 0))
    shifted = jax.random.randint(jax.random.fold_in(own, 4), (number_of // 2,), 0, 1 << 20) % (room + 1)
    lengths = lengths.at[source_of].add(-shifted).at[receiver].add(shifted)
    members = jnp.searchsorted(jnp.cumsum(lengths), jnp.arange(rows * top), side="right").astype(jnp.int32)
    listing = members.reshape(top, rows).T
    listing = listing[jax.random.permutation(jax.random.fold_in(own, 1), rows)]
    rotation = jax.random.randint(jax.random.fold_in(own, 2), (rows, 1), 0, top)
    return jnp.take_along_axis(listing, (jnp.arange(top)[None, :] + rotation) % top, axis=1)


def load_shares(number_of, total, bound, skew, full):
    portions = [(1 << 20) // math.isqrt(standing ** skew) + 1 for standing in range(1, number_of + 1)]
    largest = bound if full else min(bound, max(-(-total // number_of), total * portions[0] // sum(portions)))
    least = 1 if total - largest >= number_of - 1 else 0
    given, surplus = [largest] + [least] * (number_of - 1), total - largest - least * (number_of - 1)
    while surplus > 0:
        free = [i for i in range(1, number_of) if given[i] < largest] or [i for i in range(1, number_of) if given[i] < bound]
        pool, budget = sum([portions[i] for i in free]), surplus
        for i in free:
            addition = min(bound - given[i], max(1, budget * portions[i] // pool), surplus)
            given[i] = given[i] + addition
            surplus = surplus - addition
    return np.array(given)


def gaussian(rng, shape, scale, bound, shards=(), kind=jnp.bfloat16):
    values = jax.random.normal(rng, shape, jnp.float32) * scale
    if len(shards) > 0:
        values = levels(rng, shape, shards, -0.22, 0.18) * values
    return jnp.clip(values, min=-bound, max=bound).astype(kind)


def setup_inputs(seed: int = 0) -> dict:
    key_of = jax.random.split(jax.random.key(seed), 7)
    populations = draw_populations(jax.random.fold_in(key_of[6], 71), 0)
    rates = jnp.clip(jnp.exp(jax.random.uniform(key_of[1], (27,), jnp.float32, math.log(0.5), math.log(1.8))), 0.5, 1.8)
    grain_fraction = jnp.clip(0.3984375 * jax.random.uniform(key_of[2], (GRAINS, NY), jnp.float32) ** levels(key_of[2], (GRAINS, NY), ((0, 32),), -0.2, 0.2), 0.0, 0.3984375).astype(jnp.bfloat16)
    grain_velocity = gaussian(key_of[3], (3, GRAINS), 0.1, 0.29882812, ((1, 32),))
    grain_dest_keys = jax.random.split(jax.random.fold_in(key_of[4], 1), GRAINS // G_DEV)
    grain_dest_turns = jax.random.permutation(jax.random.fold_in(key_of[4], 3), GRAINS // G_DEV)
    grain_dest = jax.vmap(lambda own, number: assign_block(jax.random.fold_in(key_of[4], 2), own, number, G_DEV, DEVICES, 1, CAP, 2))(grain_dest_keys, grain_dest_turns).reshape((GRAINS, 1))
    grain_line = set_ends(jax.random.randint(key_of[5], (GRAINS,), 0, CZ * CX), jax.random.fold_in(key_of[5], 1), 0, (CZ * CX) - 1).astype(jnp.int32)
    return {"populations": populations, "rates": rates, "grain_fraction": grain_fraction, "grain_velocity": grain_velocity, "grain_dest": grain_dest, "grain_line": grain_line}


highest = lax.Precision.HIGHEST


def lattice_tables():
    labels = np.arange(27)
    digits = [labels // 9, (labels // 3) % 3, labels % 3]
    velocity = np.stack([digit - 1 for digit in digits]).astype(np.float32)
    count = np.abs(digits[0] - 1) + np.abs(digits[1] - 1) + np.abs(digits[2] - 1)
    weights = np.array([8.0 / 27, 2.0 / 27, 1.0 / 54, 1.0 / 216], dtype=np.float32)[count]
    vander = np.array([[1.0, 1.0, 1.0], [-1.0, 0.0, 1.0], [1.0, 0.0, 1.0]], dtype=np.float32)
    vander_inv = np.array([[0.0, -0.5, 0.5], [1.0, 0.0, -1.0], [0.0, 0.5, 0.5]], dtype=np.float32)
    moments = np.ones((27, 27), dtype=np.float32)
    inverse = np.ones((27, 27), dtype=np.float32)
    for digit in digits:
        moments = moments * vander[digit[:, None], digit[None, :]]
        inverse = inverse * vander_inv[digit[:, None], digit[None, :]]
    return velocity, weights, moments, inverse


def equilibrium(density, speed, velocity, weights):
    along = jnp.dot(velocity.T, speed, precision=highest)
    square = jnp.sum(speed * speed, axis=0)
    return weights[:, None] * density[None, :] * (1.0 + 3.0 * along + 4.5 * along * along - 1.5 * square[None, :])


def collide(fields, rates, solid, carried):
    velocity_np, weights_np, moments_np, inverse_np = lattice_tables()
    velocity = jnp.asarray(velocity_np)
    weights = jnp.asarray(weights_np)
    density = jnp.sum(fields, axis=0)
    momentum = jnp.dot(velocity, fields, precision=highest)
    speed = momentum / density[None, :]
    equil = equilibrium(density, speed, velocity, weights)
    departure = fields - equil
    projected = jnp.dot(jnp.asarray(moments_np), departure, precision=highest)
    fluid = -jnp.dot(jnp.asarray(inverse_np), rates[:, None] * projected, precision=highest)
    cover = 1.0 + solid
    share = solid / cover
    solid_equil = equilibrium(density, carried / cover[None, :], velocity, weights)
    exchange_term = departure[::-1] - (fields - solid_equil)
    post = fields + (1.0 - share)[None, :] * fluid + share[None, :] * exchange_term
    push = jnp.dot(velocity, exchange_term, precision=highest) / cover[None, :]
    return post, push


def stream(post):
    depth = post.shape[1]
    rows = jnp.arange(depth)[:, None, None]
    moved_list = []
    for population in range(27):
        step_z = population // 9 - 1
        step_x = (population // 3) % 3 - 1
        step_y = population % 3 - 1
        moved = jnp.roll(post[population], (step_z, step_x, step_y), axis=(0, 1, 2))
        if step_z == 1:
            moved = jnp.where(rows == 0, post[26 - population], moved)
        if step_z == -1:
            moved = jnp.where(rows == depth - 1, post[26 - population], moved)
        moved_list.append(moved)
    return jnp.stack(moved_list)


def reference(populations, rates, grain_fraction, grain_velocity, grain_dest, grain_line):
    depth, length, width = populations.shape[1], populations.shape[2], populations.shape[3]
    target = grain_dest[:, 0]
    row_z = (target // N_GX) * CZ + grain_line // CX
    row_x = (target % N_GX) * CX + grain_line % CX
    line_id = (row_z * length + row_x).astype(jnp.int32)
    fraction = grain_fraction.astype(jnp.float32)
    speed = grain_velocity.astype(jnp.float32)
    solid = jax.ops.segment_sum(fraction, line_id, depth * length)
    carried = jnp.stack([jax.ops.segment_sum(fraction * speed[component][:, None], line_id, depth * length) for component in range(3)])
    solid_planes = solid.reshape(depth, length * width)
    carried_planes = jnp.moveaxis(carried.reshape(3, depth, length * width), 1, 0)
    fields = populations
    push_total = jnp.zeros((3, depth, length * width), jnp.float32)

    def collide_plane(items):
        plane, solid_plane, carried_plane = items
        return collide(plane, rates, solid_plane, carried_plane)

    for turn_index in range(STEPS):
        planes = jnp.moveaxis(fields.reshape(27, depth, length * width), 1, 0)
        post, push = lax.map(collide_plane, (planes, solid_planes, carried_planes))
        post = jnp.moveaxis(post, 0, 1).reshape(27, depth, length, width)
        push_total = push_total + jnp.moveaxis(push, 0, 1)
        fields = stream(post)
    weights = jnp.asarray(lattice_tables()[1])
    scaled = fields / weights[:, None, None, None]
    push_lines = push_total.reshape(3, depth * length, width)
    picked = push_lines[:, line_id, :]
    grain_force = -jnp.sum(picked * fraction[None, :, :], axis=2)
    return scaled, grain_force
```

```python
import functools

import jax
import jax.numpy as jnp
import numpy as np
from jax import lax
from jax.experimental import pallas as pl
from jax.experimental.pallas import tpu as pltpu
from jax.sharding import PartitionSpec as P

STEPS = 2
LANES = 128
f32, bf16, i32 = jnp.float32, jnp.bfloat16, jnp.int32
DIGITS = [(i // 9, i // 3 % 3, i % 3) for i in range(27)]
STEP = [tuple(d - 1 for d in digits) for digits in DIGITS]
WEIGHT = [(8.0 / 27, 2.0 / 27, 1.0 / 54, 1.0 / 216)[sum(abs(s) for s in step)] for step in STEP]


def iota(shape, dim):
    return lax.broadcasted_iota(i32, shape, dim)


def call(kernel, outs, *operands, scalars=0, flops=0):
    smem, vmem = pl.BlockSpec(memory_space=pltpu.SMEM), pl.BlockSpec(memory_space=pltpu.VMEM)
    size = sum(o.size * o.dtype.itemsize for o in operands) + sum(
        int(np.prod(o.shape)) * o.dtype.itemsize for o in outs
    )
    return pl.pallas_call(
        kernel,
        out_shape=list(outs),
        in_specs=[smem] * scalars + [vmem] * (len(operands) - scalars),
        out_specs=[vmem] * len(outs),
        compiler_params=pltpu.CompilerParams(vmem_limit_bytes=24 * 1024 * 1024),
        cost_estimate=pl.CostEstimate(flops=flops, bytes_accessed=size, transcendentals=0),
    )(*operands)


def split3(x):
    high = x.astype(bf16)
    rest = x - high.astype(f32)
    mid = rest.astype(bf16)
    return high, mid, (rest - mid.astype(f32)).astype(bf16)


def pack_kernel(devices, capacity, dest_ref, line_ref, speed_ref, fraction_ref, send_ref, rank_ref):
    grains, width = fraction_ref.shape
    slots = devices * capacity
    dest = dest_ref[...]
    hot = jnp.where(iota((devices, grains), 0) == dest, 1.0, 0.0)
    earlier = jnp.where(iota((LANES, LANES), 0) < iota((LANES, LANES), 1), 1.0, 0.0).astype(bf16)
    total = jnp.zeros((devices, 1), f32)
    ranks = []
    for start in range(0, grains, LANES):
        part = hot[:, start : start + LANES]
        before = jnp.dot(part.astype(bf16), earlier, preferred_element_type=f32) + total
        ranks.append(jnp.sum(part * before, axis=0, keepdims=True))
        total = total + jnp.sum(part, axis=1, keepdims=True)
    rank = jnp.concatenate(ranks, axis=1).astype(i32)
    rank_ref[...] = rank
    position = dest * capacity + rank
    place = jnp.where(iota((slots, grains), 0) == position, 1.0, 0.0).astype(bf16)
    rows = jnp.dot(place, fraction_ref[...], preferred_element_type=f32)
    speed = speed_ref[...].astype(f32)
    values = [speed[0:1], speed[1:2], speed[2:3], line_ref[...].astype(f32)]
    at_rank = iota((capacity, grains), 0) == rank
    facts = [jnp.where(at_rank, value, 0.0) for value in values]
    if 4 * capacity < width:
        facts.append(jnp.zeros((width - 4 * capacity, grains), f32))
    fact_rows = lax.dot_general(
        hot.astype(bf16),
        jnp.concatenate(facts, axis=0).astype(bf16),
        (((1,), (1,)), ((), ())),
        preferred_element_type=f32,
    )
    send_ref[...] = jnp.concatenate(
        [rows.reshape(devices, capacity, width), fact_rows.reshape(devices, 1, width)], axis=1
    ).astype(bf16)


def equilibrium_parts(density, speed, i):
    step = STEP[i]
    along = None
    for s, v in zip(step, speed):
        if s:
            term = v if s > 0 else -v
            along = term if along is None else along + term
    return along


def collide(fields, rate, solid, carried):
    density = functools.reduce(lambda a, b: a + b, fields)
    momentum = []
    for axis in range(3):
        plus = functools.reduce(lambda a, b: a + b, [fields[i] for i in range(27) if STEP[i][axis] == 1])
        minus = functools.reduce(lambda a, b: a + b, [fields[i] for i in range(27) if STEP[i][axis] == -1])
        momentum.append(plus - minus)
    inverse = 1.0 / density
    speed = [m * inverse for m in momentum]
    cover = 1.0 + solid
    inv_cover = 1.0 / cover
    share = solid * inv_cover
    solid_speed = [c * inv_cover for c in carried]
    base = 1.0 - 1.5 * (speed[0] * speed[0] + speed[1] * speed[1] + speed[2] * speed[2])
    solid_base = 1.0 - 1.5 * sum(v * v for v in solid_speed[1:]) - 1.5 * solid_speed[0] * solid_speed[0]
    departure, exchange = [None] * 27, [None] * 27
    for i in range(13, 27):
        j = 26 - i
        scale = WEIGHT[i] * density
        if i == 13:
            departure[13] = fields[13] - scale * base
            exchange[13] = departure[13] - (fields[13] - scale * solid_base)
            continue
        along = equilibrium_parts(density, speed, i)
        even, odd = scale * (base + 4.5 * along * along), scale * (3.0 * along)
        departure[i] = fields[i] - (even + odd)
        departure[j] = fields[j] - (even - odd)
        along = equilibrium_parts(density, solid_speed, i)
        even, odd = scale * (solid_base + 4.5 * along * along), scale * (3.0 * along)
        exchange[i] = departure[j] - (fields[i] - (even + odd))
        exchange[j] = departure[i] - (fields[j] - (even - odd))
    push = [
        (density * v - m) * inv_cover for v, m in zip(solid_speed, momentum)
    ]
    moments = list(departure)
    for stride in (1, 3, 9):
        for i in range(27):
            if i // stride % 3 == 0:
                low, mid, high = moments[i], moments[i + stride], moments[i + 2 * stride]
                both = low + high
                moments[i], moments[i + stride], moments[i + 2 * stride] = both + mid, high - low, both
    moments = [rate[a] * moments[a] for a in range(27)]
    for stride in (9, 3, 1):
        for i in range(27):
            if i // stride % 3 == 0:
                m0, m1, m2 = moments[i], moments[i + stride], moments[i + 2 * stride]
                half1, half2 = 0.5 * m1, 0.5 * m2
                moments[i], moments[i + stride], moments[i + 2 * stride] = half2 - half1, m0 - m2, half2 + half1
    keep = 1.0 - share
    post = [fields[i] - keep * moments[i] + share * exchange[i] for i in range(27)]
    return post, push


def collide_levels(read, rates_ref, held_ref, post_ref, up_ref, down_ref):
    depth, length = post_ref.shape[1], post_ref.shape[2]
    lines = depth * length
    rate = [rates_ref[a] for a in range(27)]
    pushes = []
    for z in range(depth):
        cells = lambda k: held_ref[k * lines + z * length : k * lines + (z + 1) * length, :]
        post, push = collide(read(z), rate, cells(0), [cells(1), cells(2), cells(3)])
        pushes.append(push)
        for i in range(27):
            post_ref[i, z] = post[i]
            if STEP[i][0] == 1 and z == depth - 1:
                up_ref[i - 18] = post[i]
            if STEP[i][0] == -1 and z == 0:
                down_ref[i] = post[i]
    return pushes


def first_kernel(
    capacity, rates_ref, recv_ref, fields_ref,
    post_ref, up_ref, down_ref, push_ref, held_ref, line_ref, slot_ref,
):
    devices, _, width = recv_ref.shape
    slots = devices * capacity
    depth, length = fields_ref.shape[1], fields_ref.shape[2]
    lines = depth * length
    received = recv_ref[...].astype(f32)
    slot_rows = received[:, :capacity].reshape(slots, width).astype(bf16)
    slot_ref[...] = slot_rows
    facts = received[:, capacity:].reshape(devices, width)
    group = iota((devices, width), 1) // capacity
    stacked = jnp.concatenate([jnp.where(group == m, facts, 0.0) for m in range(4)], axis=0)
    spread = jnp.where(
        iota((width, slots), 0) % capacity == iota((width, slots), 1) % capacity, 1.0, 0.0
    ).astype(bf16)
    wide = jnp.dot(stacked.astype(bf16), spread, preferred_element_type=f32)
    own = iota((devices, slots), 0) == iota((devices, slots), 1) // capacity
    fact = [
        jnp.sum(jnp.where(own, wide[m * devices : (m + 1) * devices], 0.0), axis=0, keepdims=True)
        for m in range(4)
    ]
    line_ref[...] = fact[3].astype(i32)
    on_line = iota((lines, slots), 0) == fact[3].astype(i32)
    gather = [jnp.where(on_line, 1.0, 0.0)] + [jnp.where(on_line, fact[k], 0.0) for k in range(3)]
    held_ref[...] = jnp.dot(
        jnp.concatenate(gather, axis=0).astype(bf16), slot_rows, preferred_element_type=f32
    )
    read = lambda z: [fields_ref[i, z] for i in range(27)]
    pushes = collide_levels(read, rates_ref, held_ref, post_ref, up_ref, down_ref)
    for z in range(depth):
        for k in range(3):
            push_ref[k, z] = pushes[z][k]


def ends_kernel(place_ref, post_ref, below_ref, above_ref, inner_ref, outer_ref):
    depth, length = post_ref.shape[1], post_ref.shape[2]
    even = place_ref[1] % 2 == 0

    def row(i, z, x):
        source = z - STEP[i][0]
        if source < 0:
            return below_ref[i - 18, x : x + 1]
        if source >= depth:
            return above_ref[i, x : x + 1]
        return post_ref[i, source, x : x + 1]

    for i in range(27):
        if STEP[i][1] != 1:
            continue
        j = i - 6
        for z in range(depth):
            n = ((STEP[i][0] + 1) * 3 + STEP[i][2] + 1) * depth + z
            right, left = row(i, z, length - 1), row(j, z, 0)
            inner_ref[n : n + 1] = jnp.where(even, right, left)
            outer_ref[n : n + 1] = jnp.where(even, left, right)


def streamed(place_ref, post_ref, below_ref, above_ref, inner_ref, outer_ref, z):
    depth, length, width = post_ref.shape[1:]
    even = place_ref[1] % 2 == 0
    rows = iota((length, width), 0)
    moved_list = []
    for i in range(27):
        cz, cx, cy = STEP[i]
        source = z - cz
        if source < 0:
            moved = below_ref[i - 18]
        elif source >= depth:
            moved = above_ref[i]
        else:
            moved = post_ref[i, source]
        if cx:
            n = ((cz + 1) * 3 + cy + 1) * depth + z
            inner, outer = inner_ref[n : n + 1], outer_ref[n : n + 1]
            edge = jnp.where(even, outer, inner) if cx > 0 else jnp.where(even, inner, outer)
            moved = pltpu.roll(moved, cx % length, 0)
            moved = jnp.where(rows == (0 if cx > 0 else length - 1), edge, moved)
        if cy:
            moved = pltpu.roll(moved, cy % width, 1)
        if source < 0:
            moved = jnp.where(place_ref[0] == 0, post_ref[26 - i, z], moved)
        elif source >= depth:
            moved = jnp.where(place_ref[0] == place_ref[2] - 1, post_ref[26 - i, z], moved)
        moved_list.append(moved)
    return moved_list


def second_kernel(
    capacity, place_ref, rates_ref, post_ref, below_ref, above_ref, inner_ref, outer_ref,
    held_ref, push_ref, line_ref, slot_ref, next_ref, up_ref, down_ref, force_ref,
):
    depth, length, width = post_ref.shape[1:]
    lines = depth * length
    slots = slot_ref.shape[0]
    halo = (below_ref, above_ref, inner_ref, outer_ref)
    read = lambda z: streamed(place_ref, post_ref, *halo, z)
    pushes = collide_levels(read, rates_ref, held_ref, next_ref, up_ref, down_ref)
    total = jnp.concatenate(
        [push_ref[k, z] + pushes[z][k] for k in range(3) for z in range(depth)], axis=0
    )
    along = lax.dot_general(
        jnp.concatenate(split3(total), axis=0),
        slot_ref[...],
        (((1,), (1,)), ((), ())),
        preferred_element_type=f32,
    )
    along = along[: 3 * lines] + along[3 * lines : 6 * lines] + along[6 * lines :]
    on_line = iota((lines, slots), 0) == line_ref[...]
    tiles, per_tile = slots // LANES, LANES // capacity
    group = iota((tiles, LANES), 1) // capacity
    force = []
    for k in range(3):
        picked = -jnp.sum(jnp.where(on_line, along[k * lines : (k + 1) * lines], 0.0), axis=0, keepdims=True)
        force.append(
            jnp.concatenate([picked[:, t * LANES : (t + 1) * LANES] for t in range(tiles)], axis=0)
        )
    for a in range(per_tile):
        block = jnp.zeros((tiles, LANES), f32)
        for k in range(3):
            shift = (k - a) * capacity % LANES
            turned = pltpu.roll(force[k], shift, 1) if shift else force[k]
            block = jnp.where(group == k, turned, block)
        force_ref[pl.ds(a, tiles, stride=per_tile), :] = block


def last_kernel(place_ref, post_ref, below_ref, above_ref, inner_ref, outer_ref, scaled_ref):
    for z in range(post_ref.shape[1]):
        halo = (below_ref, above_ref, inner_ref, outer_ref)
        fields = streamed(place_ref, post_ref, *halo, z)
        for i in range(27):
            scaled_ref[i, z] = fields[i] * (1.0 / WEIGHT[i])


def unpack_kernel(capacity, dest_ref, rank_ref, back_ref, force_ref):
    devices, grains = back_ref.shape[0], dest_ref.shape[1]
    hot = jnp.where(iota((devices, grains), 0) == dest_ref[...], 1.0, 0.0).astype(bf16)
    parts = jnp.concatenate([part.astype(f32) for part in split3(back_ref[...])], axis=1).T
    picked = jnp.dot(parts.astype(bf16), hot, preferred_element_type=f32)
    picked = picked[:LANES] + picked[LANES : 2 * LANES] + picked[2 * LANES :]
    at_rank = iota((capacity, grains), 0) == rank_ref[...]
    for k in range(3):
        mine = jnp.where(at_rank, picked[k * capacity : (k + 1) * capacity], 0.0)
        force_ref[k : k + 1] = jnp.sum(mine, axis=0, keepdims=True)


def exchange_halo(place, post, up, down):
    peers, length = lax.axis_size("gz"), lax.axis_size("gx")
    below = lax.ppermute(up, "gz", [(i, (i + 1) % peers) for i in range(peers)])
    above = lax.ppermute(down, "gz", [((i + 1) % peers, i) for i in range(peers)])
    depth, width = post.shape[1], post.shape[3]
    ends = jax.ShapeDtypeStruct((9 * depth, width), f32)
    inner, outer = call(ends_kernel, [ends, ends], place, post, below, above, scalars=1)
    inner = lax.ppermute(inner, "gx", [(i, i ^ 1) for i in range(length)])
    outer = lax.ppermute(
        outer, "gx", [(i, (i + 1) % length if i % 2 else (i - 1) % length) for i in range(length)]
    )
    return below, above, inner, outer


def per_device(populations, rates, grain_fraction, grain_velocity, grain_dest, grain_line):
    _, depth, length, width = populations.shape
    lines = depth * length
    devices = lax.axis_size("gz") * lax.axis_size("gx")
    grains = grain_fraction.shape[0]
    capacity = 2 * grains // devices
    slots = devices * capacity
    shape = jax.ShapeDtypeStruct
    dest, line = grain_dest.reshape(1, grains), grain_line.reshape(1, grains)
    place = jnp.stack(
        [lax.axis_index("gz"), lax.axis_index("gx"), jnp.int32(lax.axis_size("gz"))]
    ).astype(i32)
    send, rank = call(
        functools.partial(pack_kernel, devices, capacity),
        [shape((devices, capacity + 1, width), bf16), shape((1, grains), i32)],
        dest, line, grain_velocity, grain_fraction,
    )
    recv = lax.all_to_all(send, ("gz", "gx"), split_axis=0, concat_axis=0, tiled=True)
    state = shape(populations.shape, f32)
    face = shape((9, length, width), f32)
    post, up, down, push, held, slot_line, slot_rows = call(
        functools.partial(first_kernel, capacity),
        [
            state, face, face, shape((3, depth, length, width), f32),
            shape((4 * lines, width), f32), shape((1, slots), i32), shape((slots, width), bf16),
        ],
        rates, recv, populations, scalars=1,
    )
    halo = exchange_halo(place, post, up, down)
    post, up, down, slot_force = call(
        functools.partial(second_kernel, capacity),
        [state, face, face, shape((devices, LANES), f32)],
        place, rates, post, *halo, held, push, slot_line, slot_rows, scalars=2,
    )
    back = lax.all_to_all(slot_force, ("gz", "gx"), split_axis=0, concat_axis=0, tiled=True)
    halo = exchange_halo(place, post, up, down)
    (scaled,) = call(last_kernel, [state], place, post, *halo, scalars=1)
    (grain_force,) = call(
        functools.partial(unpack_kernel, capacity), [shape((3, grains), f32)], dest, rank, back
    )
    return (scaled, grain_force)


def solution(mesh):
    in_specs = (
        P(None, "gz", "gx", None),
        P(),
        P(("gz", "gx"), None),
        P(None, ("gz", "gx")),
        P(("gz", "gx"), None),
        P(("gz", "gx")),
    )
    out_specs = (P(None, "gz", "gx", None), P(None, ("gz", "gx")))
    return jax.shard_map(
        per_device, mesh=mesh, in_specs=in_specs, out_specs=out_specs, check_vma=False
    )
```

```python
import functools

import jax
import jax.numpy as jnp
import numpy as np
from jax import lax
from jax.experimental import pallas as pl
from jax.experimental.pallas import tpu as pltpu
from jax.sharding import PartitionSpec as P

STEPS = 2
LANES = 128
f32, bf16, i32 = jnp.float32, jnp.bfloat16, jnp.int32
DIGITS = [(i // 9, i // 3 % 3, i % 3) for i in range(27)]
STEP = [tuple(d - 1 for d in digits) for digits in DIGITS]
WEIGHT = [(8.0 / 27, 2.0 / 27, 1.0 / 54, 1.0 / 216)[sum(abs(s) for s in step)] for step in STEP]


def iota(shape, dim):
    return lax.broadcasted_iota(i32, shape, dim)


def call(kernel, outs, *operands, smem=(), hbm=(), scratch=(), flops=0, vmem=24):
    space = [pltpu.SMEM if n in smem else pltpu.HBM if n in hbm else pltpu.VMEM for n in range(len(operands))]
    size = sum(o.size * o.dtype.itemsize for o in operands) + sum(
        int(np.prod(o.shape)) * o.dtype.itemsize for o in outs
    )
    return pl.pallas_call(
        kernel,
        out_shape=list(outs),
        in_specs=[pl.BlockSpec(memory_space=where) for where in space],
        out_specs=[pl.BlockSpec(memory_space=pltpu.VMEM)] * len(outs),
        scratch_shapes=list(scratch),
        compiler_params=pltpu.CompilerParams(vmem_limit_bytes=vmem * 1024 * 1024),
        cost_estimate=pl.CostEstimate(flops=flops, bytes_accessed=size, transcendentals=0),
    )(*operands)


def device_at(step_z, step_x):
    depth, length = lax.axis_size("gz"), lax.axis_size("gx")
    z = lax.rem(lax.axis_index("gz") + step_z + depth, depth)
    x = lax.rem(lax.axis_index("gx") + step_x + length, length)
    return z * length + x


def split3(x):
    high = x.astype(bf16)
    rest = x - high.astype(f32)
    mid = rest.astype(bf16)
    return high, mid, (rest - mid.astype(f32)).astype(bf16)


def pack_kernel(devices, capacity, *refs):
    sources, (send_ref, rank_ref), held, sem = refs[:4], refs[4:6], refs[6:10], refs[10]
    copies = [pltpu.make_async_copy(sources[n], held[n], sem.at[n]) for n in range(4)]
    for copy in copies:
        copy.start()
    dest_ref, line_ref, speed_ref, fraction_ref = held
    grains, width = fraction_ref.shape
    slots = devices * capacity
    copies[0].wait()
    dest = dest_ref[...]
    hot = jnp.where(iota((devices, grains), 0) == dest, 1.0, 0.0)
    earlier = jnp.where(iota((LANES, LANES), 0) < iota((LANES, LANES), 1), 1.0, 0.0).astype(bf16)
    total = jnp.zeros((devices, 1), f32)
    ranks = []
    for start in range(0, grains, LANES):
        part = hot[:, start : start + LANES]
        before = jnp.dot(part.astype(bf16), earlier, preferred_element_type=f32) + total
        ranks.append(jnp.sum(part * before, axis=0, keepdims=True))
        total = total + jnp.sum(part, axis=1, keepdims=True)
    rank = jnp.concatenate(ranks, axis=1).astype(i32)
    rank_ref[...] = rank
    position = dest * capacity + rank
    place = jnp.where(iota((slots, grains), 0) == position, 1.0, 0.0).astype(bf16)
    copies[3].wait()
    rows = jnp.dot(place, fraction_ref[...], preferred_element_type=f32)
    copies[1].wait()
    copies[2].wait()
    speed = speed_ref[...].astype(f32)
    values = [speed[0:1], speed[1:2], speed[2:3], line_ref[...].astype(f32)]
    at_rank = iota((capacity, grains), 0) == rank
    facts = [jnp.where(at_rank, value, 0.0) for value in values]
    if 4 * capacity < width:
        facts.append(jnp.zeros((width - 4 * capacity, grains), f32))
    fact_rows = lax.dot_general(
        hot.astype(bf16),
        jnp.concatenate(facts, axis=0).astype(bf16),
        (((1,), (1,)), ((), ())),
        preferred_element_type=f32,
    )
    send_ref[...] = jnp.concatenate(
        [rows.reshape(devices, capacity, width), fact_rows.reshape(devices, 1, width)], axis=1
    ).astype(bf16)


def equilibrium_parts(density, speed, i):
    step = STEP[i]
    along = None
    for s, v in zip(step, speed):
        if s:
            term = v if s > 0 else -v
            along = term if along is None else along + term
    return along


def collide(fields, rate, solid, carried):
    density = functools.reduce(lambda a, b: a + b, fields)
    momentum = []
    for axis in range(3):
        plus = functools.reduce(lambda a, b: a + b, [fields[i] for i in range(27) if STEP[i][axis] == 1])
        minus = functools.reduce(lambda a, b: a + b, [fields[i] for i in range(27) if STEP[i][axis] == -1])
        momentum.append(plus - minus)
    inverse = 1.0 / density
    speed = [m * inverse for m in momentum]
    cover = 1.0 + solid
    inv_cover = 1.0 / cover
    share = solid * inv_cover
    solid_speed = [c * inv_cover for c in carried]
    base = 1.0 - 1.5 * (speed[0] * speed[0] + speed[1] * speed[1] + speed[2] * speed[2])
    solid_base = 1.0 - 1.5 * sum(v * v for v in solid_speed[1:]) - 1.5 * solid_speed[0] * solid_speed[0]
    departure, exchange = [None] * 27, [None] * 27
    for i in range(13, 27):
        j = 26 - i
        scale = WEIGHT[i] * density
        if i == 13:
            departure[13] = fields[13] - scale * base
            exchange[13] = departure[13] - (fields[13] - scale * solid_base)
            continue
        along = equilibrium_parts(density, speed, i)
        even, odd = scale * (base + 4.5 * along * along), scale * (3.0 * along)
        departure[i] = fields[i] - (even + odd)
        departure[j] = fields[j] - (even - odd)
        along = equilibrium_parts(density, solid_speed, i)
        even, odd = scale * (solid_base + 4.5 * along * along), scale * (3.0 * along)
        exchange[i] = departure[j] - (fields[i] - (even + odd))
        exchange[j] = departure[i] - (fields[j] - (even - odd))
    push = [
        (density * v - m) * inv_cover for v, m in zip(solid_speed, momentum)
    ]
    moments = list(departure)
    for stride in (1, 3, 9):
        for i in range(27):
            if i // stride % 3 == 0:
                low, mid, high = moments[i], moments[i + stride], moments[i + 2 * stride]
                both = low + high
                moments[i], moments[i + stride], moments[i + 2 * stride] = both + mid, high - low, both
    moments = [rate[a] * moments[a] for a in range(27)]
    for stride in (9, 3, 1):
        for i in range(27):
            if i // stride % 3 == 0:
                m0, m1, m2 = moments[i], moments[i + stride], moments[i + 2 * stride]
                half1, half2 = 0.5 * m1, 0.5 * m2
                moments[i], moments[i + stride], moments[i + 2 * stride] = half2 - half1, m0 - m2, half2 + half1
    keep = 1.0 - share
    post = [fields[i] - keep * moments[i] + share * exchange[i] for i in range(27)]
    return post, push


def collide_levels(read, rates_ref, held_ref, post_ref, up_ref, down_ref):
    depth, length = post_ref.shape[1], post_ref.shape[2]
    lines = depth * length
    rate = [rates_ref[a] for a in range(27)]
    pushes = []
    for z in range(depth):
        cells = lambda k: held_ref[k * lines + z * length : k * lines + (z + 1) * length, :]
        post, push = collide(read(z), rate, cells(0), [cells(1), cells(2), cells(3)])
        pushes.append(push)
        for i in range(27):
            post_ref[i, z] = post[i]
            if STEP[i][0] == 1 and z == depth - 1:
                up_ref[i - 18] = post[i]
            if STEP[i][0] == -1 and z == 0:
                down_ref[i] = post[i]
    return pushes


def first_kernel(
    capacity, rates_ref, recv_ref, fields_ref,
    post_ref, up_ref, down_ref, push_ref, held_ref, line_ref, slot_ref,
):
    devices, _, width = recv_ref.shape
    slots = devices * capacity
    depth, length = fields_ref.shape[1], fields_ref.shape[2]
    lines = depth * length
    received = recv_ref[...].astype(f32)
    slot_rows = received[:, :capacity].reshape(slots, width).astype(bf16)
    slot_ref[...] = slot_rows
    facts = received[:, capacity:].reshape(devices, width)
    group = iota((devices, width), 1) // capacity
    stacked = jnp.concatenate([jnp.where(group == m, facts, 0.0) for m in range(4)], axis=0)
    spread = jnp.where(
        iota((width, slots), 0) % capacity == iota((width, slots), 1) % capacity, 1.0, 0.0
    ).astype(bf16)
    wide = jnp.dot(stacked.astype(bf16), spread, preferred_element_type=f32)
    own = iota((devices, slots), 0) == iota((devices, slots), 1) // capacity
    fact = [
        jnp.sum(jnp.where(own, wide[m * devices : (m + 1) * devices], 0.0), axis=0, keepdims=True)
        for m in range(4)
    ]
    line_ref[...] = fact[3].astype(i32)
    on_line = iota((lines, slots), 0) == fact[3].astype(i32)
    gather = [jnp.where(on_line, 1.0, 0.0)] + [jnp.where(on_line, fact[k], 0.0) for k in range(3)]
    held_ref[...] = jnp.dot(
        jnp.concatenate(gather, axis=0).astype(bf16), slot_rows, preferred_element_type=f32
    )
    read = lambda z: [fields_ref[i, z] for i in range(27)]
    pushes = collide_levels(read, rates_ref, held_ref, post_ref, up_ref, down_ref)
    for z in range(depth):
        for k in range(3):
            push_ref[k, z] = pushes[z][k]


def ends_kernel(post_ref, below_ref, above_ref, inner_ref, outer_ref):
    depth, length = post_ref.shape[1], post_ref.shape[2]
    even = lax.axis_index("gx") % 2 == 0

    def row(i, z, x):
        source = z - STEP[i][0]
        if source < 0:
            return below_ref[i - 18, x : x + 1]
        if source >= depth:
            return above_ref[i, x : x + 1]
        return post_ref[i, source, x : x + 1]

    for i in range(27):
        if STEP[i][1] != 1:
            continue
        j = i - 6
        for z in range(depth):
            n = end_row(i, z, depth)
            right, left = row(i, z, length - 1), row(j, z, 0)
            inner_ref[n : n + 1] = jnp.where(even, right, left)
            outer_ref[n : n + 1] = jnp.where(even, left, right)


def end_row(i, z, depth):
    return ((STEP[i][0] + 1) * 3 + STEP[i][2] + 1) * depth + z


def streamed(post_ref, below_ref, above_ref, inner_ref, outer_ref, z, back_ref=None):
    depth, length, width = post_ref.shape[1:]
    even = lax.axis_index("gx") % 2 == 0
    rows = iota((length, width), 0)
    moved_list = []
    for i in range(27):
        cz, cx, cy = STEP[i]
        source = z - cz
        inside = 0 <= source < depth
        if source < 0:
            moved = below_ref[i - 18]
        elif source >= depth:
            moved = above_ref[i]
        else:
            moved = post_ref[i, source]
        if cx:
            n = end_row(i, z, depth)
            inner, outer = inner_ref[n : n + 1], outer_ref[n : n + 1]
            edge = jnp.where(even, outer, inner) if cx > 0 else jnp.where(even, inner, outer)
            if not inside and back_ref is not None:
                edge = back_ref[pl.ds(4 * device_at(-cz, -cx) + 2 + cy, 1)]
            moved = pltpu.roll(moved, cx % length, 0)
            moved = jnp.where(rows == (0 if cx > 0 else length - 1), edge, moved)
        if cy:
            moved = pltpu.roll(moved, cy % width, 1)
        if source < 0:
            moved = jnp.where(lax.axis_index("gz") == 0, post_ref[26 - i, z], moved)
        elif source >= depth:
            top = lax.axis_size("gz") - 1
            moved = jnp.where(lax.axis_index("gz") == top, post_ref[26 - i, z], moved)
        moved_list.append(moved)
    return moved_list


def second_kernel(
    capacity, rates_ref, post_ref, below_ref, above_ref, inner_ref, outer_ref,
    held_ref, push_ref, line_ref, slot_ref,
    next_ref, up_ref, down_ref, next_inner_ref, next_outer_ref, back_ref, right_ref, left_ref,
):
    depth, length, width = post_ref.shape[1:]
    lines = depth * length
    slots = slot_ref.shape[0]
    halo = (below_ref, above_ref, inner_ref, outer_ref)
    read = lambda z: streamed(post_ref, *halo, z)
    pushes = collide_levels(read, rates_ref, held_ref, next_ref, up_ref, down_ref)
    back_ref[...] = jnp.zeros(back_ref.shape, f32)
    right_ref[...] = jnp.zeros(right_ref.shape, f32)
    left_ref[...] = jnp.zeros(left_ref.shape, f32)
    for i in range(27):
        cz, cx, cy = STEP[i]
        if cx == 0:
            continue
        x = length - 1 if cx > 0 else 0
        face_ref = right_ref if cx > 0 else left_ref
        for z in range(depth):
            if 0 <= z - cz < depth:
                n = end_row(i, z, depth)
                face_ref[n : n + 1] = next_ref[i, z - cz, x : x + 1]
        if cz:
            z = depth - 1 if cz > 0 else 0
            back_ref[pl.ds(4 * device_at(cz, cx) + 2 + cy, 1)] = next_ref[i, z, x : x + 1]
    even = lax.axis_index("gx") % 2 == 0
    right, left = right_ref[...], left_ref[...]
    next_inner_ref[...] = jnp.where(even, right, left)
    next_outer_ref[...] = jnp.where(even, left, right)
    total = jnp.concatenate(
        [push_ref[k, z] + pushes[z][k] for k in range(3) for z in range(depth)], axis=0
    )
    along = lax.dot_general(
        jnp.concatenate(split3(total), axis=0),
        slot_ref[...],
        (((1,), (1,)), ((), ())),
        preferred_element_type=f32,
    )
    along = along[: 3 * lines] + along[3 * lines : 6 * lines] + along[6 * lines :]
    on_line = iota((lines, slots), 0) == line_ref[...]
    tiles, per_tile = slots // LANES, LANES // capacity
    group = iota((tiles, LANES), 1) // capacity
    force = []
    for k in range(3):
        picked = -jnp.sum(jnp.where(on_line, along[k * lines : (k + 1) * lines], 0.0), axis=0, keepdims=True)
        force.append(
            jnp.concatenate([picked[:, t * LANES : (t + 1) * LANES] for t in range(tiles)], axis=0)
        )
    for a in range(per_tile):
        block = jnp.zeros((tiles, LANES), f32)
        for k in range(3):
            shift = (k - a) * capacity % LANES
            turned = pltpu.roll(force[k], shift, 1) if shift else force[k]
            block = jnp.where(group == k, turned, block)
        back_ref[pl.ds(4 * a, tiles, stride=4 * per_tile), :] = block


def last_kernel(post_ref, below_ref, above_ref, inner_ref, outer_ref, back_ref, scaled_ref):
    for z in range(post_ref.shape[1]):
        halo = (below_ref, above_ref, inner_ref, outer_ref)
        fields = streamed(post_ref, *halo, z, back_ref)
        for i in range(27):
            scaled_ref[i, z] = fields[i] * (1.0 / WEIGHT[i])


def unpack_kernel(capacity, dest_ref, rank_ref, back_ref, force_ref):
    devices, grains = back_ref.shape[0] // 4, dest_ref.shape[1]
    hot = jnp.where(iota((devices, grains), 0) == dest_ref[...], 1.0, 0.0).astype(bf16)
    back = back_ref[pl.ds(0, devices, stride=4), :]
    parts = jnp.concatenate([part.astype(f32) for part in split3(back)], axis=1).T
    picked = jnp.dot(parts.astype(bf16), hot, preferred_element_type=f32)
    picked = picked[:LANES] + picked[LANES : 2 * LANES] + picked[2 * LANES :]
    at_rank = iota((capacity, grains), 0) == rank_ref[...]
    for k in range(3):
        mine = jnp.where(at_rank, picked[k * capacity : (k + 1) * capacity], 0.0)
        force_ref[k : k + 1] = jnp.sum(mine, axis=0, keepdims=True)


def swap_faces(up, down):
    peers = lax.axis_size("gz")
    below = lax.ppermute(up, "gz", [(i, (i + 1) % peers) for i in range(peers)])
    above = lax.ppermute(down, "gz", [((i + 1) % peers, i) for i in range(peers)])
    return below, above


def swap_ends(inner, outer):
    length = lax.axis_size("gx")
    inner = lax.ppermute(inner, "gx", [(i, i ^ 1) for i in range(length)])
    outer = lax.ppermute(
        outer, "gx", [(i, (i + 1) % length if i % 2 else (i - 1) % length) for i in range(length)]
    )
    return inner, outer


def per_device(populations, rates, grain_fraction, grain_velocity, grain_dest, grain_line):
    _, depth, length, width = populations.shape
    lines = depth * length
    devices = lax.axis_size("gz") * lax.axis_size("gx")
    grains = grain_fraction.shape[0]
    capacity = 2 * grains // devices
    slots = devices * capacity
    shape = jax.ShapeDtypeStruct
    dest, line = grain_dest.reshape(1, grains), grain_line.reshape(1, grains)
    inputs = (dest, line, grain_velocity, grain_fraction)
    send, rank = call(
        functools.partial(pack_kernel, devices, capacity),
        [shape((devices, capacity + 1, width), bf16), shape((1, grains), i32)],
        *inputs,
        hbm=range(4), vmem=60,
        scratch=[pltpu.VMEM(x.shape, x.dtype) for x in inputs] + [pltpu.SemaphoreType.DMA((4,))],
    )
    recv = lax.all_to_all(send, ("gz", "gx"), split_axis=0, concat_axis=0, tiled=True)
    state = shape(populations.shape, f32)
    face, ends = shape((9, length, width), f32), shape((9 * depth, width), f32)
    post, up, down, push, held, slot_line, slot_rows = call(
        functools.partial(first_kernel, capacity),
        [
            state, face, face, shape((3, depth, length, width), f32),
            shape((4 * lines, width), f32), shape((1, slots), i32), shape((slots, width), bf16),
        ],
        rates, recv, populations, smem=(0,),
    )
    below, above = swap_faces(up, down)
    inner, outer = swap_ends(*call(ends_kernel, [ends, ends], post, below, above))
    post, up, down, inner, outer, back = call(
        functools.partial(second_kernel, capacity),
        [state, face, face, ends, ends, shape((4 * devices, LANES), f32)],
        rates, post, below, above, inner, outer, held, push, slot_line, slot_rows,
        smem=(0,), scratch=[pltpu.VMEM(ends.shape, f32)] * 2,
    )
    back = lax.all_to_all(
        back.reshape(devices, 4, LANES), ("gz", "gx"), split_axis=0, concat_axis=0, tiled=True
    ).reshape(4 * devices, LANES)
    below, above = swap_faces(up, down)
    inner, outer = swap_ends(inner, outer)
    (grain_force,) = call(
        functools.partial(unpack_kernel, capacity), [shape((3, grains), f32)], dest, rank, back
    )
    (scaled,) = call(last_kernel, [state], post, below, above, inner, outer, back)
    return (scaled, grain_force)


def solution(mesh):
    in_specs = (
        P(None, "gz", "gx", None),
        P(),
        P(("gz", "gx"), None),
        P(None, ("gz", "gx")),
        P(("gz", "gx"), None),
        P(("gz", "gx")),
    )
    out_specs = (P(None, "gz", "gx", None), P(None, ("gz", "gx")))
    return jax.shard_map(
        per_device, mesh=mesh, in_specs=in_specs, out_specs=out_specs, check_vma=False
    )
```

```python
import functools

import jax
import jax.numpy as jnp
import numpy as np
from jax import lax
from jax.experimental import pallas as pl
from jax.experimental.pallas import tpu as pltpu
from jax.sharding import PartitionSpec as P

STEPS = 2
LANES = 128
f32, bf16, i32 = jnp.float32, jnp.bfloat16, jnp.int32
DIGITS = [(i // 9, i // 3 % 3, i % 3) for i in range(27)]
STEP = [tuple(d - 1 for d in digits) for digits in DIGITS]
WEIGHT = [(8.0 / 27, 2.0 / 27, 1.0 / 54, 1.0 / 216)[sum(abs(s) for s in step)] for step in STEP]


def iota(shape, dim):
    return lax.broadcasted_iota(i32, shape, dim)


def call(kernel, outs, *operands, smem=(), hbm=(), hbm_out=(), scratch=(), vmem=24):
    space = [pltpu.SMEM if n in smem else pltpu.HBM if n in hbm else pltpu.VMEM for n in range(len(operands))]
    size = sum(o.size * o.dtype.itemsize for o in operands) + sum(
        int(np.prod(o.shape)) * o.dtype.itemsize for o in outs
    )
    return pl.pallas_call(
        kernel,
        out_shape=list(outs),
        in_specs=[pl.BlockSpec(memory_space=where) for where in space],
        out_specs=[
            pl.BlockSpec(memory_space=pltpu.HBM if n in hbm_out else pltpu.VMEM) for n in range(len(outs))
        ],
        scratch_shapes=list(scratch),
        compiler_params=pltpu.CompilerParams(vmem_limit_bytes=vmem * 1024 * 1024),
        cost_estimate=pl.CostEstimate(flops=0, bytes_accessed=size, transcendentals=0),
    )(*operands)


def device_at(step_z, step_x):
    depth, length = lax.axis_size("gz"), lax.axis_size("gx")
    z = lax.rem(lax.axis_index("gz") + step_z + depth, depth)
    x = lax.rem(lax.axis_index("gx") + step_x + length, length)
    return z * length + x


def split3(x):
    high = x.astype(bf16)
    rest = x - high.astype(f32)
    mid = rest.astype(bf16)
    return high, mid, (rest - mid.astype(f32)).astype(bf16)


def pack_kernel(devices, capacity, parts, *refs):
    sources, (send_ref, rank_ref), held = refs[:4], refs[4:6], refs[6:10]
    staged_ref, rows_ref, sem, out_sem = refs[10:]
    copies = [pltpu.make_async_copy(sources[n], held[n], sem.at[n]) for n in range(4)]
    for copy in copies:
        copy.start()
    dest_ref, line_ref, speed_ref, fraction_ref = held
    grains, width = fraction_ref.shape
    block = capacity + 2
    copies[0].wait()
    dest = dest_ref[...]
    hot = jnp.where(iota((devices, grains), 0) == dest, 1.0, 0.0)
    earlier = jnp.where(iota((LANES, LANES), 0) < iota((LANES, LANES), 1), 1.0, 0.0).astype(bf16)
    total = jnp.zeros((devices, 1), f32)
    ranks = []
    for start in range(0, grains, LANES):
        part = hot[:, start : start + LANES]
        before = jnp.dot(part.astype(bf16), earlier, preferred_element_type=f32) + total
        ranks.append(jnp.sum(part * before, axis=0, keepdims=True))
        total = total + jnp.sum(part, axis=1, keepdims=True)
    rank = jnp.concatenate(ranks, axis=1).astype(i32)
    rank_ref[...] = rank
    position = dest * block + rank
    copies[1].wait()
    copies[2].wait()
    speed = speed_ref[...].astype(f32)
    values = [speed[0:1], speed[1:2], speed[2:3], line_ref[...].astype(f32)]
    at_rank = iota((capacity, grains), 0) == rank
    facts = [jnp.where(at_rank, value, 0.0) for value in values]
    if 4 * capacity < width:
        facts.append(jnp.zeros((width - 4 * capacity, grains), f32))
    fact_rows = lax.dot_general(
        hot.astype(bf16),
        jnp.concatenate(facts, axis=0).astype(bf16),
        (((1,), (1,)), ((), ())),
        preferred_element_type=f32,
    )
    copies[3].wait()
    fraction = fraction_ref[...]
    size, some = devices * block // parts, devices // parts
    out = []
    for n in range(parts):
        place = jnp.where(iota((size, grains), 0) == position - n * size, 1.0, 0.0).astype(bf16)
        rows_ref[n] = jnp.dot(place, fraction, preferred_element_type=f32)
        rows_ref[n, pl.ds(capacity, some, stride=block), :] = fact_rows[n * some : (n + 1) * some]
        staged_ref[n * size : (n + 1) * size] = rows_ref[n].astype(bf16)
        rows = pl.ds(n * size, size)
        out.append(pltpu.make_async_copy(staged_ref.at[rows], send_ref.at[rows], out_sem.at[n]))
        out[n].start()
    for copy in out:
        copy.wait()


def total_of(values):
    return functools.reduce(lambda a, b: a + b, values)


def along(speed, i):
    return total_of([v if s > 0 else -v for s, v in zip(STEP[i], speed) if s])


def relax(fields, rate):
    density = total_of(fields)
    momentum = [
        total_of([fields[i] for i in range(27) if STEP[i][axis] == 1])
        - total_of([fields[i] for i in range(27) if STEP[i][axis] == -1])
        for axis in range(3)
    ]
    inverse = 1.0 / density
    speed = [m * inverse for m in momentum]
    base = 1.0 - 1.5 * total_of([v * v for v in speed])
    departure = [None] * 27
    for i in range(13, 27):
        scale = WEIGHT[i] * density
        if i == 13:
            departure[i] = fields[i] - scale * base
            continue
        dot = along(speed, i)
        even, odd = scale * (base + 4.5 * dot * dot), scale * (3.0 * dot)
        departure[i] = fields[i] - (even + odd)
        departure[26 - i] = fields[26 - i] - (even - odd)
    moments = list(departure)
    for stride in (1, 3, 9):
        for i in range(27):
            if i // stride % 3 == 0:
                low, mid, high = moments[i], moments[i + stride], moments[i + 2 * stride]
                both = low + high
                moments[i], moments[i + stride], moments[i + 2 * stride] = both + mid, high - low, both
    moments = [rate[a] * moments[a] for a in range(27)]
    for stride in (9, 3, 1):
        for i in range(27):
            if i // stride % 3 == 0:
                m0, m1, m2 = moments[i], moments[i + stride], moments[i + 2 * stride]
                half1, half2 = 0.5 * m1, 0.5 * m2
                moments[i], moments[i + stride], moments[i + 2 * stride] = half2 - half1, m0 - m2, half2 + half1
    kept = [fields[i] - moments[i] for i in range(27)]
    swapped = [departure[26 - i] - kept[i] for i in range(27)]
    return density, momentum, kept, swapped


def exchange(density, momentum, kept, swapped, solid, carried):
    inverse = 1.0 / (1.0 + solid)
    share = solid * inverse
    speed = [c * inverse for c in carried]
    base = 1.0 - 1.5 * total_of([v * v for v in speed])
    push = [(density * v - m) * inverse for v, m in zip(speed, momentum)]
    post = [None] * 27
    for i in range(13, 27):
        scale = WEIGHT[i] * density
        if i == 13:
            post[i] = kept[i] + share * (swapped[i] + scale * base)
            continue
        dot = along(speed, i)
        even, odd = scale * (base + 4.5 * dot * dot), scale * (3.0 * dot)
        post[i] = kept[i] + share * (swapped[i] + (even + odd))
        post[26 - i] = kept[26 - i] + share * (swapped[26 - i] + (even - odd))
    return post, push


def grains_at(held_ref, z, depth, length):
    lines = depth * length
    first = [held_ref[k * lines + z * length : k * lines + (z + 1) * length, :] for k in range(4)]
    return first[0], first[1:]


def store_post(post, z, post_ref, up_ref, down_ref):
    for i in range(27):
        post_ref[i, z] = post[i]
        if STEP[i][0] == 1 and z == post_ref.shape[1] - 1:
            up_ref[i - 18] = post[i]
        if STEP[i][0] == -1 and z == 0:
            down_ref[i] = post[i]


def relax_kernel(rates_ref, fields_ref, kept_ref, swapped_ref, sums_ref):
    rate = [rates_ref[a] for a in range(27)]
    for z in range(fields_ref.shape[1]):
        density, momentum, kept, swapped = relax([fields_ref[i, z] for i in range(27)], rate)
        for n, value in enumerate([density] + momentum):
            sums_ref[n, z] = value
        for i in range(27):
            kept_ref[i, z] = kept[i]
            swapped_ref[i, z] = swapped[i]


def first_kernel(
    devices, capacity, recv_ref, kept_ref, swapped_ref, sums_ref,
    post_ref, up_ref, down_ref, push_ref, held_ref, line_ref, slot_ref, wide_ref,
):
    width = recv_ref.shape[1]
    block, slots = capacity + 2, devices * capacity
    depth, length = kept_ref.shape[1], kept_ref.shape[2]
    lines = depth * length
    wide_ref[...] = recv_ref[...].astype(f32)
    facts = wide_ref[pl.ds(capacity, devices, stride=block), :]
    slot_rows = jnp.concatenate(
        [wide_ref[j * block : j * block + capacity] for j in range(devices)], axis=0
    ).astype(bf16)
    slot_ref[...] = slot_rows
    group = iota((devices, width), 1) // capacity
    stacked = jnp.concatenate([jnp.where(group == m, facts, 0.0) for m in range(4)], axis=0)
    spread = jnp.where(
        iota((width, slots), 0) % capacity == iota((width, slots), 1) % capacity, 1.0, 0.0
    ).astype(bf16)
    wide = jnp.dot(stacked.astype(bf16), spread, preferred_element_type=f32)
    own = iota((devices, slots), 0) == iota((devices, slots), 1) // capacity
    fact = [
        jnp.sum(jnp.where(own, wide[m * devices : (m + 1) * devices], 0.0), axis=0, keepdims=True)
        for m in range(4)
    ]
    line_ref[...] = fact[3].astype(i32)
    on_line = iota((lines, slots), 0) == fact[3].astype(i32)
    gather = [jnp.where(on_line, 1.0, 0.0)] + [jnp.where(on_line, fact[k], 0.0) for k in range(3)]
    held_ref[...] = jnp.dot(
        jnp.concatenate(gather, axis=0).astype(bf16), slot_rows, preferred_element_type=f32
    )
    for z in range(depth):
        sums = [sums_ref[n, z] for n in range(4)]
        kept, swapped = [kept_ref[i, z] for i in range(27)], [swapped_ref[i, z] for i in range(27)]
        grains = grains_at(held_ref, z, depth, length)
        post, push = exchange(sums[0], sums[1:], kept, swapped, *grains)
        store_post(post, z, post_ref, up_ref, down_ref)
        for k in range(3):
            push_ref[k, z] = push[k]


def turn_kernel(slot_ref, dest_ref, rank_ref, turned_ref, hot_ref, at_rank_ref):
    turned_ref[...] = slot_ref[...].astype(f32).T.astype(bf16)
    hot_ref[...] = jnp.where(iota(hot_ref.shape, 0) == dest_ref[...], 1.0, 0.0).astype(bf16)
    at_rank_ref[...] = jnp.where(iota(at_rank_ref.shape, 0) == rank_ref[...], 1.0, 0.0)


def ends_kernel(post_ref, below_ref, above_ref, inner_ref, outer_ref):
    depth, length = post_ref.shape[1], post_ref.shape[2]
    even = lax.axis_index("gx") % 2 == 0

    def row(i, z, x):
        source = z - STEP[i][0]
        if source < 0:
            return below_ref[i - 18, x : x + 1]
        if source >= depth:
            return above_ref[i, x : x + 1]
        return post_ref[i, source, x : x + 1]

    for i in range(27):
        if STEP[i][1] != 1:
            continue
        j = i - 6
        for z in range(depth):
            n = end_row(i, z, depth)
            right, left = row(i, z, length - 1), row(j, z, 0)
            inner_ref[n : n + 1] = jnp.where(even, right, left)
            outer_ref[n : n + 1] = jnp.where(even, left, right)


def end_row(i, z, depth):
    return ((STEP[i][0] + 1) * 3 + STEP[i][2] + 1) * depth + z


def streamed(post_ref, below_ref, above_ref, inner_ref, outer_ref, z, back_ref=None, part=range(27)):
    depth, length, width = post_ref.shape[1:]
    even = lax.axis_index("gx") % 2 == 0
    rows = iota((length, width), 0)
    moved_list = []
    for i in part:
        cz, cx, cy = STEP[i]
        source = z - cz
        inside = 0 <= source < depth
        if source < 0:
            moved = below_ref[i - 18]
        elif source >= depth:
            moved = above_ref[i]
        else:
            moved = post_ref[i, source]
        if cx:
            n = end_row(i, z, depth)
            inner, outer = inner_ref[n : n + 1], outer_ref[n : n + 1]
            edge = jnp.where(even, outer, inner) if cx > 0 else jnp.where(even, inner, outer)
            if not inside and back_ref is not None:
                edge = back_ref[pl.ds(4 * device_at(-cz, -cx) + 2 + cy, 1)]
            moved = pltpu.roll(moved, cx % length, 0)
            moved = jnp.where(rows == (0 if cx > 0 else length - 1), edge, moved)
        if cy:
            moved = pltpu.roll(moved, cy % width, 1)
        if source < 0:
            moved = jnp.where(lax.axis_index("gz") == 0, post_ref[26 - i, z], moved)
        elif source >= depth:
            top = lax.axis_size("gz") - 1
            moved = jnp.where(lax.axis_index("gz") == top, post_ref[26 - i, z], moved)
        moved_list.append(moved)
    return moved_list


def second_kernel(
    capacity, rates_ref, post_ref, below_ref, above_ref, inner_ref, outer_ref,
    held_ref, push_ref, line_ref, turned_ref,
    next_ref, up_ref, down_ref, next_inner_ref, next_outer_ref, back_ref, right_ref, left_ref,
):
    depth, length, width = post_ref.shape[1:]
    lines = depth * length
    slots = turned_ref.shape[1]
    halo = (below_ref, above_ref, inner_ref, outer_ref)
    rate = [rates_ref[a] for a in range(27)]
    pushes = []
    for z in range(depth):
        relaxed = relax(streamed(post_ref, *halo, z), rate)
        post, push = exchange(*relaxed, *grains_at(held_ref, z, depth, length))
        store_post(post, z, next_ref, up_ref, down_ref)
        pushes.append(push)
    back_ref[...] = jnp.zeros(back_ref.shape, f32)
    right_ref[...] = jnp.zeros(right_ref.shape, f32)
    left_ref[...] = jnp.zeros(left_ref.shape, f32)
    for i in range(27):
        cz, cx, cy = STEP[i]
        if cx == 0:
            continue
        x = length - 1 if cx > 0 else 0
        face_ref = right_ref if cx > 0 else left_ref
        for z in range(depth):
            if 0 <= z - cz < depth:
                n = end_row(i, z, depth)
                face_ref[n : n + 1] = next_ref[i, z - cz, x : x + 1]
        if cz:
            z = depth - 1 if cz > 0 else 0
            back_ref[pl.ds(4 * device_at(cz, cx) + 2 + cy, 1)] = next_ref[i, z, x : x + 1]
    even = lax.axis_index("gx") % 2 == 0
    right, left = right_ref[...], left_ref[...]
    next_inner_ref[...] = jnp.where(even, right, left)
    next_outer_ref[...] = jnp.where(even, left, right)
    total = jnp.concatenate(
        [push_ref[k, z] + pushes[z][k] for k in range(3) for z in range(depth)], axis=0
    )
    along_y = jnp.dot(
        jnp.concatenate(split3(total), axis=0), turned_ref[...], preferred_element_type=f32
    )
    along_y = along_y[: 3 * lines] + along_y[3 * lines : 6 * lines] + along_y[6 * lines :]
    on_line = iota((lines, slots), 0) == line_ref[...]
    tiles, per_tile = slots // LANES, LANES // capacity
    group = iota((tiles, LANES), 1) // capacity
    force = []
    for k in range(3):
        picked = -jnp.sum(jnp.where(on_line, along_y[k * lines : (k + 1) * lines], 0.0), axis=0, keepdims=True)
        force.append(
            jnp.concatenate([picked[:, t * LANES : (t + 1) * LANES] for t in range(tiles)], axis=0)
        )
    for a in range(per_tile):
        block = jnp.zeros((tiles, LANES), f32)
        for k in range(3):
            shift = (k - a) * capacity % LANES
            turned = pltpu.roll(force[k], shift, 1) if shift else force[k]
            block = jnp.where(group == k, turned, block)
        back_ref[pl.ds(4 * a, tiles, stride=4 * per_tile), :] = block


def last_kernel(
    capacity, post_ref, below_ref, above_ref, inner_ref, outer_ref, back_ref, hot_ref, at_rank_ref,
    scaled_ref, force_ref, staged_ref, sem,
):
    depth = post_ref.shape[1]
    halo = (below_ref, above_ref, inner_ref, outer_ref)
    copies = []
    for cz in (0, 1, -1):
        part = [i for i in range(27) if STEP[i][0] == cz]
        for z in range(depth):
            for i, field in zip(part, streamed(post_ref, *halo, z, back_ref, part)):
                staged_ref[i, z] = field * (1.0 / WEIGHT[i])
        rows = pl.ds(part[0], len(part))
        copies.append(pltpu.make_async_copy(staged_ref.at[rows], scaled_ref.at[rows], sem.at[cz + 1]))
        copies[-1].start()
    back = back_ref[pl.ds(0, hot_ref.shape[0], stride=4), :]
    parts = jnp.concatenate([part.astype(f32) for part in split3(back)], axis=1).T
    picked = jnp.dot(parts.astype(bf16), hot_ref[...], preferred_element_type=f32)
    picked = picked[:LANES] + picked[LANES : 2 * LANES] + picked[2 * LANES :]
    for k in range(3):
        mine = at_rank_ref[...] * picked[k * capacity : (k + 1) * capacity]
        force_ref[k : k + 1] = jnp.sum(mine, axis=0, keepdims=True)
    for copy in copies:
        copy.wait()


def swap_faces(up, down):
    peers = lax.axis_size("gz")
    below = lax.ppermute(up, "gz", [(i, (i + 1) % peers) for i in range(peers)])
    above = lax.ppermute(down, "gz", [((i + 1) % peers, i) for i in range(peers)])
    return below, above


def swap_ends(inner, outer):
    length = lax.axis_size("gx")
    inner = lax.ppermute(inner, "gx", [(i, i ^ 1) for i in range(length)])
    outer = lax.ppermute(
        outer, "gx", [(i, (i + 1) % length if i % 2 else (i - 1) % length) for i in range(length)]
    )
    return inner, outer


def per_device(populations, rates, grain_fraction, grain_velocity, grain_dest, grain_line):
    _, depth, length, width = populations.shape
    lines = depth * length
    devices = lax.axis_size("gz") * lax.axis_size("gx")
    grains = grain_fraction.shape[0]
    capacity = 2 * grains // devices
    slots = devices * capacity
    shape, both = jax.ShapeDtypeStruct, ("gz", "gx")
    dest, line = grain_dest.reshape(1, grains), grain_line.reshape(1, grains)
    inputs, rows, parts = (dest, line, grain_velocity, grain_fraction), devices * (capacity + 2), 4
    send, rank = call(
        functools.partial(pack_kernel, devices, capacity, parts),
        [shape((rows, width), bf16), shape((1, grains), i32)],
        *inputs,
        hbm=range(4),
        hbm_out=(0,),
        scratch=[pltpu.VMEM(x.shape, x.dtype) for x in inputs]
        + [pltpu.VMEM((rows, width), bf16), pltpu.VMEM((parts, rows // parts, width), f32)]
        + [pltpu.SemaphoreType.DMA((n,)) for n in (4, parts)],
        vmem=60,
    )
    recv = lax.all_to_all(
        send.reshape(devices, capacity // 2 + 1, 2, width), both, split_axis=0, concat_axis=0, tiled=True
    ).reshape(rows, width)
    state, sums = shape(populations.shape, f32), shape((4, depth, length, width), f32)
    face, ends = shape((9, length, width), f32), shape((9 * depth, width), f32)
    kept, swapped, sums = call(relax_kernel, [state, state, sums], rates, populations, smem=(0,))
    post, up, down, push, held, slot_line, slot_rows = call(
        functools.partial(first_kernel, devices, capacity),
        [
            state, face, face, shape((3, depth, length, width), f32),
            shape((4 * lines, width), f32), shape((1, slots), i32), shape((slots, width), bf16),
        ],
        recv, kept, swapped, sums, scratch=[pltpu.VMEM((rows, width), f32)],
    )
    below, above = swap_faces(up, down)
    turned, hot, at_rank = call(
        turn_kernel,
        [shape((width, slots), bf16), shape((devices, grains), bf16), shape((capacity, grains), f32)],
        slot_rows, dest, rank,
    )
    inner, outer = swap_ends(*call(ends_kernel, [ends, ends], post, below, above))
    post, up, down, inner, outer, back = call(
        functools.partial(second_kernel, capacity),
        [state, face, face, ends, ends, shape((4 * devices, LANES), f32)],
        rates, post, below, above, inner, outer, held, push, slot_line, turned,
        smem=(0,), scratch=[pltpu.VMEM(ends.shape, f32)] * 2,
    )
    back = lax.all_to_all(
        back.reshape(devices, 4, LANES), both, split_axis=0, concat_axis=0, tiled=True
    ).reshape(4 * devices, LANES)
    below, above = swap_faces(up, down)
    inner, outer = swap_ends(inner, outer)
    scaled, grain_force = call(
        functools.partial(last_kernel, capacity),
        [state, shape((3, grains), f32)],
        post, below, above, inner, outer, back, hot, at_rank,
        hbm_out=(0,), scratch=[pltpu.VMEM(state.shape, f32), pltpu.SemaphoreType.DMA((3,))],
    )
    return (scaled, grain_force)


def solution(mesh):
    in_specs = (
        P(None, "gz", "gx", None),
        P(),
        P(("gz", "gx"), None),
        P(None, ("gz", "gx")),
        P(("gz", "gx"), None),
        P(("gz", "gx")),
    )
    out_specs = (P(None, "gz", "gx", None), P(None, ("gz", "gx")))
    return jax.shard_map(
        per_device, mesh=mesh, in_specs=in_specs, out_specs=out_specs, check_vma=False
    )
```

```python
import functools

import jax
import jax.numpy as jnp
import numpy as np
from jax import lax
from jax.experimental import pallas as pl
from jax.experimental.pallas import tpu as pltpu
from jax.sharding import PartitionSpec as P

STEPS = 2
LANES = 128
f32, bf16, i32 = jnp.float32, jnp.bfloat16, jnp.int32
DIGITS = [(i // 9, i // 3 % 3, i % 3) for i in range(27)]
STEP = [tuple(d - 1 for d in digits) for digits in DIGITS]
WEIGHT = [(8.0 / 27, 2.0 / 27, 1.0 / 54, 1.0 / 216)[sum(abs(s) for s in step)] for step in STEP]


def iota(shape, dim):
    return lax.broadcasted_iota(i32, shape, dim)


def call(kernel, outs, *operands, smem=(), scratch=(), flops=0):
    size = sum(o.size * o.dtype.itemsize for o in operands) + sum(
        int(np.prod(o.shape)) * o.dtype.itemsize for o in outs
    )
    return pl.pallas_call(
        kernel,
        out_shape=list(outs),
        in_specs=[
            pl.BlockSpec(memory_space=pltpu.SMEM if n in smem else pltpu.VMEM) for n in range(len(operands))
        ],
        out_specs=[pl.BlockSpec(memory_space=pltpu.VMEM)] * len(outs),
        scratch_shapes=list(scratch),
        compiler_params=pltpu.CompilerParams(vmem_limit_bytes=24 * 1024 * 1024),
        cost_estimate=pl.CostEstimate(flops=flops, bytes_accessed=size, transcendentals=0),
    )(*operands)


def device_at(step_z, step_x):
    depth, length = lax.axis_size("gz"), lax.axis_size("gx")
    z = lax.rem(lax.axis_index("gz") + step_z + depth, depth)
    x = lax.rem(lax.axis_index("gx") + step_x + length, length)
    return z * length + x


def split3(x):
    high = x.astype(bf16)
    rest = x - high.astype(f32)
    mid = rest.astype(bf16)
    return high, mid, (rest - mid.astype(f32)).astype(bf16)


def tables_kernel(capacity, earlier_ref, spread_ref, own_ref):
    width, slots = spread_ref.shape
    order = iota(earlier_ref.shape, 0) < iota(earlier_ref.shape, 1)
    earlier_ref[...] = jnp.where(order, 1.0, 0.0).astype(bf16)
    same = iota((width, slots), 0) % capacity == iota((width, slots), 1) % capacity
    spread_ref[...] = jnp.where(same, 1.0, 0.0).astype(bf16)
    own_ref[...] = jnp.where(iota(own_ref.shape, 0) == iota(own_ref.shape, 1) // capacity, 1.0, 0.0)


def ranks(hot, earlier):
    devices, grains = hot.shape
    total = jnp.zeros((devices, 1), f32)
    parts = []
    for start in range(0, grains, LANES):
        part = hot[:, start : start + LANES]
        before = jnp.dot(part.astype(bf16), earlier, preferred_element_type=f32) + total
        parts.append(jnp.sum(part * before, axis=0, keepdims=True))
        total = total + jnp.sum(part, axis=1, keepdims=True)
    return jnp.concatenate(parts, axis=1)


def pack_kernel(devices, capacity, dest_ref, line_ref, speed_ref, fraction_ref, earlier_ref, send_ref, rows_ref):
    grains, width = fraction_ref.shape
    block = capacity + 2
    dest = dest_ref[...]
    hot = jnp.where(iota((devices, grains), 0) == dest, 1.0, 0.0)
    rank = ranks(hot, earlier_ref[...]).astype(i32)
    speed = speed_ref[...].astype(f32)
    values = [speed[0:1], speed[1:2], speed[2:3], line_ref[...].astype(f32)]
    at_rank = iota((capacity, grains), 0) == rank
    facts = [jnp.where(at_rank, value, 0.0) for value in values]
    if 4 * capacity < width:
        facts.append(jnp.zeros((width - 4 * capacity, grains), f32))
    fact_rows = lax.dot_general(
        hot.astype(bf16),
        jnp.concatenate(facts, axis=0).astype(bf16),
        (((1,), (1,)), ((), ())),
        preferred_element_type=f32,
    )
    place = jnp.where(iota((devices * block, grains), 0) == dest * block + rank, 1.0, 0.0).astype(bf16)
    rows_ref[...] = jnp.dot(place, fraction_ref[...], preferred_element_type=f32)
    rows_ref[pl.ds(capacity, devices, stride=block), :] = fact_rows
    send_ref[...] = rows_ref[...].astype(bf16)


def total_of(values):
    return functools.reduce(lambda a, b: a + b, values)


def along(speed, i):
    return total_of([v if s > 0 else -v for s, v in zip(STEP[i], speed) if s])


def relax(fields, rate):
    density = total_of(fields)
    momentum = [
        total_of([fields[i] for i in range(27) if STEP[i][axis] == 1])
        - total_of([fields[i] for i in range(27) if STEP[i][axis] == -1])
        for axis in range(3)
    ]
    inverse = 1.0 / density
    speed = [m * inverse for m in momentum]
    base = 1.0 - 1.5 * total_of([v * v for v in speed])
    departure = [None] * 27
    for i in range(13, 27):
        scale = WEIGHT[i] * density
        if i == 13:
            departure[i] = fields[i] - scale * base
            continue
        dot = along(speed, i)
        even, odd = scale * (base + 4.5 * dot * dot), scale * (3.0 * dot)
        departure[i] = fields[i] - (even + odd)
        departure[26 - i] = fields[26 - i] - (even - odd)
    moments = list(departure)
    for stride in (1, 3, 9):
        for i in range(27):
            if i // stride % 3 == 0:
                low, mid, high = moments[i], moments[i + stride], moments[i + 2 * stride]
                both = low + high
                moments[i], moments[i + stride], moments[i + 2 * stride] = both + mid, high - low, both
    moments = [rate[a] * moments[a] for a in range(27)]
    for stride in (9, 3, 1):
        for i in range(27):
            if i // stride % 3 == 0:
                m0, m1, m2 = moments[i], moments[i + stride], moments[i + 2 * stride]
                half1, half2 = 0.5 * m1, 0.5 * m2
                moments[i], moments[i + stride], moments[i + 2 * stride] = half2 - half1, m0 - m2, half2 + half1
    kept = [fields[i] - moments[i] for i in range(27)]
    swapped = [departure[26 - i] - kept[i] for i in range(27)]
    return density, momentum, kept, swapped


def exchange(density, momentum, kept, swapped, solid, carried):
    inverse = 1.0 / (1.0 + solid)
    share = solid * inverse
    speed = [c * inverse for c in carried]
    base = 1.0 - 1.5 * total_of([v * v for v in speed])
    push = [(density * v - m) * inverse for v, m in zip(speed, momentum)]
    post = [None] * 27
    for i in range(13, 27):
        scale = WEIGHT[i] * density
        if i == 13:
            post[i] = kept[i] + share * (swapped[i] + scale * base)
            continue
        dot = along(speed, i)
        even, odd = scale * (base + 4.5 * dot * dot), scale * (3.0 * dot)
        post[i] = kept[i] + share * (swapped[i] + (even + odd))
        post[26 - i] = kept[26 - i] + share * (swapped[26 - i] + (even - odd))
    return post, push


def grains_at(held_ref, z, depth, length):
    lines = depth * length
    first = [held_ref[k * lines + z * length : k * lines + (z + 1) * length, :] for k in range(4)]
    return first[0], first[1:]


def even_place(axis):
    return lax.axis_index(axis) % 2 == 0


def store_faces(post_ref, near_ref, far_ref):
    top = post_ref.shape[1] - 1
    for n in range(9):
        up, down = post_ref[n + 18, top], post_ref[n, 0]
        near_ref[n] = jnp.where(even_place("gz"), up, down)
        far_ref[n] = jnp.where(even_place("gz"), down, up)


def across(near_ref, far_ref, i, x=slice(None)):
    n = i % 9
    if STEP[i][0] > 0:
        return jnp.where(even_place("gz"), far_ref[n, x], near_ref[n, x])
    return jnp.where(even_place("gz"), near_ref[n, x], far_ref[n, x])


def relax_kernel(rates_ref, fields_ref, kept_ref, swapped_ref, sums_ref, rate_rows_ref):
    rate = [rates_ref[a] for a in range(27)]
    for a in range(27):
        rate_rows_ref[a : a + 1] = jnp.full((1, rate_rows_ref.shape[1]), rate[a], f32)
    for z in range(fields_ref.shape[1]):
        density, momentum, kept, swapped = relax([fields_ref[i, z] for i in range(27)], rate)
        for n, value in enumerate([density] + momentum):
            sums_ref[n, z] = value
        for i in range(27):
            kept_ref[i, z] = kept[i]
            swapped_ref[i, z] = swapped[i]


def first_kernel(
    devices, capacity, recv_ref, kept_ref, swapped_ref, sums_ref, spread_ref, own_ref,
    post_ref, near_ref, far_ref, push_ref, held_ref, line_ref, slot_ref, wide_ref,
):
    width = recv_ref.shape[1]
    block, slots = capacity + 2, devices * capacity
    depth, length = kept_ref.shape[1], kept_ref.shape[2]
    lines = depth * length
    wide_ref[...] = recv_ref[...].astype(f32)
    facts = wide_ref[pl.ds(capacity, devices, stride=block), :]
    slot_rows = jnp.concatenate(
        [wide_ref[j * block : j * block + capacity] for j in range(devices)], axis=0
    ).astype(bf16)
    slot_ref[...] = slot_rows
    group = iota((devices, width), 1) // capacity
    stacked = jnp.concatenate([jnp.where(group == m, facts, 0.0) for m in range(4)], axis=0)
    wide = jnp.dot(stacked.astype(bf16), spread_ref[...], preferred_element_type=f32)
    own = own_ref[...]
    fact = [
        jnp.sum(own * wide[m * devices : (m + 1) * devices], axis=0, keepdims=True) for m in range(4)
    ]
    line_ref[...] = fact[3].astype(i32)
    on_line = iota((lines, slots), 0) == fact[3].astype(i32)
    gather = [jnp.where(on_line, 1.0, 0.0)] + [jnp.where(on_line, fact[k], 0.0) for k in range(3)]
    held_ref[...] = jnp.dot(
        jnp.concatenate(gather, axis=0).astype(bf16), slot_rows, preferred_element_type=f32
    )
    for z in range(depth):
        sums = [sums_ref[n, z] for n in range(4)]
        kept, swapped = [kept_ref[i, z] for i in range(27)], [swapped_ref[i, z] for i in range(27)]
        grains = grains_at(held_ref, z, depth, length)
        post, push = exchange(sums[0], sums[1:], kept, swapped, *grains)
        for i in range(27):
            post_ref[i, z] = post[i]
        for k in range(3):
            push_ref[k, z] = push[k]
    store_faces(post_ref, near_ref, far_ref)


def turn_kernel(slot_ref, dest_ref, earlier_ref, turned_ref, hot_ref, at_rank_ref):
    turned_ref[...] = slot_ref[...].astype(f32).T.astype(bf16)
    hot = jnp.where(iota(hot_ref.shape, 0) == dest_ref[...], 1.0, 0.0)
    hot_ref[...] = hot.astype(bf16)
    rank = ranks(hot, earlier_ref[...]).astype(i32)
    at_rank_ref[...] = jnp.where(iota(at_rank_ref.shape, 0) == rank, 1.0, 0.0)


def ends_kernel(post_ref, near_ref, far_ref, inner_ref, outer_ref):
    depth, length = post_ref.shape[1], post_ref.shape[2]
    even = even_place("gx")

    def row(i, z, x):
        source = z - STEP[i][0]
        if 0 <= source < depth:
            return post_ref[i, source, x : x + 1]
        return across(near_ref, far_ref, i, slice(x, x + 1))

    for i in range(27):
        if STEP[i][1] != 1:
            continue
        j = i - 6
        for z in range(depth):
            n = end_row(i, z, depth)
            right, left = row(i, z, length - 1), row(j, z, 0)
            inner_ref[n : n + 1] = jnp.where(even, right, left)
            outer_ref[n : n + 1] = jnp.where(even, left, right)


def end_row(i, z, depth):
    return ((STEP[i][0] + 1) * 3 + STEP[i][2] + 1) * depth + z


def streamed(post_ref, near_ref, far_ref, inner_ref, outer_ref, z, back_ref=None):
    depth, length, width = post_ref.shape[1:]
    even = even_place("gx")
    rows = iota((length, width), 0)
    moved_list = []
    for i in range(27):
        cz, cx, cy = STEP[i]
        source = z - cz
        inside = 0 <= source < depth
        moved = post_ref[i, source] if inside else across(near_ref, far_ref, i)
        if cx:
            n = end_row(i, z, depth)
            inner, outer = inner_ref[n : n + 1], outer_ref[n : n + 1]
            edge = jnp.where(even, outer, inner) if cx > 0 else jnp.where(even, inner, outer)
            if not inside and back_ref is not None:
                edge = back_ref[pl.ds(4 * device_at(-cz, -cx) + 2 + cy, 1)]
            moved = pltpu.roll(moved, cx % length, 0)
            moved = jnp.where(rows == (0 if cx > 0 else length - 1), edge, moved)
        if cy:
            moved = pltpu.roll(moved, cy % width, 1)
        if source < 0:
            moved = jnp.where(lax.axis_index("gz") == 0, post_ref[26 - i, z], moved)
        elif source >= depth:
            top = lax.axis_size("gz") - 1
            moved = jnp.where(lax.axis_index("gz") == top, post_ref[26 - i, z], moved)
        moved_list.append(moved)
    return moved_list


def second_kernel(
    capacity, rates_ref, post_ref, near_ref, far_ref, inner_ref, outer_ref,
    held_ref, push_ref, line_ref, turned_ref,
    next_ref, next_near_ref, next_far_ref, next_inner_ref, next_outer_ref, back_ref, right_ref, left_ref,
):
    depth, length, width = post_ref.shape[1:]
    lines = depth * length
    slots = turned_ref.shape[1]
    halo = (near_ref, far_ref, inner_ref, outer_ref)
    rate = [rates_ref[a : a + 1] for a in range(27)]
    pushes = []
    for z in range(depth):
        relaxed = relax(streamed(post_ref, *halo, z), rate)
        post, push = exchange(*relaxed, *grains_at(held_ref, z, depth, length))
        for i in range(27):
            next_ref[i, z] = post[i]
        pushes.append(push)
    store_faces(next_ref, next_near_ref, next_far_ref)
    back_ref[...] = jnp.zeros(back_ref.shape, f32)
    right_ref[...] = jnp.zeros(right_ref.shape, f32)
    left_ref[...] = jnp.zeros(left_ref.shape, f32)
    for i in range(27):
        cz, cx, cy = STEP[i]
        if cx == 0:
            continue
        x = length - 1 if cx > 0 else 0
        face_ref = right_ref if cx > 0 else left_ref
        for z in range(depth):
            if 0 <= z - cz < depth:
                n = end_row(i, z, depth)
                face_ref[n : n + 1] = next_ref[i, z - cz, x : x + 1]
        if cz:
            z = depth - 1 if cz > 0 else 0
            back_ref[pl.ds(4 * device_at(cz, cx) + 2 + cy, 1)] = next_ref[i, z, x : x + 1]
    even = even_place("gx")
    right, left = right_ref[...], left_ref[...]
    next_inner_ref[...] = jnp.where(even, right, left)
    next_outer_ref[...] = jnp.where(even, left, right)
    total = jnp.concatenate(
        [push_ref[k, z] + pushes[z][k] for k in range(3) for z in range(depth)], axis=0
    )
    along_y = jnp.dot(
        jnp.concatenate(split3(total), axis=0), turned_ref[...], preferred_element_type=f32
    )
    along_y = along_y[: 3 * lines] + along_y[3 * lines : 6 * lines] + along_y[6 * lines :]
    on_line = iota((lines, slots), 0) == line_ref[...]
    tiles, per_tile = slots // LANES, LANES // capacity
    group = iota((tiles, LANES), 1) // capacity
    force = []
    for k in range(3):
        picked = -jnp.sum(jnp.where(on_line, along_y[k * lines : (k + 1) * lines], 0.0), axis=0, keepdims=True)
        force.append(
            jnp.concatenate([picked[:, t * LANES : (t + 1) * LANES] for t in range(tiles)], axis=0)
        )
    for a in range(per_tile):
        block = jnp.zeros((tiles, LANES), f32)
        for k in range(3):
            shift = (k - a) * capacity % LANES
            turned = pltpu.roll(force[k], shift, 1) if shift else force[k]
            block = jnp.where(group == k, turned, block)
        back_ref[pl.ds(4 * a, tiles, stride=4 * per_tile), :] = block


def last_kernel(
    capacity, post_ref, near_ref, far_ref, inner_ref, outer_ref, back_ref, hot_ref, at_rank_ref,
    scaled_ref, force_ref,
):
    for z in range(post_ref.shape[1]):
        fields = streamed(post_ref, near_ref, far_ref, inner_ref, outer_ref, z, back_ref)
        for i in range(27):
            scaled_ref[i, z] = fields[i] * (1.0 / WEIGHT[i])
    back = back_ref[pl.ds(0, hot_ref.shape[0], stride=4), :]
    parts = jnp.concatenate([part.astype(f32) for part in split3(back)], axis=1).T
    picked = jnp.dot(parts.astype(bf16), hot_ref[...], preferred_element_type=f32)
    picked = picked[:LANES] + picked[LANES : 2 * LANES] + picked[2 * LANES :]
    for k in range(3):
        mine = at_rank_ref[...] * picked[k * capacity : (k + 1) * capacity]
        force_ref[k : k + 1] = jnp.sum(mine, axis=0, keepdims=True)


def swap_faces(near, far):
    depth, length = lax.axis_size("gz"), lax.axis_size("gx")
    received = []
    for face, odd in ((far, 1), (near, 0)):
        pairs = []
        for z in range(depth):
            other = z + 1 if z % 2 == odd else z - 1
            for x in range(length):
                to = other * length + x if 0 <= other < depth else z * length + (x ^ 1)
                pairs.append((z * length + x, to))
        received.append(lax.ppermute(face, ("gz", "gx"), pairs))
    return received[1], received[0]


def swap_inner(inner):
    return lax.ppermute(inner, "gx", [(i, i ^ 1) for i in range(lax.axis_size("gx"))])


def swap_outer(outer):
    length = lax.axis_size("gx")
    pairs = [(i, (i + 1) % length if i % 2 else (i - 1) % length) for i in range(length)]
    return lax.ppermute(outer, "gx", pairs)


def per_device(populations, rates, grain_fraction, grain_velocity, grain_dest, grain_line):
    _, depth, length, width = populations.shape
    lines = depth * length
    devices = lax.axis_size("gz") * lax.axis_size("gx")
    grains = grain_fraction.shape[0]
    capacity = 2 * grains // devices
    slots = devices * capacity
    shape, both = jax.ShapeDtypeStruct, ("gz", "gx")
    dest, line = grain_dest.reshape(1, grains), grain_line.reshape(1, grains)
    rows = devices * (capacity + 2)
    earlier, spread, own = call(
        functools.partial(tables_kernel, capacity),
        [shape((LANES, LANES), bf16), shape((width, slots), bf16), shape((devices, slots), f32)],
        flops=10**9,
    )
    (send,) = call(
        functools.partial(pack_kernel, devices, capacity),
        [shape((rows, width), bf16)],
        dest, line, grain_velocity, grain_fraction, earlier,
        scratch=[pltpu.VMEM((rows, width), f32)],
    )
    recv = lax.all_to_all(
        send.reshape(devices, capacity // 2 + 1, 2, width), both, split_axis=0, concat_axis=0, tiled=True
    ).reshape(rows, width)
    state, sums = shape(populations.shape, f32), shape((4, depth, length, width), f32)
    face, ends = shape((9, length, width), f32), shape((9 * depth, width), f32)
    kept, swapped, sums, rate_rows = call(
        relax_kernel, [state, state, sums, shape((27, width), f32)], rates, populations, smem=(0,)
    )
    post, near, far, push, held, slot_line, slot_rows = call(
        functools.partial(first_kernel, devices, capacity),
        [
            state, face, face, shape((3, depth, length, width), f32),
            shape((4 * lines, width), f32), shape((1, slots), i32), shape((slots, width), bf16),
        ],
        recv, kept, swapped, sums, spread, own, scratch=[pltpu.VMEM((rows, width), f32)],
    )
    near, far = swap_faces(near, far)
    turned, hot, at_rank = call(
        turn_kernel,
        [shape((width, slots), bf16), shape((devices, grains), bf16), shape((capacity, grains), f32)],
        slot_rows, dest, earlier,
    )
    inner, outer = call(ends_kernel, [ends, ends], post, near, far)
    inner, outer = swap_inner(inner), swap_outer(outer)
    post, next_near, next_far, inner, outer, back = call(
        functools.partial(second_kernel, capacity),
        [state, face, face, ends, ends, shape((4 * devices, LANES), f32)],
        rate_rows, post, near, far, inner, outer, held, push, slot_line, turned,
        scratch=[pltpu.VMEM(ends.shape, f32)] * 2,
    )
    back = lax.all_to_all(
        back.reshape(devices, 4, LANES), both, split_axis=0, concat_axis=0, tiled=True
    ).reshape(4 * devices, LANES)
    outer = swap_outer(outer)
    near, far = swap_faces(next_near, next_far)
    inner = swap_inner(inner)
    scaled, grain_force = call(
        functools.partial(last_kernel, capacity),
        [state, shape((3, grains), f32)],
        post, near, far, inner, outer, back, hot, at_rank,
    )
    return (scaled, grain_force)


def solution(mesh):
    in_specs = (
        P(None, "gz", "gx", None),
        P(),
        P(("gz", "gx"), None),
        P(None, ("gz", "gx")),
        P(("gz", "gx"), None),
        P(("gz", "gx")),
    )
    out_specs = (P(None, "gz", "gx", None), P(None, ("gz", "gx")))
    return jax.shard_map(
        per_device, mesh=mesh, in_specs=in_specs, out_specs=out_specs, check_vma=False
    )
```

```python
import functools

import jax
import jax.numpy as jnp
import numpy as np
from jax import lax
from jax.experimental import pallas as pl
from jax.experimental.pallas import tpu as pltpu
from jax.sharding import PartitionSpec as P

STEPS = 2
LANES = 128
f32, bf16, i32 = jnp.float32, jnp.bfloat16, jnp.int32
DIGITS = [(i // 9, i // 3 % 3, i % 3) for i in range(27)]
STEP = [tuple(d - 1 for d in digits) for digits in DIGITS]
WEIGHT = [(8.0 / 27, 2.0 / 27, 1.0 / 54, 1.0 / 216)[sum(abs(s) for s in step)] for step in STEP]


def iota(shape, dim):
    return lax.broadcasted_iota(i32, shape, dim)


def call(kernel, outs, *operands, scratch=(), flops=0):
    size = sum(o.size * o.dtype.itemsize for o in operands) + sum(
        int(np.prod(o.shape)) * o.dtype.itemsize for o in outs
    )
    return pl.pallas_call(
        kernel,
        out_shape=list(outs),
        in_specs=[pl.BlockSpec(memory_space=pltpu.VMEM)] * len(operands),
        out_specs=[pl.BlockSpec(memory_space=pltpu.VMEM)] * len(outs),
        scratch_shapes=list(scratch),
        compiler_params=pltpu.CompilerParams(vmem_limit_bytes=24 * 1024 * 1024),
        cost_estimate=pl.CostEstimate(flops=flops, bytes_accessed=size, transcendentals=0),
    )(*operands)


def device_at(step_z, step_x):
    depth, length = lax.axis_size("gz"), lax.axis_size("gx")
    z = lax.rem(lax.axis_index("gz") + step_z + depth, depth)
    x = lax.rem(lax.axis_index("gx") + step_x + length, length)
    return z * length + x


def split3(x):
    high = x.astype(bf16)
    rest = x - high.astype(f32)
    mid = rest.astype(bf16)
    return high, mid, (rest - mid.astype(f32)).astype(bf16)


def tables_kernel(capacity, earlier_ref, spread_ref, own_ref):
    width, slots = spread_ref.shape
    order = iota(earlier_ref.shape, 0) < iota(earlier_ref.shape, 1)
    earlier_ref[...] = jnp.where(order, 1.0, 0.0).astype(bf16)
    same = iota((width, slots), 0) % capacity == iota((width, slots), 1) % capacity
    spread_ref[...] = jnp.where(same, 1.0, 0.0).astype(bf16)
    own_ref[...] = jnp.where(iota(own_ref.shape, 0) == iota(own_ref.shape, 1) // capacity, 1.0, 0.0)


def ranks(hot, earlier):
    devices, grains = hot.shape
    total = jnp.zeros((devices, 1), f32)
    parts = []
    for start in range(0, grains, LANES):
        part = hot[:, start : start + LANES]
        before = jnp.dot(part.astype(bf16), earlier, preferred_element_type=f32) + total
        parts.append(jnp.sum(part * before, axis=0, keepdims=True))
        total = total + jnp.sum(part, axis=1, keepdims=True)
    return jnp.concatenate(parts, axis=1)


def pack_kernel(devices, capacity, dest_ref, line_ref, speed_ref, fraction_ref, earlier_ref, send_ref, rows_ref):
    grains, width = fraction_ref.shape
    block = capacity + 2
    dest = dest_ref[...]
    hot = jnp.where(iota((devices, grains), 0) == dest, 1.0, 0.0)
    rank = ranks(hot, earlier_ref[...]).astype(i32)
    speed = speed_ref[...].astype(f32)
    values = [speed[0:1], speed[1:2], speed[2:3], line_ref[...].astype(f32)]
    at_rank = iota((capacity, grains), 0) == rank
    facts = [jnp.where(at_rank, value, 0.0) for value in values]
    if 4 * capacity < width:
        facts.append(jnp.zeros((width - 4 * capacity, grains), f32))
    fact_rows = lax.dot_general(
        hot.astype(bf16),
        jnp.concatenate(facts, axis=0).astype(bf16),
        (((1,), (1,)), ((), ())),
        preferred_element_type=f32,
    )
    place = jnp.where(iota((devices * block, grains), 0) == dest * block + rank, 1.0, 0.0).astype(bf16)
    rows_ref[...] = jnp.dot(place, fraction_ref[...], preferred_element_type=f32)
    rows_ref[pl.ds(capacity, devices, stride=block), :] = fact_rows
    send_ref[...] = rows_ref[...].astype(bf16)


def total_of(values):
    return functools.reduce(lambda a, b: a + b, values)


def along(speed, i):
    return total_of([v if s > 0 else -v for s, v in zip(STEP[i], speed) if s])


def relax(fields, rate):
    density = total_of(fields)
    momentum = [
        total_of([fields[i] for i in range(27) if STEP[i][axis] == 1])
        - total_of([fields[i] for i in range(27) if STEP[i][axis] == -1])
        for axis in range(3)
    ]
    inverse = 1.0 / density
    speed = [m * inverse for m in momentum]
    base = 1.0 - 1.5 * total_of([v * v for v in speed])
    departure = [None] * 27
    for i in range(13, 27):
        scale = WEIGHT[i] * density
        if i == 13:
            departure[i] = fields[i] - scale * base
            continue
        dot = along(speed, i)
        even, odd = scale * (base + 4.5 * dot * dot), scale * (3.0 * dot)
        departure[i] = fields[i] - (even + odd)
        departure[26 - i] = fields[26 - i] - (even - odd)
    moments = list(departure)
    for stride in (1, 3, 9):
        for i in range(27):
            if i // stride % 3 == 0:
                low, mid, high = moments[i], moments[i + stride], moments[i + 2 * stride]
                both = low + high
                moments[i], moments[i + stride], moments[i + 2 * stride] = both + mid, high - low, both
    moments = [rate[a] * moments[a] for a in range(27)]
    for stride in (9, 3, 1):
        for i in range(27):
            if i // stride % 3 == 0:
                m0, m1, m2 = moments[i], moments[i + stride], moments[i + 2 * stride]
                half1, half2 = 0.5 * m1, 0.5 * m2
                moments[i], moments[i + stride], moments[i + 2 * stride] = half2 - half1, m0 - m2, half2 + half1
    kept = [fields[i] - moments[i] for i in range(27)]
    swapped = [departure[26 - i] - kept[i] for i in range(27)]
    return density, momentum, kept, swapped


def exchange(density, momentum, kept, swapped, solid, carried):
    inverse = 1.0 / (1.0 + solid)
    share = solid * inverse
    speed = [c * inverse for c in carried]
    base = 1.0 - 1.5 * total_of([v * v for v in speed])
    push = [(density * v - m) * inverse for v, m in zip(speed, momentum)]
    post = [None] * 27
    for i in range(13, 27):
        scale = WEIGHT[i] * density
        if i == 13:
            post[i] = kept[i] + share * (swapped[i] + scale * base)
            continue
        dot = along(speed, i)
        even, odd = scale * (base + 4.5 * dot * dot), scale * (3.0 * dot)
        post[i] = kept[i] + share * (swapped[i] + (even + odd))
        post[26 - i] = kept[26 - i] + share * (swapped[26 - i] + (even - odd))
    return post, push


def grains_at(held_ref, z, depth, length):
    lines = depth * length
    first = [held_ref[k * lines + z * length : k * lines + (z + 1) * length, :] for k in range(4)]
    return first[0], first[1:]


def even_place(axis):
    return lax.axis_index(axis) % 2 == 0


def store_faces(post_ref, near_ref, far_ref):
    top = post_ref.shape[1] - 1
    for n in range(9):
        up, down = post_ref[n + 18, top], post_ref[n, 0]
        near_ref[n] = jnp.where(even_place("gz"), up, down)
        far_ref[n] = jnp.where(even_place("gz"), down, up)


def across(near_ref, far_ref, i, x=slice(None)):
    n = i % 9
    if STEP[i][0] > 0:
        return jnp.where(even_place("gz"), far_ref[n, x], near_ref[n, x])
    return jnp.where(even_place("gz"), near_ref[n, x], far_ref[n, x])


def first_kernel(
    devices, capacity, recv_ref, fields_ref, rates_ref, spread_ref, own_ref,
    post_ref, near_ref, far_ref, push_ref, held_ref, line_ref, slot_ref, wide_ref,
):
    width = recv_ref.shape[1]
    block, slots = capacity + 2, devices * capacity
    depth, length = fields_ref.shape[1], fields_ref.shape[2]
    lines = depth * length
    rate = [rates_ref[:, a : a + 1] for a in range(27)]
    wide_ref[...] = recv_ref[...].astype(f32)
    facts = wide_ref[pl.ds(capacity, devices, stride=block), :]
    slot_rows = jnp.concatenate(
        [wide_ref[j * block : j * block + capacity] for j in range(devices)], axis=0
    ).astype(bf16)
    slot_ref[...] = slot_rows
    group = iota((devices, width), 1) // capacity
    stacked = jnp.concatenate([jnp.where(group == m, facts, 0.0) for m in range(4)], axis=0)
    wide = jnp.dot(stacked.astype(bf16), spread_ref[...], preferred_element_type=f32)
    own = own_ref[...]
    fact = [
        jnp.sum(own * wide[m * devices : (m + 1) * devices], axis=0, keepdims=True) for m in range(4)
    ]
    line_ref[...] = fact[3].astype(i32)
    on_line = iota((lines, slots), 0) == fact[3].astype(i32)
    gather = [jnp.where(on_line, 1.0, 0.0)] + [jnp.where(on_line, fact[k], 0.0) for k in range(3)]
    held_ref[...] = jnp.dot(
        jnp.concatenate(gather, axis=0).astype(bf16), slot_rows, preferred_element_type=f32
    )
    for z in range(depth):
        relaxed = relax([fields_ref[i, z] for i in range(27)], rate)
        post, push = exchange(*relaxed, *grains_at(held_ref, z, depth, length))
        for i in range(27):
            post_ref[i, z] = post[i]
        for k in range(3):
            push_ref[k, z] = push[k]
    store_faces(post_ref, near_ref, far_ref)


def turn_kernel(slot_ref, dest_ref, earlier_ref, turned_ref, hot_ref, at_rank_ref):
    turned_ref[...] = slot_ref[...].astype(f32).T.astype(bf16)
    hot = jnp.where(iota(hot_ref.shape, 0) == dest_ref[...], 1.0, 0.0)
    hot_ref[...] = hot.astype(bf16)
    rank = ranks(hot, earlier_ref[...]).astype(i32)
    at_rank_ref[...] = jnp.where(iota(at_rank_ref.shape, 0) == rank, 1.0, 0.0)


def ends_kernel(post_ref, far_ref, near_ref, inner_ref, outer_ref):
    depth, length = post_ref.shape[1], post_ref.shape[2]
    even = even_place("gx")

    def row(i, z, x):
        source = z - STEP[i][0]
        if 0 <= source < depth:
            return post_ref[i, source, x : x + 1]
        return across(near_ref, far_ref, i, slice(x, x + 1))

    for i in range(27):
        if STEP[i][1] != 1:
            continue
        j = i - 6
        for z in range(depth):
            n = end_row(i, z, depth)
            right, left = row(i, z, length - 1), row(j, z, 0)
            inner_ref[n : n + 1] = jnp.where(even, right, left)
            outer_ref[n : n + 1] = jnp.where(even, left, right)


def end_row(i, z, depth):
    return ((STEP[i][0] + 1) * 3 + STEP[i][2] + 1) * depth + z


def streamed(post_ref, near_ref, far_ref, inner_ref, outer_ref, z, back_ref=None):
    depth, length, width = post_ref.shape[1:]
    even = even_place("gx")
    rows = iota((length, width), 0)
    moved_list = []
    for i in range(27):
        cz, cx, cy = STEP[i]
        source = z - cz
        inside = 0 <= source < depth
        moved = post_ref[i, source] if inside else across(near_ref, far_ref, i)
        if cx:
            n = end_row(i, z, depth)
            inner, outer = inner_ref[n : n + 1], outer_ref[n : n + 1]
            edge = jnp.where(even, outer, inner) if cx > 0 else jnp.where(even, inner, outer)
            if not inside and back_ref is not None:
                edge = back_ref[pl.ds(4 * device_at(-cz, -cx) + 2 + cy, 1)]
            moved = pltpu.roll(moved, cx % length, 0)
            moved = jnp.where(rows == (0 if cx > 0 else length - 1), edge, moved)
        if cy:
            moved = pltpu.roll(moved, cy % width, 1)
        if source < 0:
            moved = jnp.where(lax.axis_index("gz") == 0, post_ref[26 - i, z], moved)
        elif source >= depth:
            top = lax.axis_size("gz") - 1
            moved = jnp.where(lax.axis_index("gz") == top, post_ref[26 - i, z], moved)
        moved_list.append(moved)
    return moved_list


def second_kernel(
    capacity, rates_ref, post_ref, far_ref, near_ref, outer_ref, inner_ref,
    held_ref, push_ref, line_ref, turned_ref,
    next_ref, next_near_ref, next_far_ref, next_inner_ref, next_outer_ref, back_ref, right_ref, left_ref,
):
    depth, length, width = post_ref.shape[1:]
    lines = depth * length
    slots = turned_ref.shape[1]
    halo = (near_ref, far_ref, inner_ref, outer_ref)
    rate = [rates_ref[:, a : a + 1] for a in range(27)]
    pushes = []
    for z in range(depth):
        relaxed = relax(streamed(post_ref, *halo, z), rate)
        post, push = exchange(*relaxed, *grains_at(held_ref, z, depth, length))
        for i in range(27):
            next_ref[i, z] = post[i]
        pushes.append(push)
    store_faces(next_ref, next_near_ref, next_far_ref)
    back_ref[...] = jnp.zeros(back_ref.shape, f32)
    right_ref[...] = jnp.zeros(right_ref.shape, f32)
    left_ref[...] = jnp.zeros(left_ref.shape, f32)
    for i in range(27):
        cz, cx, cy = STEP[i]
        if cx == 0:
            continue
        x = length - 1 if cx > 0 else 0
        face_ref = right_ref if cx > 0 else left_ref
        for z in range(depth):
            if 0 <= z - cz < depth:
                n = end_row(i, z, depth)
                face_ref[n : n + 1] = next_ref[i, z - cz, x : x + 1]
        if cz:
            z = depth - 1 if cz > 0 else 0
            back_ref[pl.ds(4 * device_at(cz, cx) + 2 + cy, 1)] = next_ref[i, z, x : x + 1]
    even = even_place("gx")
    right, left = right_ref[...], left_ref[...]
    next_inner_ref[...] = jnp.where(even, right, left)
    next_outer_ref[...] = jnp.where(even, left, right)
    total = jnp.concatenate(
        [push_ref[k, z] + pushes[z][k] for k in range(3) for z in range(depth)], axis=0
    )
    along_y = jnp.dot(
        jnp.concatenate(split3(total), axis=0), turned_ref[...], preferred_element_type=f32
    )
    along_y = along_y[: 3 * lines] + along_y[3 * lines : 6 * lines] + along_y[6 * lines :]
    on_line = iota((lines, slots), 0) == line_ref[...]
    tiles, per_tile = slots // LANES, LANES // capacity
    group = iota((tiles, LANES), 1) // capacity
    force = []
    for k in range(3):
        picked = -jnp.sum(jnp.where(on_line, along_y[k * lines : (k + 1) * lines], 0.0), axis=0, keepdims=True)
        force.append(
            jnp.concatenate([picked[:, t * LANES : (t + 1) * LANES] for t in range(tiles)], axis=0)
        )
    for a in range(per_tile):
        block = jnp.zeros((tiles, LANES), f32)
        for k in range(3):
            shift = (k - a) * capacity % LANES
            turned = pltpu.roll(force[k], shift, 1) if shift else force[k]
            block = jnp.where(group == k, turned, block)
        back_ref[pl.ds(4 * a, tiles, stride=4 * per_tile), :] = block


def last_kernel(
    capacity, post_ref, outer_ref, far_ref, near_ref, inner_ref, back_ref, hot_ref, at_rank_ref,
    scaled_ref, force_ref,
):
    for z in range(post_ref.shape[1]):
        fields = streamed(post_ref, near_ref, far_ref, inner_ref, outer_ref, z, back_ref)
        for i in range(27):
            scaled_ref[i, z] = fields[i] * (1.0 / WEIGHT[i])
    back = back_ref[pl.ds(0, hot_ref.shape[0], stride=4), :]
    parts = jnp.concatenate([part.astype(f32) for part in split3(back)], axis=1).T
    picked = jnp.dot(parts.astype(bf16), hot_ref[...], preferred_element_type=f32)
    picked = picked[:LANES] + picked[LANES : 2 * LANES] + picked[2 * LANES :]
    for k in range(3):
        mine = at_rank_ref[...] * picked[k * capacity : (k + 1) * capacity]
        force_ref[k : k + 1] = jnp.sum(mine, axis=0, keepdims=True)


def swap_faces(near, far):
    depth, length = lax.axis_size("gz"), lax.axis_size("gx")
    received = []
    for face, odd in ((far, 1), (near, 0)):
        pairs = []
        for z in range(depth):
            other = z + 1 if z % 2 == odd else z - 1
            for x in range(length):
                to = other * length + x if 0 <= other < depth else z * length + (x ^ 1)
                pairs.append((z * length + x, to))
        received.append(lax.ppermute(face, ("gz", "gx"), pairs))
    return received[1], received[0]


def swap_inner(inner):
    return lax.ppermute(inner, "gx", [(i, i ^ 1) for i in range(lax.axis_size("gx"))])


def swap_outer(outer):
    length = lax.axis_size("gx")
    pairs = [(i, (i + 1) % length if i % 2 else (i - 1) % length) for i in range(length)]
    return lax.ppermute(outer, "gx", pairs)


def per_device(populations, rates, grain_fraction, grain_velocity, grain_dest, grain_line):
    _, depth, length, width = populations.shape
    lines = depth * length
    devices = lax.axis_size("gz") * lax.axis_size("gx")
    grains = grain_fraction.shape[0]
    capacity = 2 * grains // devices
    slots = devices * capacity
    shape, both = jax.ShapeDtypeStruct, ("gz", "gx")
    dest, line = grain_dest.reshape(1, grains), grain_line.reshape(1, grains)
    rows = devices * (capacity + 2)
    earlier, spread, own = call(
        functools.partial(tables_kernel, capacity),
        [shape((LANES, LANES), bf16), shape((width, slots), bf16), shape((devices, slots), f32)],
        flops=10**9,
    )
    (send,) = call(
        functools.partial(pack_kernel, devices, capacity),
        [shape((rows, width), bf16)],
        dest, line, grain_velocity, grain_fraction, earlier,
        scratch=[pltpu.VMEM((rows, width), f32)],
    )
    recv = lax.all_to_all(
        send.reshape(devices, capacity // 2 + 1, 2, width), both, split_axis=0, concat_axis=0, tiled=True
    ).reshape(rows, width)
    state = shape(populations.shape, f32)
    face, ends = shape((9, length, width), f32), shape((9 * depth, width), f32)
    rates = rates.reshape(1, 27)
    post, near, far, push, held, slot_line, slot_rows = call(
        functools.partial(first_kernel, devices, capacity),
        [
            state, face, face, shape((3, depth, length, width), f32),
            shape((4 * lines, width), f32), shape((1, slots), i32), shape((slots, width), bf16),
        ],
        recv, populations, rates, spread, own, scratch=[pltpu.VMEM((rows, width), f32)],
    )
    near, far = swap_faces(near, far)
    turned, hot, at_rank = call(
        turn_kernel,
        [shape((width, slots), bf16), shape((devices, grains), bf16), shape((capacity, grains), f32)],
        slot_rows, dest, earlier,
    )
    inner, outer = call(ends_kernel, [ends, ends], post, far, near)
    outer, inner = swap_outer(outer), swap_inner(inner)
    post, next_near, next_far, inner, outer, back = call(
        functools.partial(second_kernel, capacity),
        [state, face, face, ends, ends, shape((4 * devices, LANES), f32)],
        rates, post, far, near, outer, inner, held, push, slot_line, turned,
        scratch=[pltpu.VMEM(ends.shape, f32)] * 2,
    )
    back = lax.all_to_all(
        back.reshape(devices, 4, LANES), both, split_axis=0, concat_axis=0, tiled=True
    ).reshape(4 * devices, LANES)
    outer = swap_outer(outer)
    near, far = swap_faces(next_near, next_far)
    inner = swap_inner(inner)
    scaled, grain_force = call(
        functools.partial(last_kernel, capacity),
        [state, shape((3, grains), f32)],
        post, outer, far, near, inner, back, hot, at_rank,
    )
    return (scaled, grain_force)


def solution(mesh):
    in_specs = (
        P(None, "gz", "gx", None),
        P(),
        P(("gz", "gx"), None),
        P(None, ("gz", "gx")),
        P(("gz", "gx"), None),
        P(("gz", "gx")),
    )
    out_specs = (P(None, "gz", "gx", None), P(None, ("gz", "gx")))
    return jax.shard_map(
        per_device, mesh=mesh, in_specs=in_specs, out_specs=out_specs, check_vma=False
    )
```

```python
import functools

import jax
import jax.numpy as jnp
import numpy as np
from jax import lax
from jax.experimental import pallas as pl
from jax.experimental.pallas import tpu as pltpu
from jax.sharding import PartitionSpec as P

STEPS = 2
LANES = 128
f32, bf16, i32 = jnp.float32, jnp.bfloat16, jnp.int32
DIGITS = [(i // 9, i // 3 % 3, i % 3) for i in range(27)]
STEP = [tuple(d - 1 for d in digits) for digits in DIGITS]
WEIGHT = [(8.0 / 27, 2.0 / 27, 1.0 / 54, 1.0 / 216)[sum(abs(s) for s in step)] for step in STEP]


def iota(shape, dim):
    return lax.broadcasted_iota(i32, shape, dim)


def call(kernel, outs, *operands, scratch=(), flops=0):
    size = sum(o.size * o.dtype.itemsize for o in operands) + sum(
        int(np.prod(o.shape)) * o.dtype.itemsize for o in outs
    )
    return pl.pallas_call(
        kernel,
        out_shape=list(outs),
        in_specs=[pl.BlockSpec(memory_space=pltpu.VMEM)] * len(operands),
        out_specs=[pl.BlockSpec(memory_space=pltpu.VMEM)] * len(outs),
        scratch_shapes=list(scratch),
        compiler_params=pltpu.CompilerParams(vmem_limit_bytes=24 * 1024 * 1024),
        cost_estimate=pl.CostEstimate(flops=flops, bytes_accessed=size, transcendentals=0),
    )(*operands)


def device_at(step_z, step_x):
    depth, length = lax.axis_size("gz"), lax.axis_size("gx")
    z = lax.rem(lax.axis_index("gz") + step_z + depth, depth)
    x = lax.rem(lax.axis_index("gx") + step_x + length, length)
    return z * length + x


def split3(x):
    high = x.astype(bf16)
    rest = x - high.astype(f32)
    mid = rest.astype(bf16)
    return high, mid, (rest - mid.astype(f32)).astype(bf16)


def tables_kernel(capacity, earlier_ref, spread_ref, own_ref):
    width, slots = spread_ref.shape
    order = iota(earlier_ref.shape, 0) < iota(earlier_ref.shape, 1)
    earlier_ref[...] = jnp.where(order, 1.0, 0.0).astype(bf16)
    same = iota((width, slots), 0) % capacity == iota((width, slots), 1) % capacity
    spread_ref[...] = jnp.where(same, 1.0, 0.0).astype(bf16)
    own_ref[...] = jnp.where(iota(own_ref.shape, 0) == iota(own_ref.shape, 1) // capacity, 1.0, 0.0)


def ranks(hot, earlier):
    devices, grains = hot.shape
    total = jnp.zeros((devices, 1), f32)
    parts = []
    for start in range(0, grains, LANES):
        part = hot[:, start : start + LANES]
        before = jnp.dot(part.astype(bf16), earlier, preferred_element_type=f32) + total
        parts.append(jnp.sum(part * before, axis=0, keepdims=True))
        total = total + jnp.sum(part, axis=1, keepdims=True)
    return jnp.concatenate(parts, axis=1)


def rank_kernel(
    devices, capacity, dest_ref, line_ref, speed_ref, rates_ref, earlier_ref, position_ref, facts_ref, rates_out_ref
):
    grains, width = dest_ref.shape[1], facts_ref.shape[1]
    dest = dest_ref[...]
    hot = jnp.where(iota((devices, grains), 0) == dest, 1.0, 0.0)
    rank = ranks(hot, earlier_ref[...]).astype(i32)
    position_ref[...] = dest * (capacity + 2) + rank
    speed = speed_ref[...].astype(f32)
    values = [speed[0:1], speed[1:2], speed[2:3], line_ref[...].astype(f32)]
    at_rank = iota((capacity, grains), 0) == rank
    facts = [jnp.where(at_rank, value, 0.0) for value in values]
    if 4 * capacity < width:
        facts.append(jnp.zeros((width - 4 * capacity, grains), f32))
    facts_ref[...] = lax.dot_general(
        hot.astype(bf16),
        jnp.concatenate(facts, axis=0).astype(bf16),
        (((1,), (1,)), ((), ())),
        preferred_element_type=f32,
    )
    rates_out_ref[...] = rates_ref[...]


def pack_kernel(capacity, position_ref, facts_ref, fraction_ref, send_ref, rows_ref):
    rows, grains = rows_ref.shape[0], fraction_ref.shape[0]
    place = jnp.where(iota((rows, grains), 0) == position_ref[...], 1.0, 0.0).astype(bf16)
    rows_ref[...] = jnp.dot(place, fraction_ref[...], preferred_element_type=f32)
    rows_ref[pl.ds(capacity, facts_ref.shape[0], stride=capacity + 2), :] = facts_ref[...]
    send_ref[...] = rows_ref[...].astype(bf16)


def total_of(values):
    return functools.reduce(lambda a, b: a + b, values)


def along(speed, i):
    return total_of([v if s > 0 else -v for s, v in zip(STEP[i], speed) if s])


def relax(fields, rate):
    density = total_of(fields)
    momentum = [
        total_of([fields[i] for i in range(27) if STEP[i][axis] == 1])
        - total_of([fields[i] for i in range(27) if STEP[i][axis] == -1])
        for axis in range(3)
    ]
    inverse = 1.0 / density
    speed = [m * inverse for m in momentum]
    base = 1.0 - 1.5 * total_of([v * v for v in speed])
    departure = [None] * 27
    for i in range(13, 27):
        scale = WEIGHT[i] * density
        if i == 13:
            departure[i] = fields[i] - scale * base
            continue
        dot = along(speed, i)
        even, odd = scale * (base + 4.5 * dot * dot), scale * (3.0 * dot)
        departure[i] = fields[i] - (even + odd)
        departure[26 - i] = fields[26 - i] - (even - odd)
    moments = list(departure)
    for stride in (1, 3, 9):
        for i in range(27):
            if i // stride % 3 == 0:
                low, mid, high = moments[i], moments[i + stride], moments[i + 2 * stride]
                both = low + high
                moments[i], moments[i + stride], moments[i + 2 * stride] = both + mid, high - low, both
    moments = [rate[a] * moments[a] for a in range(27)]
    for stride in (9, 3, 1):
        for i in range(27):
            if i // stride % 3 == 0:
                m0, m1, m2 = moments[i], moments[i + stride], moments[i + 2 * stride]
                half1, half2 = 0.5 * m1, 0.5 * m2
                moments[i], moments[i + stride], moments[i + 2 * stride] = half2 - half1, m0 - m2, half2 + half1
    kept = [fields[i] - moments[i] for i in range(27)]
    swapped = [departure[26 - i] - kept[i] for i in range(27)]
    return density, momentum, kept, swapped


def exchange(density, momentum, kept, swapped, solid, carried):
    inverse = 1.0 / (1.0 + solid)
    share = solid * inverse
    speed = [c * inverse for c in carried]
    base = 1.0 - 1.5 * total_of([v * v for v in speed])
    push = [(density * v - m) * inverse for v, m in zip(speed, momentum)]
    post = [None] * 27
    for i in range(13, 27):
        scale = WEIGHT[i] * density
        if i == 13:
            post[i] = kept[i] + share * (swapped[i] + scale * base)
            continue
        dot = along(speed, i)
        even, odd = scale * (base + 4.5 * dot * dot), scale * (3.0 * dot)
        post[i] = kept[i] + share * (swapped[i] + (even + odd))
        post[26 - i] = kept[26 - i] + share * (swapped[26 - i] + (even - odd))
    return post, push


def grains_at(held_ref, z, depth, length):
    lines = depth * length
    first = [held_ref[k * lines + z * length : k * lines + (z + 1) * length, :] for k in range(4)]
    return first[0], first[1:]


def even_place(axis):
    return lax.axis_index(axis) % 2 == 0


def store_faces(post_ref, near_ref, far_ref):
    top = post_ref.shape[1] - 1
    for n in range(9):
        up, down = post_ref[n + 18, top], post_ref[n, 0]
        near_ref[n] = jnp.where(even_place("gz"), up, down)
        far_ref[n] = jnp.where(even_place("gz"), down, up)


def across(near_ref, far_ref, i, x=slice(None)):
    n = i % 9
    if STEP[i][0] > 0:
        return jnp.where(even_place("gz"), far_ref[n, x], near_ref[n, x])
    return jnp.where(even_place("gz"), near_ref[n, x], far_ref[n, x])


def first_kernel(
    devices, capacity, recv_ref, fields_ref, rates_ref, spread_ref, own_ref,
    post_ref, near_ref, far_ref, push_ref, held_ref, line_ref, slot_ref, wide_ref,
):
    width = recv_ref.shape[1]
    block, slots = capacity + 2, devices * capacity
    depth, length = fields_ref.shape[1], fields_ref.shape[2]
    lines = depth * length
    rate = [rates_ref[:, a : a + 1] for a in range(27)]
    wide_ref[...] = recv_ref[...].astype(f32)
    facts = wide_ref[pl.ds(capacity, devices, stride=block), :]
    slot_rows = jnp.concatenate(
        [wide_ref[j * block : j * block + capacity] for j in range(devices)], axis=0
    ).astype(bf16)
    slot_ref[...] = slot_rows
    group = iota((devices, width), 1) // capacity
    stacked = jnp.concatenate([jnp.where(group == m, facts, 0.0) for m in range(4)], axis=0)
    wide = jnp.dot(stacked.astype(bf16), spread_ref[...], preferred_element_type=f32)
    own = own_ref[...]
    fact = [
        jnp.sum(own * wide[m * devices : (m + 1) * devices], axis=0, keepdims=True) for m in range(4)
    ]
    line_ref[...] = fact[3].astype(i32)
    on_line = iota((lines, slots), 0) == fact[3].astype(i32)
    gather = [jnp.where(on_line, 1.0, 0.0)] + [jnp.where(on_line, fact[k], 0.0) for k in range(3)]
    held_ref[...] = jnp.dot(
        jnp.concatenate(gather, axis=0).astype(bf16), slot_rows, preferred_element_type=f32
    )
    for z in range(depth):
        relaxed = relax([fields_ref[i, z] for i in range(27)], rate)
        post, push = exchange(*relaxed, *grains_at(held_ref, z, depth, length))
        for i in range(27):
            post_ref[i, z] = post[i]
        for k in range(3):
            push_ref[k, z] = push[k]
    store_faces(post_ref, near_ref, far_ref)


def turn_kernel(slot_ref, dest_ref, earlier_ref, turned_ref, hot_ref, at_rank_ref):
    turned_ref[...] = slot_ref[...].astype(f32).T.astype(bf16)
    hot = jnp.where(iota(hot_ref.shape, 0) == dest_ref[...], 1.0, 0.0)
    hot_ref[...] = hot.astype(bf16)
    rank = ranks(hot, earlier_ref[...]).astype(i32)
    at_rank_ref[...] = jnp.where(iota(at_rank_ref.shape, 0) == rank, 1.0, 0.0)


def ends_kernel(post_ref, far_ref, near_ref, inner_ref, outer_ref):
    depth, length = post_ref.shape[1], post_ref.shape[2]
    even = even_place("gx")

    def row(i, z, x):
        source = z - STEP[i][0]
        if 0 <= source < depth:
            return post_ref[i, source, x : x + 1]
        return across(near_ref, far_ref, i, slice(x, x + 1))

    for i in range(27):
        if STEP[i][1] != 1:
            continue
        j = i - 6
        for z in range(depth):
            n = end_row(i, z, depth)
            right, left = row(i, z, length - 1), row(j, z, 0)
            inner_ref[n : n + 1] = jnp.where(even, right, left)
            outer_ref[n : n + 1] = jnp.where(even, left, right)


def end_row(i, z, depth):
    return ((STEP[i][0] + 1) * 3 + STEP[i][2] + 1) * depth + z


def streamed(post_ref, near_ref, far_ref, inner_ref, outer_ref, z, back_ref=None):
    depth, length, width = post_ref.shape[1:]
    even = even_place("gx")
    rows = iota((length, width), 0)
    moved_list = []
    for i in range(27):
        cz, cx, cy = STEP[i]
        source = z - cz
        inside = 0 <= source < depth
        moved = post_ref[i, source] if inside else across(near_ref, far_ref, i)
        if cx:
            n = end_row(i, z, depth)
            inner, outer = inner_ref[n : n + 1], outer_ref[n : n + 1]
            edge = jnp.where(even, outer, inner) if cx > 0 else jnp.where(even, inner, outer)
            if not inside and back_ref is not None:
                edge = back_ref[pl.ds(4 * device_at(-cz, -cx) + 2 + cy, 1)]
            moved = pltpu.roll(moved, cx % length, 0)
            moved = jnp.where(rows == (0 if cx > 0 else length - 1), edge, moved)
        if cy:
            moved = pltpu.roll(moved, cy % width, 1)
        if source < 0:
            moved = jnp.where(lax.axis_index("gz") == 0, post_ref[26 - i, z], moved)
        elif source >= depth:
            top = lax.axis_size("gz") - 1
            moved = jnp.where(lax.axis_index("gz") == top, post_ref[26 - i, z], moved)
        moved_list.append(moved)
    return moved_list


def second_kernel(
    capacity, rates_ref, post_ref, far_ref, near_ref, outer_ref, inner_ref,
    held_ref, push_ref, line_ref, turned_ref,
    next_ref, next_near_ref, next_far_ref, next_inner_ref, next_outer_ref, back_ref, right_ref, left_ref,
):
    depth, length, width = post_ref.shape[1:]
    lines = depth * length
    slots = turned_ref.shape[1]
    halo = (near_ref, far_ref, inner_ref, outer_ref)
    rate = [rates_ref[:, a : a + 1] for a in range(27)]
    pushes = []
    for z in range(depth):
        relaxed = relax(streamed(post_ref, *halo, z), rate)
        post, push = exchange(*relaxed, *grains_at(held_ref, z, depth, length))
        for i in range(27):
            next_ref[i, z] = post[i]
        pushes.append(push)
    store_faces(next_ref, next_near_ref, next_far_ref)
    back_ref[...] = jnp.zeros(back_ref.shape, f32)
    right_ref[...] = jnp.zeros(right_ref.shape, f32)
    left_ref[...] = jnp.zeros(left_ref.shape, f32)
    for i in range(27):
        cz, cx, cy = STEP[i]
        if cx == 0:
            continue
        x = length - 1 if cx > 0 else 0
        face_ref = right_ref if cx > 0 else left_ref
        for z in range(depth):
            if 0 <= z - cz < depth:
                n = end_row(i, z, depth)
                face_ref[n : n + 1] = next_ref[i, z - cz, x : x + 1]
        if cz:
            z = depth - 1 if cz > 0 else 0
            back_ref[pl.ds(4 * device_at(cz, cx) + 2 + cy, 1)] = next_ref[i, z, x : x + 1]
    even = even_place("gx")
    right, left = right_ref[...], left_ref[...]
    next_inner_ref[...] = jnp.where(even, right, left)
    next_outer_ref[...] = jnp.where(even, left, right)
    total = jnp.concatenate(
        [push_ref[k, z] + pushes[z][k] for k in range(3) for z in range(depth)], axis=0
    )
    along_y = jnp.dot(
        jnp.concatenate(split3(total), axis=0), turned_ref[...], preferred_element_type=f32
    )
    along_y = along_y[: 3 * lines] + along_y[3 * lines : 6 * lines] + along_y[6 * lines :]
    on_line = iota((lines, slots), 0) == line_ref[...]
    tiles, per_tile = slots // LANES, LANES // capacity
    group = iota((tiles, LANES), 1) // capacity
    force = []
    for k in range(3):
        picked = -jnp.sum(jnp.where(on_line, along_y[k * lines : (k + 1) * lines], 0.0), axis=0, keepdims=True)
        force.append(
            jnp.concatenate([picked[:, t * LANES : (t + 1) * LANES] for t in range(tiles)], axis=0)
        )
    for a in range(per_tile):
        block = jnp.zeros((tiles, LANES), f32)
        for k in range(3):
            shift = (k - a) * capacity % LANES
            turned = pltpu.roll(force[k], shift, 1) if shift else force[k]
            block = jnp.where(group == k, turned, block)
        back_ref[pl.ds(4 * a, tiles, stride=4 * per_tile), :] = block


def last_kernel(
    capacity, post_ref, outer_ref, far_ref, near_ref, inner_ref, back_ref, hot_ref, at_rank_ref,
    scaled_ref, force_ref,
):
    for z in range(post_ref.shape[1]):
        fields = streamed(post_ref, near_ref, far_ref, inner_ref, outer_ref, z, back_ref)
        for i in range(27):
            scaled_ref[i, z] = fields[i] * (1.0 / WEIGHT[i])
    back = back_ref[pl.ds(0, hot_ref.shape[0], stride=4), :]
    parts = jnp.concatenate([part.astype(f32) for part in split3(back)], axis=1).T
    picked = jnp.dot(parts.astype(bf16), hot_ref[...], preferred_element_type=f32)
    picked = picked[:LANES] + picked[LANES : 2 * LANES] + picked[2 * LANES :]
    for k in range(3):
        mine = at_rank_ref[...] * picked[k * capacity : (k + 1) * capacity]
        force_ref[k : k + 1] = jnp.sum(mine, axis=0, keepdims=True)


def swap_faces(near, far):
    depth, length = lax.axis_size("gz"), lax.axis_size("gx")
    received = []
    for face, odd in ((far, 1), (near, 0)):
        pairs = []
        for z in range(depth):
            other = z + 1 if z % 2 == odd else z - 1
            for x in range(length):
                to = other * length + x if 0 <= other < depth else z * length + (x ^ 1)
                pairs.append((z * length + x, to))
        received.append(lax.ppermute(face, ("gz", "gx"), pairs))
    return received[1], received[0]


def swap_inner(inner):
    return lax.ppermute(inner, "gx", [(i, i ^ 1) for i in range(lax.axis_size("gx"))])


def swap_outer(outer):
    length = lax.axis_size("gx")
    pairs = [(i, (i + 1) % length if i % 2 else (i - 1) % length) for i in range(length)]
    return lax.ppermute(outer, "gx", pairs)


def per_device(populations, rates, grain_fraction, grain_velocity, grain_dest, grain_line):
    _, depth, length, width = populations.shape
    lines = depth * length
    devices = lax.axis_size("gz") * lax.axis_size("gx")
    grains = grain_fraction.shape[0]
    capacity = 2 * grains // devices
    slots = devices * capacity
    shape, both = jax.ShapeDtypeStruct, ("gz", "gx")
    dest, line = grain_dest.reshape(1, grains), grain_line.reshape(1, grains)
    rows = devices * (capacity + 2)
    earlier, spread, own = call(
        functools.partial(tables_kernel, capacity),
        [shape((LANES, LANES), bf16), shape((width, slots), bf16), shape((devices, slots), f32)],
        flops=10**9,
    )
    position, facts, rates = call(
        functools.partial(rank_kernel, devices, capacity),
        [shape((1, grains), i32), shape((devices, width), f32), shape((1, 27), f32)],
        dest, line, grain_velocity, rates.reshape(1, 27), earlier,
    )
    (send,) = call(
        functools.partial(pack_kernel, capacity),
        [shape((rows, width), bf16)],
        position, facts, grain_fraction,
        scratch=[pltpu.VMEM((rows, width), f32)],
    )
    recv = lax.all_to_all(
        send.reshape(devices, capacity // 2 + 1, 2, width), both, split_axis=0, concat_axis=0, tiled=True
    ).reshape(rows, width)
    state = shape(populations.shape, f32)
    face, ends = shape((9, length, width), f32), shape((9 * depth, width), f32)
    post, near, far, push, held, slot_line, slot_rows = call(
        functools.partial(first_kernel, devices, capacity),
        [
            state, face, face, shape((3, depth, length, width), f32),
            shape((4 * lines, width), f32), shape((1, slots), i32), shape((slots, width), bf16),
        ],
        recv, populations, rates, spread, own, scratch=[pltpu.VMEM((rows, width), f32)],
    )
    near, far = swap_faces(near, far)
    turned, hot, at_rank = call(
        turn_kernel,
        [shape((width, slots), bf16), shape((devices, grains), bf16), shape((capacity, grains), f32)],
        slot_rows, dest, earlier,
    )
    inner, outer = call(ends_kernel, [ends, ends], post, far, near)
    outer, inner = swap_outer(outer), swap_inner(inner)
    post, next_near, next_far, inner, outer, back = call(
        functools.partial(second_kernel, capacity),
        [state, face, face, ends, ends, shape((4 * devices, LANES), f32)],
        rates, post, far, near, outer, inner, held, push, slot_line, turned,
        scratch=[pltpu.VMEM(ends.shape, f32)] * 2,
    )
    back = lax.all_to_all(
        back.reshape(devices, 4, LANES), both, split_axis=0, concat_axis=0, tiled=True
    ).reshape(4 * devices, LANES)
    outer = swap_outer(outer)
    near, far = swap_faces(next_near, next_far)
    inner = swap_inner(inner)
    scaled, grain_force = call(
        functools.partial(last_kernel, capacity),
        [state, shape((3, grains), f32)],
        post, outer, far, near, inner, back, hot, at_rank,
    )
    return (scaled, grain_force)


def solution(mesh):
    in_specs = (
        P(None, "gz", "gx", None),
        P(),
        P(("gz", "gx"), None),
        P(None, ("gz", "gx")),
        P(("gz", "gx"), None),
        P(("gz", "gx")),
    )
    out_specs = (P(None, "gz", "gx", None), P(None, ("gz", "gx")))
    return jax.shard_map(
        per_device, mesh=mesh, in_specs=in_specs, out_specs=out_specs, check_vma=False
    )
```

```python
import functools

import jax
import jax.numpy as jnp
import numpy as np
from jax import lax
from jax.experimental import pallas as pl
from jax.experimental.pallas import tpu as pltpu
from jax.sharding import PartitionSpec as P

STEPS = 2
LANES = 128
f32, bf16, i32 = jnp.float32, jnp.bfloat16, jnp.int32
DIGITS = [(i // 9, i // 3 % 3, i % 3) for i in range(27)]
STEP = [tuple(d - 1 for d in digits) for digits in DIGITS]
WEIGHT = [(8.0 / 27, 2.0 / 27, 1.0 / 54, 1.0 / 216)[sum(abs(s) for s in step)] for step in STEP]


def iota(shape, dim):
    return lax.broadcasted_iota(i32, shape, dim)


def call(kernel, outs, *operands, scratch=(), flops=0):
    size = sum(o.size * o.dtype.itemsize for o in operands) + sum(
        int(np.prod(o.shape)) * o.dtype.itemsize for o in outs
    )
    return pl.pallas_call(
        kernel,
        out_shape=list(outs),
        in_specs=[pl.BlockSpec(memory_space=pltpu.VMEM)] * len(operands),
        out_specs=[pl.BlockSpec(memory_space=pltpu.VMEM)] * len(outs),
        scratch_shapes=list(scratch),
        compiler_params=pltpu.CompilerParams(vmem_limit_bytes=24 * 1024 * 1024),
        cost_estimate=pl.CostEstimate(flops=flops, bytes_accessed=size, transcendentals=0),
    )(*operands)


def device_at(step_z, step_x):
    depth, length = lax.axis_size("gz"), lax.axis_size("gx")
    z = lax.rem(lax.axis_index("gz") + step_z + depth, depth)
    x = lax.rem(lax.axis_index("gx") + step_x + length, length)
    return z * length + x


def split3(x):
    high = x.astype(bf16)
    rest = x - high.astype(f32)
    mid = rest.astype(bf16)
    return high, mid, (rest - mid.astype(f32)).astype(bf16)


def tables_kernel(capacity, earlier_ref, spread_ref, own_ref):
    width, slots = spread_ref.shape
    order = iota(earlier_ref.shape, 0) < iota(earlier_ref.shape, 1)
    earlier_ref[...] = jnp.where(order, 1.0, 0.0).astype(bf16)
    same = iota((width, slots), 0) % capacity == iota((width, slots), 1) % capacity
    spread_ref[...] = jnp.where(same, 1.0, 0.0).astype(bf16)
    own_ref[...] = jnp.where(iota(own_ref.shape, 0) == iota(own_ref.shape, 1) // capacity, 1.0, 0.0)


def ranks(hot, earlier):
    devices, grains = hot.shape
    total = jnp.zeros((devices, 1), f32)
    parts = []
    for start in range(0, grains, LANES):
        part = hot[:, start : start + LANES]
        before = jnp.dot(part.astype(bf16), earlier, preferred_element_type=f32) + total
        parts.append(jnp.sum(part * before, axis=0, keepdims=True))
        total = total + jnp.sum(part, axis=1, keepdims=True)
    return jnp.concatenate(parts, axis=1)


def rank_kernel(devices, dest_ref, rates_ref, earlier_ref, rank_ref, rates_out_ref):
    hot = jnp.where(iota((devices, dest_ref.shape[1]), 0) == dest_ref[...], 1.0, 0.0)
    rank_ref[...] = ranks(hot, earlier_ref[...]).astype(i32)
    rates_out_ref[...] = rates_ref[...]


def pack_kernel(devices, capacity, dest_ref, rank_ref, line_ref, speed_ref, fraction_ref, send_ref, rows_ref):
    grains, width = fraction_ref.shape
    dest, rank = dest_ref[...], rank_ref[...]
    place = jnp.where(iota((rows_ref.shape[0], grains), 0) == dest * (capacity + 2) + rank, 1.0, 0.0)
    rows_ref[...] = jnp.dot(place.astype(bf16), fraction_ref[...], preferred_element_type=f32)
    speed = speed_ref[...].astype(f32)
    values = [speed[0:1], speed[1:2], speed[2:3], line_ref[...].astype(f32)]
    at_rank = iota((capacity, grains), 0) == rank
    facts = [jnp.where(at_rank, value, 0.0) for value in values]
    if 4 * capacity < width:
        facts.append(jnp.zeros((width - 4 * capacity, grains), f32))
    rows_ref[pl.ds(capacity, devices, stride=capacity + 2), :] = lax.dot_general(
        jnp.where(iota((devices, grains), 0) == dest, 1.0, 0.0).astype(bf16),
        jnp.concatenate(facts, axis=0).astype(bf16),
        (((1,), (1,)), ((), ())),
        preferred_element_type=f32,
    )
    send_ref[...] = rows_ref[...].astype(bf16)


def total_of(values):
    return functools.reduce(lambda a, b: a + b, values)


def along(speed, i):
    return total_of([v if s > 0 else -v for s, v in zip(STEP[i], speed) if s])


def relax(fields, rate):
    density = total_of(fields)
    momentum = [
        total_of([fields[i] for i in range(27) if STEP[i][axis] == 1])
        - total_of([fields[i] for i in range(27) if STEP[i][axis] == -1])
        for axis in range(3)
    ]
    inverse = 1.0 / density
    speed = [m * inverse for m in momentum]
    base = 1.0 - 1.5 * total_of([v * v for v in speed])
    departure = [None] * 27
    for i in range(13, 27):
        scale = WEIGHT[i] * density
        if i == 13:
            departure[i] = fields[i] - scale * base
            continue
        dot = along(speed, i)
        even, odd = scale * (base + 4.5 * dot * dot), scale * (3.0 * dot)
        departure[i] = fields[i] - (even + odd)
        departure[26 - i] = fields[26 - i] - (even - odd)
    moments = list(departure)
    for stride in (1, 3, 9):
        for i in range(27):
            if i // stride % 3 == 0:
                low, mid, high = moments[i], moments[i + stride], moments[i + 2 * stride]
                both = low + high
                moments[i], moments[i + stride], moments[i + 2 * stride] = both + mid, high - low, both
    moments = [rate[a] * moments[a] for a in range(27)]
    for stride in (9, 3, 1):
        for i in range(27):
            if i // stride % 3 == 0:
                m0, m1, m2 = moments[i], moments[i + stride], moments[i + 2 * stride]
                half1, half2 = 0.5 * m1, 0.5 * m2
                moments[i], moments[i + stride], moments[i + 2 * stride] = half2 - half1, m0 - m2, half2 + half1
    kept = [fields[i] - moments[i] for i in range(27)]
    swapped = [departure[26 - i] - kept[i] for i in range(27)]
    return density, momentum, kept, swapped


def exchange(density, momentum, kept, swapped, solid, carried):
    inverse = 1.0 / (1.0 + solid)
    share = solid * inverse
    speed = [c * inverse for c in carried]
    base = 1.0 - 1.5 * total_of([v * v for v in speed])
    push = [(density * v - m) * inverse for v, m in zip(speed, momentum)]
    post = [None] * 27
    for i in range(13, 27):
        scale = WEIGHT[i] * density
        if i == 13:
            post[i] = kept[i] + share * (swapped[i] + scale * base)
            continue
        dot = along(speed, i)
        even, odd = scale * (base + 4.5 * dot * dot), scale * (3.0 * dot)
        post[i] = kept[i] + share * (swapped[i] + (even + odd))
        post[26 - i] = kept[26 - i] + share * (swapped[26 - i] + (even - odd))
    return post, push


def grains_at(held_ref, z, depth, length):
    lines = depth * length
    first = [held_ref[k * lines + z * length : k * lines + (z + 1) * length, :] for k in range(4)]
    return first[0], first[1:]


def even_place(axis):
    return lax.axis_index(axis) % 2 == 0


def store_faces(post_ref, near_ref, far_ref):
    top = post_ref.shape[1] - 1
    for n in range(9):
        up, down = post_ref[n + 18, top], post_ref[n, 0]
        near_ref[n] = jnp.where(even_place("gz"), up, down)
        far_ref[n] = jnp.where(even_place("gz"), down, up)


def across(near_ref, far_ref, i, x=slice(None)):
    n = i % 9
    if STEP[i][0] > 0:
        return jnp.where(even_place("gz"), far_ref[n, x], near_ref[n, x])
    return jnp.where(even_place("gz"), near_ref[n, x], far_ref[n, x])


def first_kernel(
    devices, capacity, recv_ref, fields_ref, rates_ref, spread_ref, own_ref,
    post_ref, near_ref, far_ref, push_ref, held_ref, line_ref, slot_ref, wide_ref,
):
    width = recv_ref.shape[1]
    block, slots = capacity + 2, devices * capacity
    depth, length = fields_ref.shape[1], fields_ref.shape[2]
    lines = depth * length
    rate = [rates_ref[:, a : a + 1] for a in range(27)]
    wide_ref[...] = recv_ref[...].astype(f32)
    facts = wide_ref[pl.ds(capacity, devices, stride=block), :]
    slot_rows = jnp.concatenate(
        [wide_ref[j * block : j * block + capacity] for j in range(devices)], axis=0
    ).astype(bf16)
    slot_ref[...] = slot_rows
    group = iota((devices, width), 1) // capacity
    stacked = jnp.concatenate([jnp.where(group == m, facts, 0.0) for m in range(4)], axis=0)
    wide = jnp.dot(stacked.astype(bf16), spread_ref[...], preferred_element_type=f32)
    own = own_ref[...]
    fact = [
        jnp.sum(own * wide[m * devices : (m + 1) * devices], axis=0, keepdims=True) for m in range(4)
    ]
    line_ref[...] = fact[3].astype(i32)
    on_line = iota((lines, slots), 0) == fact[3].astype(i32)
    gather = [jnp.where(on_line, 1.0, 0.0)] + [jnp.where(on_line, fact[k], 0.0) for k in range(3)]
    held_ref[...] = jnp.dot(
        jnp.concatenate(gather, axis=0).astype(bf16), slot_rows, preferred_element_type=f32
    )
    for z in range(depth):
        relaxed = relax([fields_ref[i, z] for i in range(27)], rate)
        post, push = exchange(*relaxed, *grains_at(held_ref, z, depth, length))
        for i in range(27):
            post_ref[i, z] = post[i]
        for k in range(3):
            push_ref[k, z] = push[k]
    store_faces(post_ref, near_ref, far_ref)


def turn_kernel(slot_ref, dest_ref, rank_ref, turned_ref, hot_ref, at_rank_ref):
    turned_ref[...] = slot_ref[...].astype(f32).T.astype(bf16)
    hot_ref[...] = jnp.where(iota(hot_ref.shape, 0) == dest_ref[...], 1.0, 0.0).astype(bf16)
    at_rank_ref[...] = jnp.where(iota(at_rank_ref.shape, 0) == rank_ref[...], 1.0, 0.0)


def ends_kernel(post_ref, far_ref, near_ref, inner_ref, outer_ref):
    depth, length = post_ref.shape[1], post_ref.shape[2]
    even = even_place("gx")

    def row(i, z, x):
        source = z - STEP[i][0]
        if 0 <= source < depth:
            return post_ref[i, source, x : x + 1]
        return across(near_ref, far_ref, i, slice(x, x + 1))

    for i in range(27):
        if STEP[i][1] != 1:
            continue
        j = i - 6
        for z in range(depth):
            n = end_row(i, z, depth)
            right, left = row(i, z, length - 1), row(j, z, 0)
            inner_ref[n : n + 1] = jnp.where(even, right, left)
            outer_ref[n : n + 1] = jnp.where(even, left, right)


def end_row(i, z, depth):
    return ((STEP[i][0] + 1) * 3 + STEP[i][2] + 1) * depth + z


def streamed(post_ref, near_ref, far_ref, inner_ref, outer_ref, z, back_ref=None):
    depth, length, width = post_ref.shape[1:]
    even = even_place("gx")
    rows = iota((length, width), 0)
    moved_list = []
    for i in range(27):
        cz, cx, cy = STEP[i]
        source = z - cz
        inside = 0 <= source < depth
        moved = post_ref[i, source] if inside else across(near_ref, far_ref, i)
        if cx:
            n = end_row(i, z, depth)
            inner, outer = inner_ref[n : n + 1], outer_ref[n : n + 1]
            edge = jnp.where(even, outer, inner) if cx > 0 else jnp.where(even, inner, outer)
            if not inside and back_ref is not None:
                edge = back_ref[pl.ds(4 * device_at(-cz, -cx) + 2 + cy, 1)]
            moved = pltpu.roll(moved, cx % length, 0)
            moved = jnp.where(rows == (0 if cx > 0 else length - 1), edge, moved)
        if cy:
            moved = pltpu.roll(moved, cy % width, 1)
        if source < 0:
            moved = jnp.where(lax.axis_index("gz") == 0, post_ref[26 - i, z], moved)
        elif source >= depth:
            top = lax.axis_size("gz") - 1
            moved = jnp.where(lax.axis_index("gz") == top, post_ref[26 - i, z], moved)
        moved_list.append(moved)
    return moved_list


def second_kernel(
    capacity, rates_ref, post_ref, far_ref, near_ref, outer_ref, inner_ref,
    held_ref, push_ref, line_ref, turned_ref,
    next_ref, next_near_ref, next_far_ref, next_inner_ref, next_outer_ref, back_ref, right_ref, left_ref,
):
    depth, length, width = post_ref.shape[1:]
    lines = depth * length
    slots = turned_ref.shape[1]
    halo = (near_ref, far_ref, inner_ref, outer_ref)
    rate = [rates_ref[:, a : a + 1] for a in range(27)]
    pushes = []
    for z in range(depth):
        relaxed = relax(streamed(post_ref, *halo, z), rate)
        post, push = exchange(*relaxed, *grains_at(held_ref, z, depth, length))
        for i in range(27):
            next_ref[i, z] = post[i]
        pushes.append(push)
    store_faces(next_ref, next_near_ref, next_far_ref)
    back_ref[...] = jnp.zeros(back_ref.shape, f32)
    right_ref[...] = jnp.zeros(right_ref.shape, f32)
    left_ref[...] = jnp.zeros(left_ref.shape, f32)
    for i in range(27):
        cz, cx, cy = STEP[i]
        if cx == 0:
            continue
        x = length - 1 if cx > 0 else 0
        face_ref = right_ref if cx > 0 else left_ref
        for z in range(depth):
            if 0 <= z - cz < depth:
                n = end_row(i, z, depth)
                face_ref[n : n + 1] = next_ref[i, z - cz, x : x + 1]
        if cz:
            z = depth - 1 if cz > 0 else 0
            back_ref[pl.ds(4 * device_at(cz, cx) + 2 + cy, 1)] = next_ref[i, z, x : x + 1]
    even = even_place("gx")
    right, left = right_ref[...], left_ref[...]
    next_inner_ref[...] = jnp.where(even, right, left)
    next_outer_ref[...] = jnp.where(even, left, right)
    total = jnp.concatenate(
        [push_ref[k, z] + pushes[z][k] for k in range(3) for z in range(depth)], axis=0
    )
    along_y = jnp.dot(
        jnp.concatenate(split3(total), axis=0), turned_ref[...], preferred_element_type=f32
    )
    along_y = along_y[: 3 * lines] + along_y[3 * lines : 6 * lines] + along_y[6 * lines :]
    on_line = iota((lines, slots), 0) == line_ref[...]
    tiles, per_tile = slots // LANES, LANES // capacity
    group = iota((tiles, LANES), 1) // capacity
    force = []
    for k in range(3):
        picked = -jnp.sum(jnp.where(on_line, along_y[k * lines : (k + 1) * lines], 0.0), axis=0, keepdims=True)
        force.append(
            jnp.concatenate([picked[:, t * LANES : (t + 1) * LANES] for t in range(tiles)], axis=0)
        )
    for a in range(per_tile):
        block = jnp.zeros((tiles, LANES), f32)
        for k in range(3):
            shift = (k - a) * capacity % LANES
            turned = pltpu.roll(force[k], shift, 1) if shift else force[k]
            block = jnp.where(group == k, turned, block)
        back_ref[pl.ds(4 * a, tiles, stride=4 * per_tile), :] = block


def last_kernel(
    capacity, post_ref, near_ref, far_ref, outer_ref, inner_ref, back_ref, hot_ref, at_rank_ref,
    scaled_ref, force_ref,
):
    for z in range(post_ref.shape[1]):
        fields = streamed(post_ref, near_ref, far_ref, inner_ref, outer_ref, z, back_ref)
        for i in range(27):
            scaled_ref[i, z] = fields[i] * (1.0 / WEIGHT[i])
    back = back_ref[pl.ds(0, hot_ref.shape[0], stride=4), :]
    parts = jnp.concatenate([part.astype(f32) for part in split3(back)], axis=1).T
    picked = jnp.dot(parts.astype(bf16), hot_ref[...], preferred_element_type=f32)
    picked = picked[:LANES] + picked[LANES : 2 * LANES] + picked[2 * LANES :]
    for k in range(3):
        mine = at_rank_ref[...] * picked[k * capacity : (k + 1) * capacity]
        force_ref[k : k + 1] = jnp.sum(mine, axis=0, keepdims=True)


def swap_faces(near, far):
    depth, length = lax.axis_size("gz"), lax.axis_size("gx")
    received = []
    for face, odd in ((far, 1), (near, 0)):
        pairs = []
        for z in range(depth):
            other = z + 1 if z % 2 == odd else z - 1
            for x in range(length):
                to = other * length + x if 0 <= other < depth else z * length + (x ^ 1)
                pairs.append((z * length + x, to))
        received.append(lax.ppermute(face, ("gz", "gx"), pairs))
    return received[1], received[0]


def swap_inner(inner):
    return lax.ppermute(inner, "gx", [(i, i ^ 1) for i in range(lax.axis_size("gx"))])


def swap_outer(outer):
    length = lax.axis_size("gx")
    pairs = [(i, (i + 1) % length if i % 2 else (i - 1) % length) for i in range(length)]
    return lax.ppermute(outer, "gx", pairs)


def per_device(populations, rates, grain_fraction, grain_velocity, grain_dest, grain_line):
    _, depth, length, width = populations.shape
    lines = depth * length
    devices = lax.axis_size("gz") * lax.axis_size("gx")
    grains = grain_fraction.shape[0]
    capacity = 2 * grains // devices
    slots = devices * capacity
    shape, both = jax.ShapeDtypeStruct, ("gz", "gx")
    dest, line = grain_dest.reshape(1, grains), grain_line.reshape(1, grains)
    rows = devices * (capacity + 2)
    earlier, spread, own = call(
        functools.partial(tables_kernel, capacity),
        [shape((LANES, LANES), bf16), shape((width, slots), bf16), shape((devices, slots), f32)],
        flops=10**9,
    )
    rank, rates = call(
        functools.partial(rank_kernel, devices),
        [shape((1, grains), i32), shape((1, 27), f32)],
        dest, rates.reshape(1, 27), earlier,
    )
    (send,) = call(
        functools.partial(pack_kernel, devices, capacity),
        [shape((rows, width), bf16)],
        dest, rank, line, grain_velocity, grain_fraction,
        scratch=[pltpu.VMEM((rows, width), f32)],
    )
    recv = lax.all_to_all(
        send.reshape(devices, capacity // 2 + 1, 2, width), both, split_axis=0, concat_axis=0, tiled=True
    ).reshape(rows, width)
    state = shape(populations.shape, f32)
    face, ends = shape((9, length, width), f32), shape((9 * depth, width), f32)
    post, near, far, push, held, slot_line, slot_rows = call(
        functools.partial(first_kernel, devices, capacity),
        [
            state, face, face, shape((3, depth, length, width), f32),
            shape((4 * lines, width), f32), shape((1, slots), i32), shape((slots, width), bf16),
        ],
        recv, populations, rates, spread, own, scratch=[pltpu.VMEM((rows, width), f32)],
    )
    near, far = swap_faces(near, far)
    turned, hot, at_rank = call(
        turn_kernel,
        [shape((width, slots), bf16), shape((devices, grains), bf16), shape((capacity, grains), f32)],
        slot_rows, dest, rank,
    )
    inner, outer = call(ends_kernel, [ends, ends], post, far, near)
    outer, inner = swap_outer(outer), swap_inner(inner)
    post, next_near, next_far, inner, outer, back = call(
        functools.partial(second_kernel, capacity),
        [state, face, face, ends, ends, shape((4 * devices, LANES), f32)],
        rates, post, far, near, outer, inner, held, push, slot_line, turned,
        scratch=[pltpu.VMEM(ends.shape, f32)] * 2,
    )
    back = lax.all_to_all(
        back.reshape(devices, 4, LANES), both, split_axis=0, concat_axis=0, tiled=True
    ).reshape(4 * devices, LANES)
    outer = swap_outer(outer)
    near, far = swap_faces(next_near, next_far)
    inner = swap_inner(inner)
    scaled, grain_force = call(
        functools.partial(last_kernel, capacity),
        [state, shape((3, grains), f32)],
        post, near, far, outer, inner, back, hot, at_rank,
    )
    return (scaled, grain_force)


def solution(mesh):
    in_specs = (
        P(None, "gz", "gx", None),
        P(),
        P(("gz", "gx"), None),
        P(None, ("gz", "gx")),
        P(("gz", "gx"), None),
        P(("gz", "gx")),
    )
    out_specs = (P(None, "gz", "gx", None), P(None, ("gz", "gx")))
    return jax.shard_map(
        per_device, mesh=mesh, in_specs=in_specs, out_specs=out_specs, check_vma=False
    )
```

```python
import functools

import jax
import jax.numpy as jnp
import numpy as np
from jax import lax
from jax.experimental import pallas as pl
from jax.experimental.pallas import tpu as pltpu
from jax.sharding import PartitionSpec as P

STEPS = 2
LANES = 128
f32, bf16, i32 = jnp.float32, jnp.bfloat16, jnp.int32
DIGITS = [(i // 9, i // 3 % 3, i % 3) for i in range(27)]
STEP = [tuple(d - 1 for d in digits) for digits in DIGITS]
WEIGHT = [(8.0 / 27, 2.0 / 27, 1.0 / 54, 1.0 / 216)[sum(abs(s) for s in step)] for step in STEP]


def iota(shape, dim):
    return lax.broadcasted_iota(i32, shape, dim)


def call(kernel, outs, *operands, scratch=(), flops=0):
    size = sum(o.size * o.dtype.itemsize for o in operands) + sum(
        int(np.prod(o.shape)) * o.dtype.itemsize for o in outs
    )
    return pl.pallas_call(
        kernel,
        out_shape=list(outs),
        in_specs=[pl.BlockSpec(memory_space=pltpu.VMEM)] * len(operands),
        out_specs=[pl.BlockSpec(memory_space=pltpu.VMEM)] * len(outs),
        scratch_shapes=list(scratch),
        compiler_params=pltpu.CompilerParams(vmem_limit_bytes=24 * 1024 * 1024),
        cost_estimate=pl.CostEstimate(flops=flops, bytes_accessed=size, transcendentals=0),
    )(*operands)


def device_at(step_z, step_x):
    depth, length = lax.axis_size("gz"), lax.axis_size("gx")
    z = lax.rem(lax.axis_index("gz") + step_z + depth, depth)
    x = lax.rem(lax.axis_index("gx") + step_x + length, length)
    return z * length + x


def split3(x):
    high = x.astype(bf16)
    rest = x - high.astype(f32)
    mid = rest.astype(bf16)
    return high, mid, (rest - mid.astype(f32)).astype(bf16)


def tables_kernel(capacity, earlier_ref, spread_ref, own_ref):
    width, slots = spread_ref.shape
    order = iota(earlier_ref.shape, 0) < iota(earlier_ref.shape, 1)
    earlier_ref[...] = jnp.where(order, 1.0, 0.0).astype(bf16)
    same = iota((width, slots), 0) % capacity == iota((width, slots), 1) % capacity
    spread_ref[...] = jnp.where(same, 1.0, 0.0).astype(bf16)
    own_ref[...] = jnp.where(iota(own_ref.shape, 0) == iota(own_ref.shape, 1) // capacity, 1.0, 0.0)


def ranks(hot, earlier):
    devices, grains = hot.shape
    total = jnp.zeros((devices, 1), f32)
    parts = []
    for start in range(0, grains, LANES):
        part = hot[:, start : start + LANES]
        before = jnp.dot(part.astype(bf16), earlier, preferred_element_type=f32) + total
        parts.append(jnp.sum(part * before, axis=0, keepdims=True))
        total = total + jnp.sum(part, axis=1, keepdims=True)
    return jnp.concatenate(parts, axis=1)


def rank_kernel(
    devices, dest_ref, line_ref, speed_ref, rates_ref, earlier_ref, rank_ref, facts_ref, rates_out_ref
):
    hot = jnp.where(iota((devices, dest_ref.shape[1]), 0) == dest_ref[...], 1.0, 0.0)
    rank_ref[...] = ranks(hot, earlier_ref[...]).astype(i32)
    facts_ref[0:3] = speed_ref[...].astype(f32)
    facts_ref[3:4] = line_ref[...].astype(f32)
    rates_out_ref[...] = rates_ref[...]


def pack_kernel(devices, capacity, dest_ref, rank_ref, facts_ref, fraction_ref, send_ref, rows_ref):
    grains, width = fraction_ref.shape
    dest, rank = dest_ref[...], rank_ref[...]
    place = jnp.where(iota((rows_ref.shape[0], grains), 0) == dest * (capacity + 2) + rank, 1.0, 0.0)
    rows_ref[...] = jnp.dot(place.astype(bf16), fraction_ref[...], preferred_element_type=f32)
    at_rank = iota((capacity, grains), 0) == rank
    facts = [jnp.where(at_rank, facts_ref[m : m + 1], 0.0) for m in range(4)]
    if 4 * capacity < width:
        facts.append(jnp.zeros((width - 4 * capacity, grains), f32))
    rows_ref[pl.ds(capacity, devices, stride=capacity + 2), :] = lax.dot_general(
        jnp.where(iota((devices, grains), 0) == dest, 1.0, 0.0).astype(bf16),
        jnp.concatenate(facts, axis=0).astype(bf16),
        (((1,), (1,)), ((), ())),
        preferred_element_type=f32,
    )
    send_ref[...] = rows_ref[...].astype(bf16)


def total_of(values):
    return functools.reduce(lambda a, b: a + b, values)


def along(speed, i):
    return total_of([v if s > 0 else -v for s, v in zip(STEP[i], speed) if s])


def relax(fields, rate):
    density = total_of(fields)
    momentum = [
        total_of([fields[i] for i in range(27) if STEP[i][axis] == 1])
        - total_of([fields[i] for i in range(27) if STEP[i][axis] == -1])
        for axis in range(3)
    ]
    inverse = 1.0 / density
    speed = [m * inverse for m in momentum]
    base = 1.0 - 1.5 * total_of([v * v for v in speed])
    departure = [None] * 27
    for i in range(13, 27):
        scale = WEIGHT[i] * density
        if i == 13:
            departure[i] = fields[i] - scale * base
            continue
        dot = along(speed, i)
        even, odd = scale * (base + 4.5 * dot * dot), scale * (3.0 * dot)
        departure[i] = fields[i] - (even + odd)
        departure[26 - i] = fields[26 - i] - (even - odd)
    moments = list(departure)
    for stride in (1, 3, 9):
        for i in range(27):
            if i // stride % 3 == 0:
                low, mid, high = moments[i], moments[i + stride], moments[i + 2 * stride]
                both = low + high
                moments[i], moments[i + stride], moments[i + 2 * stride] = both + mid, high - low, both
    moments = [rate[a] * moments[a] for a in range(27)]
    for stride in (9, 3, 1):
        for i in range(27):
            if i // stride % 3 == 0:
                m0, m1, m2 = moments[i], moments[i + stride], moments[i + 2 * stride]
                half1, half2 = 0.5 * m1, 0.5 * m2
                moments[i], moments[i + stride], moments[i + 2 * stride] = half2 - half1, m0 - m2, half2 + half1
    kept = [fields[i] - moments[i] for i in range(27)]
    swapped = [departure[26 - i] - kept[i] for i in range(27)]
    return density, momentum, kept, swapped


def exchange(density, momentum, kept, swapped, solid, carried):
    inverse = 1.0 / (1.0 + solid)
    share = solid * inverse
    speed = [c * inverse for c in carried]
    base = 1.0 - 1.5 * total_of([v * v for v in speed])
    push = [(density * v - m) * inverse for v, m in zip(speed, momentum)]
    post = [None] * 27
    for i in range(13, 27):
        scale = WEIGHT[i] * density
        if i == 13:
            post[i] = kept[i] + share * (swapped[i] + scale * base)
            continue
        dot = along(speed, i)
        even, odd = scale * (base + 4.5 * dot * dot), scale * (3.0 * dot)
        post[i] = kept[i] + share * (swapped[i] + (even + odd))
        post[26 - i] = kept[26 - i] + share * (swapped[26 - i] + (even - odd))
    return post, push


def grains_at(held_ref, z, depth, length):
    lines = depth * length
    first = [held_ref[k * lines + z * length : k * lines + (z + 1) * length, :] for k in range(4)]
    return first[0], first[1:]


def even_place(axis):
    return lax.axis_index(axis) % 2 == 0


def store_faces(ups, downs, near_ref, far_ref):
    for n in range(9):
        near_ref[n] = jnp.where(even_place("gz"), ups[n], downs[n])
        far_ref[n] = jnp.where(even_place("gz"), downs[n], ups[n])


def end_row(i, z, depth):
    return ((STEP[i][0] + 1) * 3 + STEP[i][2] + 1) * depth + z


def store_ends(post_ref, inner_ref, outer_ref):
    depth, length = post_ref.shape[1], post_ref.shape[2]
    for i in range(27):
        if STEP[i][1] == 1:
            for z in range(depth):
                n = end_row(i, z, depth)
                right, left = post_ref[i, z, length - 1 : length], post_ref[i - 6, z, 0:1]
                inner_ref[n : n + 1] = jnp.where(even_place("gx"), right, left)
                outer_ref[n : n + 1] = jnp.where(even_place("gx"), left, right)


def moved_along_x(field, i, z, depth, outer_ref, inner_ref, corner=None):
    cx = STEP[i][1]
    if not cx:
        return field
    n, length = end_row(i, z, depth), field.shape[0]
    outer, inner = outer_ref[n : n + 1], inner_ref[n : n + 1]
    if corner is not None:
        end = corner
    elif cx > 0:
        end = jnp.where(even_place("gx"), outer, inner)
    else:
        end = jnp.where(even_place("gx"), inner, outer)
    place = 0 if cx > 0 else length - 1
    return jnp.where(iota(field.shape, 0) == place, end, pltpu.roll(field, cx % length, 0))


def across(near_ref, far_ref, i):
    n = i % 9
    if STEP[i][0] > 0:
        return jnp.where(even_place("gz"), far_ref[n], near_ref[n])
    return jnp.where(even_place("gz"), near_ref[n], far_ref[n])


def first_kernel(
    devices, capacity, recv_ref, fields_ref, rates_ref, spread_ref, own_ref,
    post_ref, outer_ref, inner_ref, push_ref, held_ref, line_ref, slot_ref, wide_ref,
):
    width = recv_ref.shape[1]
    block, slots = capacity + 2, devices * capacity
    depth, length = fields_ref.shape[1], fields_ref.shape[2]
    lines = depth * length
    rate = [rates_ref[:, a : a + 1] for a in range(27)]
    wide_ref[...] = recv_ref[...].astype(f32)
    facts = wide_ref[pl.ds(capacity, devices, stride=block), :]
    slot_rows = jnp.concatenate(
        [wide_ref[j * block : j * block + capacity] for j in range(devices)], axis=0
    ).astype(bf16)
    slot_ref[...] = slot_rows
    group = iota((devices, width), 1) // capacity
    stacked = jnp.concatenate([jnp.where(group == m, facts, 0.0) for m in range(4)], axis=0)
    wide = jnp.dot(stacked.astype(bf16), spread_ref[...], preferred_element_type=f32)
    own = own_ref[...]
    fact = [
        jnp.sum(own * wide[m * devices : (m + 1) * devices], axis=0, keepdims=True) for m in range(4)
    ]
    line_ref[...] = fact[3].astype(i32)
    on_line = iota((lines, slots), 0) == fact[3].astype(i32)
    gather = [jnp.where(on_line, 1.0, 0.0)] + [jnp.where(on_line, fact[k], 0.0) for k in range(3)]
    held_ref[...] = jnp.dot(
        jnp.concatenate(gather, axis=0).astype(bf16), slot_rows, preferred_element_type=f32
    )
    for z in range(depth):
        relaxed = relax([fields_ref[i, z] for i in range(27)], rate)
        post, push = exchange(*relaxed, *grains_at(held_ref, z, depth, length))
        for i in range(27):
            post_ref[i, z] = post[i]
        for k in range(3):
            push_ref[k, z] = push[k]
    store_ends(post_ref, inner_ref, outer_ref)


def turn_kernel(slot_ref, dest_ref, rank_ref, turned_ref, hot_ref, at_rank_ref):
    turned_ref[...] = slot_ref[...].astype(f32).T.astype(bf16)
    hot_ref[...] = jnp.where(iota(hot_ref.shape, 0) == dest_ref[...], 1.0, 0.0).astype(bf16)
    at_rank_ref[...] = jnp.where(iota(at_rank_ref.shape, 0) == rank_ref[...], 1.0, 0.0)


def faces_kernel(post_ref, outer_ref, inner_ref, near_ref, far_ref):
    depth = post_ref.shape[1]
    move = lambda i, z: moved_along_x(post_ref[i, z], i, z, depth, outer_ref, inner_ref)
    ups, downs = [move(n + 18, depth - 1) for n in range(9)], [move(n, 0) for n in range(9)]
    store_faces(ups, downs, near_ref, far_ref)


def streamed(post_ref, outer_ref, inner_ref, far_ref, near_ref, z, back_ref=None):
    depth, width = post_ref.shape[1], post_ref.shape[3]
    moved_list = []
    for i in range(27):
        cz, cx, cy = STEP[i]
        source = z - cz
        inside = 0 <= source < depth
        moved = post_ref[i, source] if inside else across(near_ref, far_ref, i)
        if inside:
            moved = moved_along_x(moved, i, source, depth, outer_ref, inner_ref)
        elif cx and back_ref is not None:
            corner = back_ref[pl.ds(4 * device_at(-cz, -cx) + 2 + cy, 1)]
            moved = moved_along_x(moved, i, 0, depth, outer_ref, inner_ref, corner)
        if cy:
            moved = pltpu.roll(moved, cy % width, 1)
        if not inside:
            wall = 0 if cz > 0 else lax.axis_size("gz") - 1
            moved = jnp.where(lax.axis_index("gz") == wall, post_ref[26 - i, z], moved)
        moved_list.append(moved)
    return moved_list


def second_kernel(
    capacity, rates_ref, post_ref, outer_ref, inner_ref, far_ref, near_ref,
    held_ref, push_ref, line_ref, turned_ref,
    next_ref, next_near_ref, next_far_ref, next_inner_ref, next_outer_ref, back_ref,
):
    depth, length, width = post_ref.shape[1:]
    lines = depth * length
    slots = turned_ref.shape[1]
    halo = (outer_ref, inner_ref, far_ref, near_ref)
    rate = [rates_ref[:, a : a + 1] for a in range(27)]
    pushes = []
    for z in range(depth):
        relaxed = relax(streamed(post_ref, *halo, z), rate)
        post, push = exchange(*relaxed, *grains_at(held_ref, z, depth, length))
        for i in range(27):
            next_ref[i, z] = post[i]
        pushes.append(push)
    ups, downs = [next_ref[n + 18, depth - 1] for n in range(9)], [next_ref[n, 0] for n in range(9)]
    store_faces(ups, downs, next_near_ref, next_far_ref)
    store_ends(next_ref, next_inner_ref, next_outer_ref)
    back_ref[...] = jnp.zeros(back_ref.shape, f32)
    for i in range(27):
        cz, cx, cy = STEP[i]
        if cz and cx:
            z, x = depth - 1 if cz > 0 else 0, length - 1 if cx > 0 else 0
            back_ref[pl.ds(4 * device_at(cz, cx) + 2 + cy, 1)] = next_ref[i, z, x : x + 1]
    total = jnp.concatenate(
        [push_ref[k, z] + pushes[z][k] for k in range(3) for z in range(depth)], axis=0
    )
    along_y = jnp.dot(
        jnp.concatenate(split3(total), axis=0), turned_ref[...], preferred_element_type=f32
    )
    along_y = along_y[: 3 * lines] + along_y[3 * lines : 6 * lines] + along_y[6 * lines :]
    on_line = iota((lines, slots), 0) == line_ref[...]
    tiles, per_tile = slots // LANES, LANES // capacity
    group = iota((tiles, LANES), 1) // capacity
    force = []
    for k in range(3):
        picked = -jnp.sum(jnp.where(on_line, along_y[k * lines : (k + 1) * lines], 0.0), axis=0, keepdims=True)
        force.append(
            jnp.concatenate([picked[:, t * LANES : (t + 1) * LANES] for t in range(tiles)], axis=0)
        )
    for a in range(per_tile):
        block = jnp.zeros((tiles, LANES), f32)
        for k in range(3):
            shift = (k - a) * capacity % LANES
            turned = pltpu.roll(force[k], shift, 1) if shift else force[k]
            block = jnp.where(group == k, turned, block)
        back_ref[pl.ds(4 * a, tiles, stride=4 * per_tile), :] = block


def last_kernel(
    capacity, post_ref, near_ref, far_ref, outer_ref, inner_ref, back_ref, hot_ref, at_rank_ref,
    scaled_ref, force_ref,
):
    for z in range(post_ref.shape[1]):
        fields = streamed(post_ref, outer_ref, inner_ref, far_ref, near_ref, z, back_ref)
        for i in range(27):
            scaled_ref[i, z] = fields[i] * (1.0 / WEIGHT[i])
    back = back_ref[pl.ds(0, hot_ref.shape[0], stride=4), :]
    parts = jnp.concatenate([part.astype(f32) for part in split3(back)], axis=1).T
    picked = jnp.dot(parts.astype(bf16), hot_ref[...], preferred_element_type=f32)
    picked = picked[:LANES] + picked[LANES : 2 * LANES] + picked[2 * LANES :]
    for k in range(3):
        mine = at_rank_ref[...] * picked[k * capacity : (k + 1) * capacity]
        force_ref[k : k + 1] = jnp.sum(mine, axis=0, keepdims=True)


def swap_faces(near, far):
    depth, length = lax.axis_size("gz"), lax.axis_size("gx")
    received = []
    for face, odd in ((far, 1), (near, 0)):
        pairs = []
        for z in range(depth):
            other = z + 1 if z % 2 == odd else z - 1
            for x in range(length):
                to = other * length + x if 0 <= other < depth else z * length + (x ^ 1)
                pairs.append((z * length + x, to))
        received.append(lax.ppermute(face, ("gz", "gx"), pairs))
    return received[1], received[0]


def swap_inner(inner):
    return lax.ppermute(inner, "gx", [(i, i ^ 1) for i in range(lax.axis_size("gx"))])


def swap_outer(outer):
    length = lax.axis_size("gx")
    pairs = [(i, (i + 1) % length if i % 2 else (i - 1) % length) for i in range(length)]
    return lax.ppermute(outer, "gx", pairs)


def per_device(populations, rates, grain_fraction, grain_velocity, grain_dest, grain_line):
    _, depth, length, width = populations.shape
    lines = depth * length
    devices = lax.axis_size("gz") * lax.axis_size("gx")
    grains = grain_fraction.shape[0]
    capacity = 2 * grains // devices
    slots = devices * capacity
    shape, both = jax.ShapeDtypeStruct, ("gz", "gx")
    dest, line = grain_dest.reshape(1, grains), grain_line.reshape(1, grains)
    rows = devices * (capacity + 2)
    earlier, spread, own = call(
        functools.partial(tables_kernel, capacity),
        [shape((LANES, LANES), bf16), shape((width, slots), bf16), shape((devices, slots), f32)],
        flops=10**9,
    )
    rank, facts, rates = call(
        functools.partial(rank_kernel, devices),
        [shape((1, grains), i32), shape((4, grains), f32), shape((1, 27), f32)],
        dest, line, grain_velocity, rates.reshape(1, 27), earlier,
    )
    (send,) = call(
        functools.partial(pack_kernel, devices, capacity),
        [shape((rows, width), bf16)],
        dest, rank, facts, grain_fraction,
        scratch=[pltpu.VMEM((rows, width), f32)],
    )
    recv = lax.all_to_all(
        send.reshape(devices, capacity // 2 + 1, 2, width), both, split_axis=0, concat_axis=0, tiled=True
    ).reshape(rows, width)
    state = shape(populations.shape, f32)
    face, ends = shape((9, length, width), f32), shape((9 * depth, width), f32)
    post, outer, inner, push, held, slot_line, slot_rows = call(
        functools.partial(first_kernel, devices, capacity),
        [
            state, ends, ends, shape((3, depth, length, width), f32),
            shape((4 * lines, width), f32), shape((1, slots), i32), shape((slots, width), bf16),
        ],
        recv, populations, rates, spread, own, scratch=[pltpu.VMEM((rows, width), f32)],
    )
    outer, inner = swap_outer(outer), swap_inner(inner)
    turned, hot, at_rank = call(
        turn_kernel,
        [shape((width, slots), bf16), shape((devices, grains), bf16), shape((capacity, grains), f32)],
        slot_rows, dest, rank,
    )
    near, far = swap_faces(*call(faces_kernel, [face, face], post, outer, inner))
    post, next_near, next_far, inner, outer, back = call(
        functools.partial(second_kernel, capacity),
        [state, face, face, ends, ends, shape((4 * devices, LANES), f32)],
        rates, post, outer, inner, far, near, held, push, slot_line, turned,
    )
    back = lax.all_to_all(
        back.reshape(devices, 4, LANES), both, split_axis=0, concat_axis=0, tiled=True
    ).reshape(4 * devices, LANES)
    outer = swap_outer(outer)
    near, far = swap_faces(next_near, next_far)
    inner = swap_inner(inner)
    scaled, grain_force = call(
        functools.partial(last_kernel, capacity),
        [state, shape((3, grains), f32)],
        post, near, far, outer, inner, back, hot, at_rank,
    )
    return (scaled, grain_force)


def solution(mesh):
    in_specs = (
        P(None, "gz", "gx", None),
        P(),
        P(("gz", "gx"), None),
        P(None, ("gz", "gx")),
        P(("gz", "gx"), None),
        P(("gz", "gx")),
    )
    out_specs = (P(None, "gz", "gx", None), P(None, ("gz", "gx")))
    return jax.shard_map(
        per_device, mesh=mesh, in_specs=in_specs, out_specs=out_specs, check_vma=False
    )
```

```python
import functools

import jax
import jax.numpy as jnp
import numpy as np
from jax import lax
from jax.experimental import pallas as pl
from jax.experimental.pallas import tpu as pltpu
from jax.sharding import PartitionSpec as P

STEPS = 2
LANES = 128
f32, bf16, i32 = jnp.float32, jnp.bfloat16, jnp.int32
DIGITS = [(i // 9, i // 3 % 3, i % 3) for i in range(27)]
STEP = [tuple(d - 1 for d in digits) for digits in DIGITS]
WEIGHT = [(8.0 / 27, 2.0 / 27, 1.0 / 54, 1.0 / 216)[sum(abs(s) for s in step)] for step in STEP]


def iota(shape, dim):
    return lax.broadcasted_iota(i32, shape, dim)


def call(kernel, outs, *operands, scratch=(), flops=0):
    size = sum(o.size * o.dtype.itemsize for o in operands) + sum(
        int(np.prod(o.shape)) * o.dtype.itemsize for o in outs
    )
    return pl.pallas_call(
        kernel,
        out_shape=list(outs),
        in_specs=[pl.BlockSpec(memory_space=pltpu.VMEM)] * len(operands),
        out_specs=[pl.BlockSpec(memory_space=pltpu.VMEM)] * len(outs),
        scratch_shapes=list(scratch),
        compiler_params=pltpu.CompilerParams(vmem_limit_bytes=24 * 1024 * 1024),
        cost_estimate=pl.CostEstimate(flops=flops, bytes_accessed=size, transcendentals=0),
    )(*operands)


def device_at(step_z, step_x):
    depth, length = lax.axis_size("gz"), lax.axis_size("gx")
    z = lax.rem(lax.axis_index("gz") + step_z + depth, depth)
    x = lax.rem(lax.axis_index("gx") + step_x + length, length)
    return z * length + x


def split2(x):
    high = x.astype(bf16)
    return high, (x - high.astype(f32)).astype(bf16)


def tables_kernel(capacity, earlier_ref, spread_ref):
    row, column = iota(earlier_ref.shape, 0), iota(earlier_ref.shape, 1)
    earlier_ref[...] = jnp.where(row < column, 1.0, 0.0).astype(bf16)
    spread_ref[...] = jnp.where(row % capacity == column % capacity, 1.0, 0.0).astype(bf16)


def ranks(hot, earlier):
    devices, grains = hot.shape
    total = jnp.zeros((devices, 1), f32)
    parts = []
    for start in range(0, grains, LANES):
        part = hot[:, start : start + LANES]
        before = jnp.dot(part.astype(bf16), earlier, preferred_element_type=f32) + total
        parts.append(jnp.sum(part * before, axis=0, keepdims=True))
        total = total + jnp.sum(part, axis=1, keepdims=True)
    return jnp.concatenate(parts, axis=1)


def rank_kernel(
    devices, dest_ref, line_ref, speed_ref, rates_ref, earlier_ref, rank_ref, facts_ref, rates_out_ref
):
    hot = jnp.where(iota((devices, dest_ref.shape[1]), 0) == dest_ref[...], 1.0, 0.0)
    rank_ref[...] = ranks(hot, earlier_ref[...]).astype(i32)
    facts_ref[0:3] = speed_ref[...].astype(f32)
    facts_ref[3:4] = line_ref[...].astype(f32)
    rates_out_ref[...] = rates_ref[...]


def pack_kernel(devices, capacity, dest_ref, rank_ref, facts_ref, fraction_ref, send_ref, rows_ref):
    grains, width = fraction_ref.shape
    dest, rank = dest_ref[...], rank_ref[...]
    place = jnp.where(iota((rows_ref.shape[0], grains), 0) == dest * (capacity + 2) + rank, 1.0, 0.0)
    rows_ref[...] = jnp.dot(place.astype(bf16), fraction_ref[...], preferred_element_type=f32)
    at_rank = iota((capacity, grains), 0) == rank
    facts = [jnp.where(at_rank, facts_ref[m : m + 1], 0.0) for m in range(4)]
    if 4 * capacity < width:
        facts.append(jnp.zeros((width - 4 * capacity, grains), f32))
    rows_ref[pl.ds(capacity, devices, stride=capacity + 2), :] = lax.dot_general(
        jnp.where(iota((devices, grains), 0) == dest, 1.0, 0.0).astype(bf16),
        jnp.concatenate(facts, axis=0).astype(bf16),
        (((1,), (1,)), ((), ())),
        preferred_element_type=f32,
    )
    send_ref[...] = rows_ref[...].astype(bf16)


def total_of(values):
    return functools.reduce(lambda a, b: a + b, values)


def along(speed, i):
    return total_of([v if s > 0 else -v for s, v in zip(STEP[i], speed) if s])


def relax(fields, rate):
    density = total_of(fields)
    momentum = [
        total_of([fields[i] for i in range(27) if STEP[i][axis] == 1])
        - total_of([fields[i] for i in range(27) if STEP[i][axis] == -1])
        for axis in range(3)
    ]
    inverse = 1.0 / density
    speed = [m * inverse for m in momentum]
    base = 1.0 - 1.5 * total_of([v * v for v in speed])
    departure = [None] * 27
    for i in range(13, 27):
        scale = WEIGHT[i] * density
        if i == 13:
            departure[i] = fields[i] - scale * base
            continue
        dot = along(speed, i)
        even, odd = scale * (base + 4.5 * dot * dot), scale * (3.0 * dot)
        departure[i] = fields[i] - (even + odd)
        departure[26 - i] = fields[26 - i] - (even - odd)
    moments = list(departure)
    for stride in (1, 3, 9):
        for i in range(27):
            if i // stride % 3 == 0:
                low, mid, high = moments[i], moments[i + stride], moments[i + 2 * stride]
                both = low + high
                moments[i], moments[i + stride], moments[i + 2 * stride] = both + mid, high - low, both
    moments = [rate[a] * moments[a] for a in range(27)]
    for stride in (9, 3, 1):
        for i in range(27):
            if i // stride % 3 == 0:
                m0, m1, m2 = moments[i], moments[i + stride], moments[i + 2 * stride]
                half1, half2 = 0.5 * m1, 0.5 * m2
                moments[i], moments[i + stride], moments[i + 2 * stride] = half2 - half1, m0 - m2, half2 + half1
    kept = [fields[i] - moments[i] for i in range(27)]
    swapped = [departure[26 - i] - kept[i] for i in range(27)]
    return density, momentum, kept, swapped


def exchange(density, momentum, kept, swapped, solid, carried):
    inverse = 1.0 / (1.0 + solid)
    share = solid * inverse
    speed = [c * inverse for c in carried]
    base = 1.0 - 1.5 * total_of([v * v for v in speed])
    push = [(density * v - m) * inverse for v, m in zip(speed, momentum)]
    post = [None] * 27
    for i in range(13, 27):
        scale = WEIGHT[i] * density
        if i == 13:
            post[i] = kept[i] + share * (swapped[i] + scale * base)
            continue
        dot = along(speed, i)
        even, odd = scale * (base + 4.5 * dot * dot), scale * (3.0 * dot)
        post[i] = kept[i] + share * (swapped[i] + (even + odd))
        post[26 - i] = kept[26 - i] + share * (swapped[26 - i] + (even - odd))
    return post, push


def grains_at(held_ref, z, depth, length):
    lines = depth * length
    first = [held_ref[k * lines + z * length : k * lines + (z + 1) * length, :] for k in range(4)]
    return first[0], first[1:]


def even_place(axis):
    return lax.axis_index(axis) % 2 == 0


def store_faces(ups, downs, near_ref, far_ref):
    for n in range(9):
        near_ref[n] = jnp.where(even_place("gz"), ups[n], downs[n])
        far_ref[n] = jnp.where(even_place("gz"), downs[n], ups[n])


def end_row(i, z, depth):
    return ((STEP[i][0] + 1) * 3 + STEP[i][2] + 1) * depth + z


def store_ends(post_ref, inner_ref, outer_ref):
    depth, length = post_ref.shape[1], post_ref.shape[2]
    for i in range(27):
        if STEP[i][1] == 1:
            for z in range(depth):
                n = end_row(i, z, depth)
                right, left = post_ref[i, z, length - 1 : length], post_ref[i - 6, z, 0:1]
                inner_ref[n : n + 1] = jnp.where(even_place("gx"), right, left)
                outer_ref[n : n + 1] = jnp.where(even_place("gx"), left, right)


def moved_along_x(field, i, z, depth, outer_ref, inner_ref, corner=None):
    cx = STEP[i][1]
    if not cx:
        return field
    n, length = end_row(i, z, depth), field.shape[0]
    outer, inner = outer_ref[n : n + 1], inner_ref[n : n + 1]
    if corner is not None:
        end = corner
    elif cx > 0:
        end = jnp.where(even_place("gx"), outer, inner)
    else:
        end = jnp.where(even_place("gx"), inner, outer)
    place = 0 if cx > 0 else length - 1
    return jnp.where(iota(field.shape, 0) == place, end, pltpu.roll(field, cx % length, 0))


def across(near_ref, far_ref, i):
    n = i % 9
    if STEP[i][0] > 0:
        return jnp.where(even_place("gz"), far_ref[n], near_ref[n])
    return jnp.where(even_place("gz"), near_ref[n], far_ref[n])


def first_kernel(
    devices, capacity, recv_ref, fields_ref, rates_ref, spread_ref,
    post_ref, outer_ref, inner_ref, push_ref, held_ref, line_ref, slot_ref, wide_ref,
):
    width = recv_ref.shape[1]
    block, slots = capacity + 2, devices * capacity
    depth, length = fields_ref.shape[1], fields_ref.shape[2]
    lines = depth * length
    rate = [rates_ref[:, a : a + 1] for a in range(27)]
    wide_ref[...] = recv_ref[...].astype(f32)
    slot_rows = jnp.concatenate(
        [wide_ref[j * block : j * block + capacity] for j in range(devices)], axis=0
    ).astype(bf16)
    slot_ref[...] = slot_rows
    tiles, shared = slots // LANES, LANES // capacity
    group = iota((tiles, width), 1) // capacity
    rows = [wide_ref[pl.ds(capacity + a * block, tiles, stride=shared * block), :] for a in range(shared)]
    picked = jnp.concatenate([jnp.where(group == m, row, 0.0) for m in range(4) for row in rows], axis=0)
    placed = jnp.dot(picked.astype(bf16), spread_ref[...], preferred_element_type=f32)
    fact = []
    for m in range(4):
        first = m * shared * tiles
        fact.append(
            total_of(
                [
                    jnp.where(group == a, placed[first + a * tiles : first + (a + 1) * tiles], 0.0)
                    for a in range(shared)
                ]
            )
        )
    line_ref[...] = fact[3].astype(i32)
    gather = []
    for t in range(tiles):
        on_line = iota((lines, LANES), 0) == fact[3][t : t + 1].astype(i32)
        gather.append(
            jnp.concatenate(
                [jnp.where(on_line, 1.0, 0.0)]
                + [jnp.where(on_line, fact[k][t : t + 1], 0.0) for k in range(3)],
                axis=0,
            ).astype(bf16)
        )
    held_ref[...] = jnp.dot(jnp.concatenate(gather, axis=1), slot_rows, preferred_element_type=f32)
    for z in range(depth):
        relaxed = relax([fields_ref[i, z] for i in range(27)], rate)
        post, push = exchange(*relaxed, *grains_at(held_ref, z, depth, length))
        for i in range(27):
            post_ref[i, z] = post[i]
        for k in range(3):
            push_ref[k, z] = push[k]
    store_ends(post_ref, inner_ref, outer_ref)


def turn_kernel(slot_ref, dest_ref, rank_ref, turned_ref, hot_ref, at_rank_ref):
    turned_ref[...] = slot_ref[...].astype(f32).T.astype(bf16)
    devices = hot_ref.shape[0] // 2
    hot_ref[...] = jnp.where(iota(hot_ref.shape, 0) % devices == dest_ref[...], 1.0, 0.0).astype(bf16)
    at_rank_ref[...] = jnp.where(iota(at_rank_ref.shape, 0) == rank_ref[...], 1.0, 0.0)


def faces_kernel(post_ref, outer_ref, inner_ref, near_ref, far_ref):
    depth = post_ref.shape[1]
    move = lambda i, z: moved_along_x(post_ref[i, z], i, z, depth, outer_ref, inner_ref)
    ups, downs = [move(n + 18, depth - 1) for n in range(9)], [move(n, 0) for n in range(9)]
    store_faces(ups, downs, near_ref, far_ref)


def streamed(post_ref, outer_ref, inner_ref, far_ref, near_ref, z, back_ref=None):
    depth, width = post_ref.shape[1], post_ref.shape[3]
    moved_list = []
    for i in range(27):
        cz, cx, cy = STEP[i]
        source = z - cz
        inside = 0 <= source < depth
        moved = post_ref[i, source] if inside else across(near_ref, far_ref, i)
        if inside:
            moved = moved_along_x(moved, i, source, depth, outer_ref, inner_ref)
        elif cx and back_ref is not None:
            corner = back_ref[pl.ds(4 * device_at(-cz, -cx) + 2 + cy, 1)]
            moved = moved_along_x(moved, i, 0, depth, outer_ref, inner_ref, corner)
        if cy:
            moved = pltpu.roll(moved, cy % width, 1)
        if not inside:
            wall = 0 if cz > 0 else lax.axis_size("gz") - 1
            moved = jnp.where(lax.axis_index("gz") == wall, post_ref[26 - i, z], moved)
        moved_list.append(moved)
    return moved_list


def second_kernel(
    capacity, rates_ref, post_ref, outer_ref, inner_ref, far_ref, near_ref,
    held_ref, push_ref, line_ref, turned_ref,
    next_ref, next_near_ref, next_far_ref, next_inner_ref, next_outer_ref, back_ref,
):
    depth, length, width = post_ref.shape[1:]
    lines = depth * length
    slots = turned_ref.shape[1]
    halo = (outer_ref, inner_ref, far_ref, near_ref)
    rate = [rates_ref[:, a : a + 1] for a in range(27)]
    pushes = []
    for z in range(depth):
        relaxed = relax(streamed(post_ref, *halo, z), rate)
        post, push = exchange(*relaxed, *grains_at(held_ref, z, depth, length))
        for i in range(27):
            next_ref[i, z] = post[i]
        pushes.append(push)
    ups, downs = [next_ref[n + 18, depth - 1] for n in range(9)], [next_ref[n, 0] for n in range(9)]
    store_faces(ups, downs, next_near_ref, next_far_ref)
    store_ends(next_ref, next_inner_ref, next_outer_ref)
    back_ref[...] = jnp.zeros(back_ref.shape, f32)
    for i in range(27):
        cz, cx, cy = STEP[i]
        if cz and cx:
            z, x = depth - 1 if cz > 0 else 0, length - 1 if cx > 0 else 0
            back_ref[pl.ds(4 * device_at(cz, cx) + 2 + cy, 1)] = next_ref[i, z, x : x + 1]
    total = jnp.concatenate(
        [push_ref[k, z] + pushes[z][k] for k in range(3) for z in range(depth)], axis=0
    )
    along_y = jnp.dot(
        jnp.concatenate(split2(total), axis=0), turned_ref[...], preferred_element_type=f32
    )
    along_y = along_y[: 3 * lines] + along_y[3 * lines :]
    tiles, per_tile = slots // LANES, LANES // capacity
    group = iota((tiles, LANES), 1) // capacity
    force = [[], [], []]
    for t in range(tiles):
        on_line = iota((lines, LANES), 0) == line_ref[t : t + 1]
        for k in range(3):
            part = along_y[k * lines : (k + 1) * lines, t * LANES : (t + 1) * LANES]
            force[k].append(-jnp.sum(jnp.where(on_line, part, 0.0), axis=0, keepdims=True))
    force = [jnp.concatenate(parts, axis=0) for parts in force]
    for a in range(per_tile):
        block = jnp.zeros((tiles, LANES), f32)
        for k in range(3):
            shift = (k - a) * capacity % LANES
            turned = pltpu.roll(force[k], shift, 1) if shift else force[k]
            block = jnp.where(group == k, turned, block)
        back_ref[pl.ds(4 * a, tiles, stride=4 * per_tile), :] = block


def last_kernel(
    capacity, post_ref, near_ref, far_ref, outer_ref, inner_ref, back_ref, hot_ref, at_rank_ref,
    scaled_ref, force_ref,
):
    for z in range(post_ref.shape[1]):
        fields = streamed(post_ref, outer_ref, inner_ref, far_ref, near_ref, z, back_ref)
        for i in range(27):
            scaled_ref[i, z] = fields[i] * (1.0 / WEIGHT[i])
    back = back_ref[pl.ds(0, hot_ref.shape[0] // 2, stride=4), :]
    parts = jnp.concatenate([part.astype(f32) for part in split2(back)], axis=0).T
    picked = jnp.dot(parts.astype(bf16), hot_ref[...], preferred_element_type=f32)
    for k in range(3):
        mine = at_rank_ref[...] * picked[k * capacity : (k + 1) * capacity]
        force_ref[k : k + 1] = jnp.sum(mine, axis=0, keepdims=True)


def swap_faces(near, far):
    depth, length = lax.axis_size("gz"), lax.axis_size("gx")
    received = []
    for face, odd in ((far, 1), (near, 0)):
        pairs = []
        for z in range(depth):
            other = z + 1 if z % 2 == odd else z - 1
            for x in range(length):
                to = other * length + x if 0 <= other < depth else z * length + (x ^ 1)
                pairs.append((z * length + x, to))
        received.append(lax.ppermute(face, ("gz", "gx"), pairs))
    return received[1], received[0]


def swap_inner(inner):
    return lax.ppermute(inner, "gx", [(i, i ^ 1) for i in range(lax.axis_size("gx"))])


def swap_outer(outer):
    length = lax.axis_size("gx")
    pairs = [(i, (i + 1) % length if i % 2 else (i - 1) % length) for i in range(length)]
    return lax.ppermute(outer, "gx", pairs)


def per_device(populations, rates, grain_fraction, grain_velocity, grain_dest, grain_line):
    _, depth, length, width = populations.shape
    lines = depth * length
    devices = lax.axis_size("gz") * lax.axis_size("gx")
    grains = grain_fraction.shape[0]
    capacity = 2 * grains // devices
    slots = devices * capacity
    shape, both = jax.ShapeDtypeStruct, ("gz", "gx")
    dest, line = grain_dest.reshape(1, grains), grain_line.reshape(1, grains)
    rows = devices * (capacity + 2)
    earlier, spread = call(
        functools.partial(tables_kernel, capacity), [shape((LANES, LANES), bf16)] * 2, flops=10**9
    )
    rank, facts, rates = call(
        functools.partial(rank_kernel, devices),
        [shape((1, grains), i32), shape((4, grains), f32), shape((1, 27), f32)],
        dest, line, grain_velocity, rates.reshape(1, 27), earlier,
    )
    (send,) = call(
        functools.partial(pack_kernel, devices, capacity),
        [shape((rows, width), bf16)],
        dest, rank, facts, grain_fraction,
        scratch=[pltpu.VMEM((rows, width), f32)],
    )
    recv = lax.all_to_all(
        send.reshape(devices, capacity // 2 + 1, 2, width), both, split_axis=0, concat_axis=0, tiled=True
    ).reshape(rows, width)
    state = shape(populations.shape, f32)
    face, ends = shape((9, length, width), f32), shape((9 * depth, width), f32)
    post, outer, inner, push, held, slot_line, slot_rows = call(
        functools.partial(first_kernel, devices, capacity),
        [
            state, ends, ends, shape((3, depth, length, width), f32),
            shape((4 * lines, width), f32), shape((slots // LANES, LANES), i32), shape((slots, width), bf16),
        ],
        recv, populations, rates, spread, scratch=[pltpu.VMEM((rows, width), f32)],
    )
    outer, inner = swap_outer(outer), swap_inner(inner)
    turned, hot, at_rank = call(
        turn_kernel,
        [shape((width, slots), bf16), shape((2 * devices, grains), bf16), shape((capacity, grains), f32)],
        slot_rows, dest, rank,
    )
    near, far = swap_faces(*call(faces_kernel, [face, face], post, outer, inner))
    post, next_near, next_far, inner, outer, back = call(
        functools.partial(second_kernel, capacity),
        [state, face, face, ends, ends, shape((4 * devices, LANES), f32)],
        rates, post, outer, inner, far, near, held, push, slot_line, turned,
    )
    back = lax.all_to_all(
        back.reshape(devices, 4, LANES), both, split_axis=0, concat_axis=0, tiled=True
    ).reshape(4 * devices, LANES)
    outer = swap_outer(outer)
    near, far = swap_faces(next_near, next_far)
    inner = swap_inner(inner)
    scaled, grain_force = call(
        functools.partial(last_kernel, capacity),
        [state, shape((3, grains), f32)],
        post, near, far, outer, inner, back, hot, at_rank,
    )
    return (scaled, grain_force)


def solution(mesh):
    in_specs = (
        P(None, "gz", "gx", None),
        P(),
        P(("gz", "gx"), None),
        P(None, ("gz", "gx")),
        P(("gz", "gx"), None),
        P(("gz", "gx")),
    )
    out_specs = (P(None, "gz", "gx", None), P(None, ("gz", "gx")))
    return jax.shard_map(
        per_device, mesh=mesh, in_specs=in_specs, out_specs=out_specs, check_vma=False
    )
```

```python
import functools

import jax
import jax.numpy as jnp
import numpy as np
from jax import lax
from jax.experimental import pallas as pl
from jax.experimental.pallas import tpu as pltpu
from jax.sharding import PartitionSpec as P

STEPS = 2
LANES = 128
f32, bf16, i32 = jnp.float32, jnp.bfloat16, jnp.int32
DIGITS = [(i // 9, i // 3 % 3, i % 3) for i in range(27)]
STEP = [tuple(d - 1 for d in digits) for digits in DIGITS]
WEIGHT = [(8.0 / 27, 2.0 / 27, 1.0 / 54, 1.0 / 216)[sum(abs(s) for s in step)] for step in STEP]


def iota(shape, dim):
    return lax.broadcasted_iota(i32, shape, dim)


def call(kernel, outs, *operands, scratch=(), flops=0):
    size = sum(o.size * o.dtype.itemsize for o in operands) + sum(
        int(np.prod(o.shape)) * o.dtype.itemsize for o in outs
    )
    return pl.pallas_call(
        kernel,
        out_shape=list(outs),
        in_specs=[pl.BlockSpec(memory_space=pltpu.VMEM)] * len(operands),
        out_specs=[pl.BlockSpec(memory_space=pltpu.VMEM)] * len(outs),
        scratch_shapes=list(scratch),
        compiler_params=pltpu.CompilerParams(vmem_limit_bytes=24 * 1024 * 1024),
        cost_estimate=pl.CostEstimate(flops=flops, bytes_accessed=size, transcendentals=0),
    )(*operands)


def device_at(step_z, step_x):
    depth, length = lax.axis_size("gz"), lax.axis_size("gx")
    z = lax.rem(lax.axis_index("gz") + step_z + depth, depth)
    x = lax.rem(lax.axis_index("gx") + step_x + length, length)
    return z * length + x


def split2(x):
    high = x.astype(bf16)
    return high, (x - high.astype(f32)).astype(bf16)


def tables_kernel(capacity, earlier_ref, spread_ref):
    row, column = iota(earlier_ref.shape, 0), iota(earlier_ref.shape, 1)
    earlier_ref[...] = jnp.where(row < column, 1.0, 0.0).astype(bf16)
    spread_ref[...] = jnp.where(row % capacity == column % capacity, 1.0, 0.0).astype(bf16)


def ranks(hot, earlier):
    devices, grains = hot.shape
    total = jnp.zeros((devices, 1), f32)
    parts = []
    for start in range(0, grains, LANES):
        part = hot[:, start : start + LANES]
        before = jnp.dot(part.astype(bf16), earlier, preferred_element_type=f32) + total
        parts.append(jnp.sum(part * before, axis=0, keepdims=True))
        total = total + jnp.sum(part, axis=1, keepdims=True)
    return jnp.concatenate(parts, axis=1)


def rank_kernel(
    devices, dest_ref, line_ref, speed_ref, rates_ref, earlier_ref, rank_ref, facts_ref, rates_out_ref
):
    hot = jnp.where(iota((devices, dest_ref.shape[1]), 0) == dest_ref[...], 1.0, 0.0)
    rank_ref[...] = ranks(hot, earlier_ref[...]).astype(i32)
    facts_ref[0:3] = speed_ref[...].astype(f32)
    facts_ref[3:4] = line_ref[...].astype(f32)
    rates_out_ref[...] = rates_ref[...]


def pack_kernel(devices, capacity, dest_ref, rank_ref, facts_ref, fraction_ref, send_ref, rows_ref):
    grains, width = fraction_ref.shape
    dest, rank = dest_ref[...], rank_ref[...]
    place = jnp.where(iota((rows_ref.shape[0], grains), 0) == dest * (capacity + 2) + rank, 1.0, 0.0)
    rows_ref[...] = jnp.dot(place.astype(bf16), fraction_ref[...], preferred_element_type=f32)
    at_rank = iota((capacity, grains), 0) == rank
    facts = [jnp.where(at_rank, facts_ref[m : m + 1], 0.0) for m in range(4)]
    if 4 * capacity < width:
        facts.append(jnp.zeros((width - 4 * capacity, grains), f32))
    rows_ref[pl.ds(capacity, devices, stride=capacity + 2), :] = lax.dot_general(
        jnp.where(iota((devices, grains), 0) == dest, 1.0, 0.0).astype(bf16),
        jnp.concatenate(facts, axis=0).astype(bf16),
        (((1,), (1,)), ((), ())),
        preferred_element_type=f32,
    )
    send_ref[...] = rows_ref[...].astype(bf16)


def total_of(values):
    return functools.reduce(lambda a, b: a + b, values)


def along(speed, i):
    return total_of([v if s > 0 else -v for s, v in zip(STEP[i], speed) if s])


def relax(fields, rate):
    density = total_of(fields)
    momentum = [
        total_of([fields[i] for i in range(27) if STEP[i][axis] == 1])
        - total_of([fields[i] for i in range(27) if STEP[i][axis] == -1])
        for axis in range(3)
    ]
    inverse = 1.0 / density
    speed = [m * inverse for m in momentum]
    base = 1.0 - 1.5 * total_of([v * v for v in speed])
    departure = [None] * 27
    for i in range(13, 27):
        scale = WEIGHT[i] * density
        if i == 13:
            departure[i] = fields[i] - scale * base
            continue
        dot = along(speed, i)
        even, odd = scale * (base + 4.5 * dot * dot), scale * (3.0 * dot)
        departure[i] = fields[i] - (even + odd)
        departure[26 - i] = fields[26 - i] - (even - odd)
    moments = list(departure)
    for stride in (1, 3, 9):
        for i in range(27):
            if i // stride % 3 == 0:
                low, mid, high = moments[i], moments[i + stride], moments[i + 2 * stride]
                both = low + high
                moments[i], moments[i + stride], moments[i + 2 * stride] = both + mid, high - low, both
    moments = [rate[a] * moments[a] for a in range(27)]
    for stride in (9, 3, 1):
        for i in range(27):
            if i // stride % 3 == 0:
                m0, m1, m2 = moments[i], moments[i + stride], moments[i + 2 * stride]
                half1, half2 = 0.5 * m1, 0.5 * m2
                moments[i], moments[i + stride], moments[i + 2 * stride] = half2 - half1, m0 - m2, half2 + half1
    kept = [fields[i] - moments[i] for i in range(27)]
    swapped = [departure[26 - i] - kept[i] for i in range(27)]
    return density, momentum, kept, swapped


def exchange(density, momentum, kept, swapped, solid, carried):
    inverse = 1.0 / (1.0 + solid)
    share = solid * inverse
    speed = [c * inverse for c in carried]
    base = 1.0 - 1.5 * total_of([v * v for v in speed])
    push = [(density * v - m) * inverse for v, m in zip(speed, momentum)]
    post = [None] * 27
    for i in range(13, 27):
        scale = WEIGHT[i] * density
        if i == 13:
            post[i] = kept[i] + share * (swapped[i] + scale * base)
            continue
        dot = along(speed, i)
        even, odd = scale * (base + 4.5 * dot * dot), scale * (3.0 * dot)
        post[i] = kept[i] + share * (swapped[i] + (even + odd))
        post[26 - i] = kept[26 - i] + share * (swapped[26 - i] + (even - odd))
    return post, push


def grains_at(held_ref, z, depth, length):
    lines = depth * length
    first = [held_ref[k * lines + z * length : k * lines + (z + 1) * length, :] for k in range(4)]
    return first[0], first[1:]


def even_place(axis):
    return lax.axis_index(axis) % 2 == 0


def store_faces(post_ref, near_ref, far_ref):
    top = post_ref.shape[1] - 1
    for n in range(9):
        up, down = post_ref[n + 18, top], post_ref[n, 0]
        near_ref[n] = jnp.where(even_place("gz"), up, down)
        far_ref[n] = jnp.where(even_place("gz"), down, up)


def end_row(i, z, depth):
    return ((STEP[i][0] + 1) * 3 + STEP[i][2] + 1) * depth + z


def store_ends(post_ref, inner_ref, outer_ref):
    depth, length = post_ref.shape[1], post_ref.shape[2]
    for i in range(27):
        if STEP[i][1] == 1:
            for z in range(depth):
                n = end_row(i, z, depth)
                right, left = post_ref[i, z, length - 1 : length], post_ref[i - 6, z, 0:1]
                inner_ref[n : n + 1] = jnp.where(even_place("gx"), right, left)
                outer_ref[n : n + 1] = jnp.where(even_place("gx"), left, right)


def end_from(i, outer, inner):
    if STEP[i][1] > 0:
        return jnp.where(even_place("gx"), outer, inner)
    return jnp.where(even_place("gx"), inner, outer)


def moved_along_x(field, i, end):
    cx, length = STEP[i][1], field.shape[0]
    place = 0 if cx > 0 else length - 1
    return jnp.where(iota(field.shape, 0) == place, end, pltpu.roll(field, cx % length, 0))


def across(near, far, i):
    if STEP[i][0] > 0:
        return jnp.where(even_place("gz"), far, near)
    return jnp.where(even_place("gz"), near, far)


def first_kernel(
    devices, capacity, recv_ref, fields_ref, rates_ref, spread_ref,
    post_ref, outer_ref, inner_ref, far_ref, near_ref, push_ref, held_ref, line_ref, slot_ref, wide_ref,
):
    width = recv_ref.shape[1]
    block, slots = capacity + 2, devices * capacity
    depth, length = fields_ref.shape[1], fields_ref.shape[2]
    lines = depth * length
    rate = [rates_ref[:, a : a + 1] for a in range(27)]
    wide_ref[...] = recv_ref[...].astype(f32)
    slot_rows = jnp.concatenate(
        [wide_ref[j * block : j * block + capacity] for j in range(devices)], axis=0
    ).astype(bf16)
    slot_ref[...] = slot_rows
    tiles, shared = slots // LANES, LANES // capacity
    group = iota((tiles, width), 1) // capacity
    rows = [wide_ref[pl.ds(capacity + a * block, tiles, stride=shared * block), :] for a in range(shared)]
    picked = jnp.concatenate([jnp.where(group == m, row, 0.0) for m in range(4) for row in rows], axis=0)
    placed = jnp.dot(picked.astype(bf16), spread_ref[...], preferred_element_type=f32)
    fact = []
    for m in range(4):
        first = m * shared * tiles
        fact.append(
            total_of(
                [
                    jnp.where(group == a, placed[first + a * tiles : first + (a + 1) * tiles], 0.0)
                    for a in range(shared)
                ]
            )
        )
    line_ref[...] = fact[3].astype(i32)
    gather = []
    for t in range(tiles):
        on_line = iota((lines, LANES), 0) == fact[3][t : t + 1].astype(i32)
        gather.append(
            jnp.concatenate(
                [jnp.where(on_line, 1.0, 0.0)]
                + [jnp.where(on_line, fact[k][t : t + 1], 0.0) for k in range(3)],
                axis=0,
            ).astype(bf16)
        )
    held_ref[...] = jnp.dot(jnp.concatenate(gather, axis=1), slot_rows, preferred_element_type=f32)
    for z in range(depth):
        relaxed = relax([fields_ref[i, z] for i in range(27)], rate)
        post, push = exchange(*relaxed, *grains_at(held_ref, z, depth, length))
        for i in range(27):
            post_ref[i, z] = post[i]
        for k in range(3):
            push_ref[k, z] = push[k]
    store_ends(post_ref, inner_ref, outer_ref)
    store_faces(post_ref, near_ref, far_ref)


def turn_kernel(slot_ref, dest_ref, rank_ref, turned_ref, hot_ref, at_rank_ref):
    turned_ref[...] = slot_ref[...].astype(f32).T.astype(bf16)
    devices = hot_ref.shape[0] // 2
    hot_ref[...] = jnp.where(iota(hot_ref.shape, 0) % devices == dest_ref[...], 1.0, 0.0).astype(bf16)
    at_rank_ref[...] = jnp.where(iota(at_rank_ref.shape, 0) == rank_ref[...], 1.0, 0.0)


def corners_kernel(depth, outer_ref, inner_ref, far_ref, near_ref):
    for i in range(9):
        if STEP[i][1]:
            up, down = [
                end_from(i, outer_ref[n : n + 1], inner_ref[n : n + 1])
                for n in (end_row(18 + i, depth - 1, depth), end_row(i, 0, depth))
            ]
            n = corner_row(i)
            near_ref[n : n + 1] = jnp.where(even_place("gz"), up, down)
            far_ref[n : n + 1] = jnp.where(even_place("gz"), down, up)


def corner_row(i):
    return (3 if STEP[i][1] > 0 else 0) + STEP[i][2] + 1


def streamed(post_ref, outer_ref, inner_ref, far_ref, near_ref, z, corner):
    depth, width = post_ref.shape[1], post_ref.shape[3]
    moved_list = []
    for i in range(27):
        cz, cx, cy = STEP[i]
        source = z - cz
        inside = 0 <= source < depth
        moved = post_ref[i, source] if inside else across(near_ref[i % 9], far_ref[i % 9], i)
        if cx and inside:
            n = end_row(i, source, depth)
            moved = moved_along_x(moved, i, end_from(i, outer_ref[n : n + 1], inner_ref[n : n + 1]))
        elif cx:
            moved = moved_along_x(moved, i, corner(i))
        if cy:
            moved = pltpu.roll(moved, cy % width, 1)
        if not inside:
            wall = 0 if cz > 0 else lax.axis_size("gz") - 1
            moved = jnp.where(lax.axis_index("gz") == wall, post_ref[26 - i, z], moved)
        moved_list.append(moved)
    return moved_list


def second_kernel(
    capacity, rates_ref, post_ref, outer_ref, inner_ref, far_ref, near_ref, far_rows_ref, near_rows_ref,
    held_ref, push_ref, line_ref, turned_ref,
    next_ref, next_near_ref, next_far_ref, next_inner_ref, next_outer_ref, back_ref,
):
    depth, length, width = post_ref.shape[1:]
    lines = depth * length
    slots = turned_ref.shape[1]
    halo = (outer_ref, inner_ref, far_ref, near_ref)
    rate = [rates_ref[:, a : a + 1] for a in range(27)]

    def corner(i):
        n = corner_row(i)
        return across(near_rows_ref[n : n + 1], far_rows_ref[n : n + 1], i)

    pushes = []
    for z in range(depth):
        relaxed = relax(streamed(post_ref, *halo, z, corner), rate)
        post, push = exchange(*relaxed, *grains_at(held_ref, z, depth, length))
        for i in range(27):
            next_ref[i, z] = post[i]
        pushes.append(push)
    store_faces(next_ref, next_near_ref, next_far_ref)
    store_ends(next_ref, next_inner_ref, next_outer_ref)
    back_ref[...] = jnp.zeros(back_ref.shape, f32)
    for i in range(27):
        cz, cx, cy = STEP[i]
        if cz and cx:
            z, x = depth - 1 if cz > 0 else 0, length - 1 if cx > 0 else 0
            back_ref[pl.ds(4 * device_at(cz, cx) + 2 + cy, 1)] = next_ref[i, z, x : x + 1]
    total = jnp.concatenate(
        [push_ref[k, z] + pushes[z][k] for k in range(3) for z in range(depth)], axis=0
    )
    along_y = jnp.dot(
        jnp.concatenate(split2(total), axis=0), turned_ref[...], preferred_element_type=f32
    )
    along_y = along_y[: 3 * lines] + along_y[3 * lines :]
    tiles, per_tile = slots // LANES, LANES // capacity
    group = iota((tiles, LANES), 1) // capacity
    force = [[], [], []]
    for t in range(tiles):
        on_line = iota((lines, LANES), 0) == line_ref[t : t + 1]
        for k in range(3):
            part = along_y[k * lines : (k + 1) * lines, t * LANES : (t + 1) * LANES]
            force[k].append(-jnp.sum(jnp.where(on_line, part, 0.0), axis=0, keepdims=True))
    force = [jnp.concatenate(parts, axis=0) for parts in force]
    for a in range(per_tile):
        block = jnp.zeros((tiles, LANES), f32)
        for k in range(3):
            shift = (k - a) * capacity % LANES
            turned = pltpu.roll(force[k], shift, 1) if shift else force[k]
            block = jnp.where(group == k, turned, block)
        back_ref[pl.ds(4 * a, tiles, stride=4 * per_tile), :] = block


def last_kernel(
    capacity, post_ref, near_ref, far_ref, outer_ref, inner_ref, back_ref, hot_ref, at_rank_ref,
    scaled_ref, force_ref,
):
    def corner(i):
        cz, cx, cy = STEP[i]
        return back_ref[pl.ds(4 * device_at(-cz, -cx) + 2 + cy, 1)]

    for z in range(post_ref.shape[1]):
        fields = streamed(post_ref, outer_ref, inner_ref, far_ref, near_ref, z, corner)
        for i in range(27):
            scaled_ref[i, z] = fields[i] * (1.0 / WEIGHT[i])
    back = back_ref[pl.ds(0, hot_ref.shape[0] // 2, stride=4), :]
    parts = jnp.concatenate([part.astype(f32) for part in split2(back)], axis=0).T
    picked = jnp.dot(parts.astype(bf16), hot_ref[...], preferred_element_type=f32)
    for k in range(3):
        mine = at_rank_ref[...] * picked[k * capacity : (k + 1) * capacity]
        force_ref[k : k + 1] = jnp.sum(mine, axis=0, keepdims=True)


def swap_faces(near, far):
    depth, length = lax.axis_size("gz"), lax.axis_size("gx")
    received = []
    for face, odd in ((far, 1), (near, 0)):
        pairs = []
        for z in range(depth):
            other = z + 1 if z % 2 == odd else z - 1
            for x in range(length):
                to = other * length + x if 0 <= other < depth else z * length + (x ^ 1)
                pairs.append((z * length + x, to))
        received.append(lax.ppermute(face, ("gz", "gx"), pairs))
    return received[1], received[0]


def swap_inner(inner):
    return lax.ppermute(inner, "gx", [(i, i ^ 1) for i in range(lax.axis_size("gx"))])


def swap_outer(outer):
    length = lax.axis_size("gx")
    pairs = [(i, (i + 1) % length if i % 2 else (i - 1) % length) for i in range(length)]
    return lax.ppermute(outer, "gx", pairs)


def per_device(populations, rates, grain_fraction, grain_velocity, grain_dest, grain_line):
    _, depth, length, width = populations.shape
    lines = depth * length
    devices = lax.axis_size("gz") * lax.axis_size("gx")
    grains = grain_fraction.shape[0]
    capacity = 2 * grains // devices
    slots = devices * capacity
    shape, both = jax.ShapeDtypeStruct, ("gz", "gx")
    dest, line = grain_dest.reshape(1, grains), grain_line.reshape(1, grains)
    rows = devices * (capacity + 2)
    earlier, spread = call(
        functools.partial(tables_kernel, capacity), [shape((LANES, LANES), bf16)] * 2, flops=10**9
    )
    rank, facts, rates = call(
        functools.partial(rank_kernel, devices),
        [shape((1, grains), i32), shape((4, grains), f32), shape((1, 27), f32)],
        dest, line, grain_velocity, rates.reshape(1, 27), earlier,
    )
    (send,) = call(
        functools.partial(pack_kernel, devices, capacity),
        [shape((rows, width), bf16)],
        dest, rank, facts, grain_fraction,
        scratch=[pltpu.VMEM((rows, width), f32)],
    )
    recv = lax.all_to_all(
        send.reshape(devices, capacity // 2 + 1, 2, width), both, split_axis=0, concat_axis=0, tiled=True
    ).reshape(rows, width)
    state = shape(populations.shape, f32)
    face, ends = shape((9, length, width), f32), shape((9 * depth, width), f32)
    post, outer, inner, far, near, push, held, slot_line, slot_rows = call(
        functools.partial(first_kernel, devices, capacity),
        [
            state, ends, ends, face, face, shape((3, depth, length, width), f32),
            shape((4 * lines, width), f32), shape((slots // LANES, LANES), i32), shape((slots, width), bf16),
        ],
        recv, populations, rates, spread, scratch=[pltpu.VMEM((rows, width), f32)],
    )
    outer, inner = swap_outer(outer), swap_inner(inner)
    near, far = swap_faces(near, far)
    turned, hot, at_rank = call(
        turn_kernel,
        [shape((width, slots), bf16), shape((2 * devices, grains), bf16), shape((capacity, grains), f32)],
        slot_rows, dest, rank,
    )
    corners = shape((6, width), f32)
    far_rows, near_rows = call(
        functools.partial(corners_kernel, depth), [corners, corners], outer, inner, flops=10**10
    )
    near_rows, far_rows = swap_faces(near_rows, far_rows)
    post, next_near, next_far, inner, outer, back = call(
        functools.partial(second_kernel, capacity),
        [state, face, face, ends, ends, shape((4 * devices, LANES), f32)],
        rates, post, outer, inner, far, near, far_rows, near_rows, held, push, slot_line, turned,
    )
    back = lax.all_to_all(
        back.reshape(devices, 4, LANES), both, split_axis=0, concat_axis=0, tiled=True
    ).reshape(4 * devices, LANES)
    outer = swap_outer(outer)
    near, far = swap_faces(next_near, next_far)
    inner = swap_inner(inner)
    scaled, grain_force = call(
        functools.partial(last_kernel, capacity),
        [state, shape((3, grains), f32)],
        post, near, far, outer, inner, back, hot, at_rank,
    )
    return (scaled, grain_force)


def solution(mesh):
    in_specs = (
        P(None, "gz", "gx", None),
        P(),
        P(("gz", "gx"), None),
        P(None, ("gz", "gx")),
        P(("gz", "gx"), None),
        P(("gz", "gx")),
    )
    out_specs = (P(None, "gz", "gx", None), P(None, ("gz", "gx")))
    return jax.shard_map(
        per_device, mesh=mesh, in_specs=in_specs, out_specs=out_specs, check_vma=False
    )
```

```python
import functools

import jax
import jax.numpy as jnp
import numpy as np
from jax import lax
from jax.experimental import pallas as pl
from jax.experimental.pallas import tpu as pltpu
from jax.sharding import PartitionSpec as P

STEPS = 2
LANES = 128
f32, bf16, i32 = jnp.float32, jnp.bfloat16, jnp.int32
DIGITS = [(i // 9, i // 3 % 3, i % 3) for i in range(27)]
STEP = [tuple(d - 1 for d in digits) for digits in DIGITS]
WEIGHT = [(8.0 / 27, 2.0 / 27, 1.0 / 54, 1.0 / 216)[sum(abs(s) for s in step)] for step in STEP]


def iota(shape, dim):
    return lax.broadcasted_iota(i32, shape, dim)


def call(kernel, outs, *operands, scratch=(), flops=0):
    size = sum(o.size * o.dtype.itemsize for o in operands) + sum(
        int(np.prod(o.shape)) * o.dtype.itemsize for o in outs
    )
    return pl.pallas_call(
        kernel,
        out_shape=list(outs),
        in_specs=[pl.BlockSpec(memory_space=pltpu.VMEM)] * len(operands),
        out_specs=[pl.BlockSpec(memory_space=pltpu.VMEM)] * len(outs),
        scratch_shapes=list(scratch),
        compiler_params=pltpu.CompilerParams(vmem_limit_bytes=24 * 1024 * 1024),
        cost_estimate=pl.CostEstimate(flops=flops, bytes_accessed=size, transcendentals=0),
    )(*operands)


def device_at(step_z, step_x):
    depth, length = lax.axis_size("gz"), lax.axis_size("gx")
    z = lax.rem(lax.axis_index("gz") + step_z + depth, depth)
    x = lax.rem(lax.axis_index("gx") + step_x + length, length)
    return z * length + x


def split2(x):
    high = x.astype(bf16)
    return high, (x - high.astype(f32)).astype(bf16)


def tables_kernel(capacity, earlier_ref, spread_ref):
    row, column = iota(earlier_ref.shape, 0), iota(earlier_ref.shape, 1)
    earlier_ref[...] = jnp.where(row < column, 1.0, 0.0).astype(bf16)
    spread_ref[...] = jnp.where(row % capacity == column % capacity, 1.0, 0.0).astype(bf16)


def ranks(hot, earlier):
    devices, grains = hot.shape
    total = jnp.zeros((devices, 1), f32)
    parts = []
    for start in range(0, grains, LANES):
        part = hot[:, start : start + LANES]
        before = jnp.dot(part.astype(bf16), earlier, preferred_element_type=f32) + total
        parts.append(jnp.sum(part * before, axis=0, keepdims=True))
        total = total + jnp.sum(part, axis=1, keepdims=True)
    return jnp.concatenate(parts, axis=1)


def rank_kernel(
    devices, dest_ref, line_ref, speed_ref, rates_ref, earlier_ref, rank_ref, facts_ref, rates_out_ref
):
    hot = jnp.where(iota((devices, dest_ref.shape[1]), 0) == dest_ref[...], 1.0, 0.0)
    rank_ref[...] = ranks(hot, earlier_ref[...]).astype(i32)
    facts_ref[0:3] = speed_ref[...].astype(f32)
    facts_ref[3:4] = line_ref[...].astype(f32)
    rates_out_ref[...] = rates_ref[...]


def pack_kernel(devices, capacity, dest_ref, rank_ref, facts_ref, fraction_ref, send_ref, rows_ref):
    grains, width = fraction_ref.shape
    dest, rank = dest_ref[...], rank_ref[...]
    place = jnp.where(iota((rows_ref.shape[0], grains), 0) == dest * (capacity + 2) + rank, 1.0, 0.0)
    rows_ref[...] = jnp.dot(place.astype(bf16), fraction_ref[...], preferred_element_type=f32)
    at_rank = iota((capacity, grains), 0) == rank
    facts = [jnp.where(at_rank, facts_ref[m : m + 1], 0.0) for m in range(4)]
    if 4 * capacity < width:
        facts.append(jnp.zeros((width - 4 * capacity, grains), f32))
    rows_ref[pl.ds(capacity, devices, stride=capacity + 2), :] = lax.dot_general(
        jnp.where(iota((devices, grains), 0) == dest, 1.0, 0.0).astype(bf16),
        jnp.concatenate(facts, axis=0).astype(bf16),
        (((1,), (1,)), ((), ())),
        preferred_element_type=f32,
    )
    send_ref[...] = rows_ref[...].astype(bf16)


def total_of(values):
    return functools.reduce(lambda a, b: a + b, values)


def along(speed, i):
    return total_of([v if s > 0 else -v for s, v in zip(STEP[i], speed) if s])


def relax(fields, rate):
    density = total_of(fields)
    momentum = [
        total_of([fields[i] for i in range(27) if STEP[i][axis] == 1])
        - total_of([fields[i] for i in range(27) if STEP[i][axis] == -1])
        for axis in range(3)
    ]
    inverse = 1.0 / density
    speed = [m * inverse for m in momentum]
    base = 1.0 - 1.5 * total_of([v * v for v in speed])
    departure = [None] * 27
    for i in range(13, 27):
        scale = WEIGHT[i] * density
        if i == 13:
            departure[i] = fields[i] - scale * base
            continue
        dot = along(speed, i)
        even, odd = scale * (base + 4.5 * dot * dot), scale * (3.0 * dot)
        departure[i] = fields[i] - (even + odd)
        departure[26 - i] = fields[26 - i] - (even - odd)
    moments = list(departure)
    for stride in (1, 3, 9):
        for i in range(27):
            if i // stride % 3 == 0:
                low, mid, high = moments[i], moments[i + stride], moments[i + 2 * stride]
                both = low + high
                moments[i], moments[i + stride], moments[i + 2 * stride] = both + mid, high - low, both
    moments = [rate[a] * moments[a] for a in range(27)]
    for stride in (9, 3, 1):
        for i in range(27):
            if i // stride % 3 == 0:
                m0, m1, m2 = moments[i], moments[i + stride], moments[i + 2 * stride]
                half1, half2 = 0.5 * m1, 0.5 * m2
                moments[i], moments[i + stride], moments[i + 2 * stride] = half2 - half1, m0 - m2, half2 + half1
    kept = [fields[i] - moments[i] for i in range(27)]
    swapped = [departure[26 - i] - kept[i] for i in range(27)]
    return density, momentum, kept, swapped


def exchange(density, momentum, kept, swapped, solid, carried):
    inverse = 1.0 / (1.0 + solid)
    share = solid * inverse
    speed = [c * inverse for c in carried]
    base = 1.0 - 1.5 * total_of([v * v for v in speed])
    push = [(density * v - m) * inverse for v, m in zip(speed, momentum)]
    post = [None] * 27
    for i in range(13, 27):
        scale = WEIGHT[i] * density
        if i == 13:
            post[i] = kept[i] + share * (swapped[i] + scale * base)
            continue
        dot = along(speed, i)
        even, odd = scale * (base + 4.5 * dot * dot), scale * (3.0 * dot)
        post[i] = kept[i] + share * (swapped[i] + (even + odd))
        post[26 - i] = kept[26 - i] + share * (swapped[26 - i] + (even - odd))
    return post, push


def grains_at(held_ref, z, depth, length):
    lines = depth * length
    first = [held_ref[k * lines + z * length : k * lines + (z + 1) * length, :] for k in range(4)]
    return first[0], first[1:]


def even_place(axis):
    return lax.axis_index(axis) % 2 == 0


def store_faces(post_ref, near_ref, far_ref):
    top = post_ref.shape[1] - 1
    for n in range(9):
        up, down = post_ref[n + 18, top], post_ref[n, 0]
        near_ref[n] = jnp.where(even_place("gz"), up, down)
        far_ref[n] = jnp.where(even_place("gz"), down, up)


def end_row(i, z, depth):
    return ((STEP[i][0] + 1) * 3 + STEP[i][2] + 1) * depth + z


def store_ends(post_ref, inner_ref, outer_ref):
    depth, length = post_ref.shape[1], post_ref.shape[2]
    for i in range(27):
        if STEP[i][1] == 1:
            for z in range(depth):
                n = end_row(i, z, depth)
                right, left = post_ref[i, z, length - 1 : length], post_ref[i - 6, z, 0:1]
                inner_ref[n : n + 1] = jnp.where(even_place("gx"), right, left)
                outer_ref[n : n + 1] = jnp.where(even_place("gx"), left, right)


def end_from(i, outer, inner):
    if STEP[i][1] > 0:
        return jnp.where(even_place("gx"), outer, inner)
    return jnp.where(even_place("gx"), inner, outer)


def moved_along_x(field, i, end):
    cx, length = STEP[i][1], field.shape[0]
    place = 0 if cx > 0 else length - 1
    return jnp.where(iota(field.shape, 0) == place, end, pltpu.roll(field, cx % length, 0))


def across(near, far, i):
    if STEP[i][0] > 0:
        return jnp.where(even_place("gz"), far, near)
    return jnp.where(even_place("gz"), near, far)


def first_kernel(
    devices, capacity, recv_ref, fields_ref, rates_ref, spread_ref,
    post_ref, outer_ref, inner_ref, far_ref, near_ref, push_ref, held_ref, line_ref, slot_ref, wide_ref,
):
    width = recv_ref.shape[1]
    block, slots = capacity + 2, devices * capacity
    depth, length = fields_ref.shape[1], fields_ref.shape[2]
    lines = depth * length
    rate = [rates_ref[:, a : a + 1] for a in range(27)]
    wide_ref[...] = recv_ref[...].astype(f32)
    slot_rows = jnp.concatenate(
        [wide_ref[j * block : j * block + capacity] for j in range(devices)], axis=0
    ).astype(bf16)
    slot_ref[...] = slot_rows
    tiles, shared = slots // LANES, LANES // capacity
    group = iota((tiles, width), 1) // capacity
    rows = [wide_ref[pl.ds(capacity + a * block, tiles, stride=shared * block), :] for a in range(shared)]
    picked = jnp.concatenate([jnp.where(group == m, row, 0.0) for m in range(4) for row in rows], axis=0)
    placed = jnp.dot(picked.astype(bf16), spread_ref[...], preferred_element_type=f32)
    fact = []
    for m in range(4):
        first = m * shared * tiles
        fact.append(
            total_of(
                [
                    jnp.where(group == a, placed[first + a * tiles : first + (a + 1) * tiles], 0.0)
                    for a in range(shared)
                ]
            )
        )
    line_ref[...] = fact[3].astype(i32)
    gather = []
    for t in range(tiles):
        on_line = iota((lines, LANES), 0) == fact[3][t : t + 1].astype(i32)
        gather.append(
            jnp.concatenate(
                [jnp.where(on_line, 1.0, 0.0)]
                + [jnp.where(on_line, fact[k][t : t + 1], 0.0) for k in range(3)],
                axis=0,
            ).astype(bf16)
        )
    held_ref[...] = jnp.dot(jnp.concatenate(gather, axis=1), slot_rows, preferred_element_type=f32)
    for z in range(depth):
        relaxed = relax([fields_ref[i, z] for i in range(27)], rate)
        post, push = exchange(*relaxed, *grains_at(held_ref, z, depth, length))
        for i in range(27):
            post_ref[i, z] = post[i]
        for k in range(3):
            push_ref[k, z] = push[k]
    store_ends(post_ref, inner_ref, outer_ref)
    store_faces(post_ref, near_ref, far_ref)


def turn_kernel(slot_ref, dest_ref, rank_ref, turned_ref, hot_ref, at_rank_ref):
    turned_ref[...] = slot_ref[...].astype(f32).T.astype(bf16)
    devices = hot_ref.shape[0] // 2
    hot_ref[...] = jnp.where(iota(hot_ref.shape, 0) % devices == dest_ref[...], 1.0, 0.0).astype(bf16)
    at_rank_ref[...] = jnp.where(iota(at_rank_ref.shape, 0) == rank_ref[...], 1.0, 0.0)


def corners_kernel(depth, outer_ref, inner_ref, far_ref, near_ref):
    for i in range(9):
        if STEP[i][1]:
            up, down = [
                end_from(i, outer_ref[n : n + 1], inner_ref[n : n + 1])
                for n in (end_row(18 + i, depth - 1, depth), end_row(i, 0, depth))
            ]
            n = corner_row(i)
            near_ref[n : n + 1] = jnp.where(even_place("gz"), up, down)
            far_ref[n : n + 1] = jnp.where(even_place("gz"), down, up)


def corner_row(i):
    return (3 if STEP[i][1] > 0 else 0) + STEP[i][2] + 1


def streamed(post_ref, outer_ref, inner_ref, far_ref, near_ref, z, corner):
    depth, width = post_ref.shape[1], post_ref.shape[3]
    moved_list = []
    for i in range(27):
        cz, cx, cy = STEP[i]
        source = z - cz
        inside = 0 <= source < depth
        moved = post_ref[i, source] if inside else across(near_ref[i % 9], far_ref[i % 9], i)
        if cx and inside:
            n = end_row(i, source, depth)
            moved = moved_along_x(moved, i, end_from(i, outer_ref[n : n + 1], inner_ref[n : n + 1]))
        elif cx:
            moved = moved_along_x(moved, i, corner(i))
        if cy:
            moved = pltpu.roll(moved, cy % width, 1)
        if not inside:
            wall = 0 if cz > 0 else lax.axis_size("gz") - 1
            moved = jnp.where(lax.axis_index("gz") == wall, post_ref[26 - i, z], moved)
        moved_list.append(moved)
    return moved_list


def second_kernel(
    capacity, rates_ref, post_ref, outer_ref, inner_ref, far_ref, near_ref, far_rows_ref, near_rows_ref,
    held_ref, push_ref, line_ref, turned_ref,
    next_ref, next_near_ref, next_far_ref, next_inner_ref, next_outer_ref, back_ref,
):
    depth, length, width = post_ref.shape[1:]
    lines = depth * length
    slots = turned_ref.shape[1]
    halo = (outer_ref, inner_ref, far_ref, near_ref)
    rate = [rates_ref[:, a : a + 1] for a in range(27)]

    def corner(i):
        n = corner_row(i)
        return across(near_rows_ref[n : n + 1], far_rows_ref[n : n + 1], i)

    pushes = []
    for z in range(depth):
        relaxed = relax(streamed(post_ref, *halo, z, corner), rate)
        post, push = exchange(*relaxed, *grains_at(held_ref, z, depth, length))
        for i in range(27):
            next_ref[i, z] = post[i]
        pushes.append(push)
    store_faces(next_ref, next_near_ref, next_far_ref)
    store_ends(next_ref, next_inner_ref, next_outer_ref)
    back_ref[...] = jnp.zeros(back_ref.shape, f32)
    for i in range(27):
        cz, cx, cy = STEP[i]
        if cz and cx:
            z, x = depth - 1 if cz > 0 else 0, length - 1 if cx > 0 else 0
            back_ref[pl.ds(4 * device_at(cz, cx) + 2 + cy, 1)] = next_ref[i, z, x : x + 1]
    total = jnp.concatenate(
        [push_ref[k, z] + pushes[z][k] for k in range(3) for z in range(depth)], axis=0
    )
    along_y = jnp.dot(
        jnp.concatenate(split2(total), axis=0), turned_ref[...], preferred_element_type=f32
    )
    along_y = along_y[: 3 * lines] + along_y[3 * lines :]
    tiles, per_tile = slots // LANES, LANES // capacity
    group = iota((tiles, LANES), 1) // capacity
    force = [[], [], []]
    for t in range(tiles):
        on_line = iota((lines, LANES), 0) == line_ref[t : t + 1]
        for k in range(3):
            part = along_y[k * lines : (k + 1) * lines, t * LANES : (t + 1) * LANES]
            force[k].append(-jnp.sum(jnp.where(on_line, part, 0.0), axis=0, keepdims=True))
    force = [jnp.concatenate(parts, axis=0) for parts in force]
    for a in range(per_tile):
        block = jnp.zeros((tiles, LANES), f32)
        for k in range(3):
            shift = (k - a) * capacity % LANES
            turned = pltpu.roll(force[k], shift, 1) if shift else force[k]
            block = jnp.where(group == k, turned, block)
        back_ref[pl.ds(4 * a, tiles, stride=4 * per_tile), :] = block


def scale_kernel(post_ref, near_ref, far_ref, outer_ref, inner_ref, staged_ref):
    none = jnp.zeros((1, post_ref.shape[3]), f32)
    for z in range(post_ref.shape[1]):
        fields = streamed(post_ref, outer_ref, inner_ref, far_ref, near_ref, z, lambda i: none)
        for i in range(27):
            staged_ref[i, z] = fields[i] * (1.0 / WEIGHT[i])


def last_kernel(capacity, staged_ref, back_ref, hot_ref, at_rank_ref, scaled_ref, force_ref):
    depth, length, width = staged_ref.shape[1:]
    for z in range(depth):
        for i in range(27):
            cz, cx, cy = STEP[i]
            value = staged_ref[i, z]
            if cx and not 0 <= z - cz < depth:
                row = back_ref[pl.ds(4 * device_at(-cz, -cx) + 2 + cy, 1)] * (1.0 / WEIGHT[i])
                row = pltpu.roll(row, cy % width, 1) if cy else row
                wall = 0 if cz > 0 else lax.axis_size("gz") - 1
                place = jnp.where(lax.axis_index("gz") == wall, -1, 0 if cx > 0 else length - 1)
                value = jnp.where(iota(value.shape, 0) == place, row, value)
            scaled_ref[i, z] = value
    back = back_ref[pl.ds(0, hot_ref.shape[0] // 2, stride=4), :]
    picked = lax.dot_general(
        jnp.concatenate(split2(back), axis=0),
        hot_ref[...],
        (((0,), (0,)), ((), ())),
        preferred_element_type=f32,
    )
    for k in range(3):
        mine = at_rank_ref[...] * picked[k * capacity : (k + 1) * capacity]
        force_ref[k : k + 1] = jnp.sum(mine, axis=0, keepdims=True)


def swap_faces(near, far):
    depth, length = lax.axis_size("gz"), lax.axis_size("gx")
    received = []
    for face, odd in ((far, 1), (near, 0)):
        pairs = []
        for z in range(depth):
            other = z + 1 if z % 2 == odd else z - 1
            for x in range(length):
                to = other * length + x if 0 <= other < depth else z * length + (x ^ 1)
                pairs.append((z * length + x, to))
        received.append(lax.ppermute(face, ("gz", "gx"), pairs))
    return received[1], received[0]


def swap_inner(inner):
    return lax.ppermute(inner, "gx", [(i, i ^ 1) for i in range(lax.axis_size("gx"))])


def swap_outer(outer):
    length = lax.axis_size("gx")
    pairs = [(i, (i + 1) % length if i % 2 else (i - 1) % length) for i in range(length)]
    return lax.ppermute(outer, "gx", pairs)


def per_device(populations, rates, grain_fraction, grain_velocity, grain_dest, grain_line):
    _, depth, length, width = populations.shape
    lines = depth * length
    devices = lax.axis_size("gz") * lax.axis_size("gx")
    grains = grain_fraction.shape[0]
    capacity = 2 * grains // devices
    slots = devices * capacity
    shape, both = jax.ShapeDtypeStruct, ("gz", "gx")
    dest, line = grain_dest.reshape(1, grains), grain_line.reshape(1, grains)
    rows = devices * (capacity + 2)
    earlier, spread = call(
        functools.partial(tables_kernel, capacity), [shape((LANES, LANES), bf16)] * 2, flops=10**9
    )
    rank, facts, rates = call(
        functools.partial(rank_kernel, devices),
        [shape((1, grains), i32), shape((4, grains), f32), shape((1, 27), f32)],
        dest, line, grain_velocity, rates.reshape(1, 27), earlier,
    )
    (send,) = call(
        functools.partial(pack_kernel, devices, capacity),
        [shape((rows, width), bf16)],
        dest, rank, facts, grain_fraction,
        scratch=[pltpu.VMEM((rows, width), f32)],
    )
    recv = lax.all_to_all(
        send.reshape(devices, capacity // 2 + 1, 2, width), both, split_axis=0, concat_axis=0, tiled=True
    ).reshape(rows, width)
    state = shape(populations.shape, f32)
    face, ends = shape((9, length, width), f32), shape((9 * depth, width), f32)
    post, outer, inner, far, near, push, held, slot_line, slot_rows = call(
        functools.partial(first_kernel, devices, capacity),
        [
            state, ends, ends, face, face, shape((3, depth, length, width), f32),
            shape((4 * lines, width), f32), shape((slots // LANES, LANES), i32), shape((slots, width), bf16),
        ],
        recv, populations, rates, spread, scratch=[pltpu.VMEM((rows, width), f32)],
    )
    outer, inner = swap_outer(outer), swap_inner(inner)
    near, far = swap_faces(near, far)
    turned, hot, at_rank = call(
        turn_kernel,
        [shape((width, slots), bf16), shape((2 * devices, grains), bf16), shape((capacity, grains), f32)],
        slot_rows, dest, rank,
    )
    corners = shape((6, width), f32)
    far_rows, near_rows = call(
        functools.partial(corners_kernel, depth), [corners, corners], outer, inner, flops=10**10
    )
    near_rows, far_rows = swap_faces(near_rows, far_rows)
    post, next_near, next_far, inner, outer, back = call(
        functools.partial(second_kernel, capacity),
        [state, face, face, ends, ends, shape((4 * devices, LANES), f32)],
        rates, post, outer, inner, far, near, far_rows, near_rows, held, push, slot_line, turned,
    )
    back = lax.all_to_all(
        back.reshape(devices, 4, LANES), both, split_axis=0, concat_axis=0, tiled=True
    ).reshape(4 * devices, LANES)
    outer = swap_outer(outer)
    near, far = swap_faces(next_near, next_far)
    inner = swap_inner(inner)
    (staged,) = call(scale_kernel, [state], post, near, far, outer, inner)
    scaled, grain_force = call(
        functools.partial(last_kernel, capacity),
        [state, shape((3, grains), f32)],
        staged, back, hot, at_rank,
    )
    return (scaled, grain_force)


def solution(mesh):
    in_specs = (
        P(None, "gz", "gx", None),
        P(),
        P(("gz", "gx"), None),
        P(None, ("gz", "gx")),
        P(("gz", "gx"), None),
        P(("gz", "gx")),
    )
    out_specs = (P(None, "gz", "gx", None), P(None, ("gz", "gx")))
    return jax.shard_map(
        per_device, mesh=mesh, in_specs=in_specs, out_specs=out_specs, check_vma=False
    )
```

```python
import functools

import jax
import jax.numpy as jnp
import numpy as np
from jax import lax
from jax.experimental import pallas as pl
from jax.experimental.pallas import tpu as pltpu
from jax.sharding import PartitionSpec as P

STEPS = 2
LANES = 128
f32, bf16, i32 = jnp.float32, jnp.bfloat16, jnp.int32
DIGITS = [(i // 9, i // 3 % 3, i % 3) for i in range(27)]
STEP = [tuple(d - 1 for d in digits) for digits in DIGITS]
WEIGHT = [(8.0 / 27, 2.0 / 27, 1.0 / 54, 1.0 / 216)[sum(abs(s) for s in step)] for step in STEP]


def iota(shape, dim):
    return lax.broadcasted_iota(i32, shape, dim)


def call(kernel, outs, *operands, scratch=(), flops=0):
    size = sum(o.size * o.dtype.itemsize for o in operands) + sum(
        int(np.prod(o.shape)) * o.dtype.itemsize for o in outs
    )
    return pl.pallas_call(
        kernel,
        out_shape=list(outs),
        in_specs=[pl.BlockSpec(memory_space=pltpu.VMEM)] * len(operands),
        out_specs=[pl.BlockSpec(memory_space=pltpu.VMEM)] * len(outs),
        scratch_shapes=list(scratch),
        compiler_params=pltpu.CompilerParams(vmem_limit_bytes=24 * 1024 * 1024),
        cost_estimate=pl.CostEstimate(flops=flops, bytes_accessed=size, transcendentals=0),
    )(*operands)


def device_at(step_z, step_x):
    depth, length = lax.axis_size("gz"), lax.axis_size("gx")
    z = lax.rem(lax.axis_index("gz") + step_z + depth, depth)
    x = lax.rem(lax.axis_index("gx") + step_x + length, length)
    return z * length + x


def split2(x):
    high = x.astype(bf16)
    return high, (x - high.astype(f32)).astype(bf16)


def tables_kernel(earlier_ref):
    row, column = iota(earlier_ref.shape, 0), iota(earlier_ref.shape, 1)
    earlier_ref[...] = jnp.where(row < column, 1.0, 0.0).astype(bf16)


def ranks(hot, earlier):
    devices, grains = hot.shape
    total = jnp.zeros((devices, 1), f32)
    parts = []
    for start in range(0, grains, LANES):
        part = hot[:, start : start + LANES]
        before = jnp.dot(part.astype(bf16), earlier, preferred_element_type=f32) + total
        parts.append(jnp.sum(part * before, axis=0, keepdims=True))
        total = total + jnp.sum(part, axis=1, keepdims=True)
    return jnp.concatenate(parts, axis=1)


def rank_kernel(
    devices, dest_ref, line_ref, speed_ref, rates_ref, earlier_ref, rank_ref, facts_ref, rates_out_ref
):
    hot = jnp.where(iota((devices, dest_ref.shape[1]), 0) == dest_ref[...], 1.0, 0.0)
    rank_ref[...] = ranks(hot, earlier_ref[...]).astype(i32)
    shared = facts_ref.shape[0]
    place = device_at(0, 0) % shared
    speed = speed_ref[...].astype(f32)
    values = [speed[0:1], speed[1:2], speed[2:3], line_ref[...].astype(f32)]
    for group in range(shared):
        row = jnp.zeros(values[3].shape, f32)
        for m, value in enumerate(values):
            row = jnp.where(place == (group - m) % shared, value, row)
        facts_ref[group : group + 1] = row
    rates_out_ref[...] = rates_ref[...]


def pack_kernel(devices, capacity, dest_ref, rank_ref, facts_ref, fraction_ref, send_ref, rows_ref):
    grains, width = fraction_ref.shape
    dest, rank = dest_ref[...], rank_ref[...]
    chosen = jnp.where(iota((rows_ref.shape[0], grains), 0) == dest * (capacity + 2) + rank, 1.0, 0.0)
    rows_ref[...] = jnp.dot(chosen.astype(bf16), fraction_ref[...], preferred_element_type=f32)
    at_rank = iota((capacity, grains), 0) == rank
    facts = [jnp.where(at_rank, facts_ref[m : m + 1], 0.0) for m in range(facts_ref.shape[0])]
    rows_ref[pl.ds(capacity, devices, stride=capacity + 2), :] = lax.dot_general(
        jnp.where(iota((devices, grains), 0) == dest, 1.0, 0.0).astype(bf16),
        jnp.concatenate(facts, axis=0).astype(bf16),
        (((1,), (1,)), ((), ())),
        preferred_element_type=f32,
    )
    send_ref[...] = rows_ref[...].astype(bf16)


def total_of(values):
    return functools.reduce(lambda a, b: a + b, values)


def along(speed, i):
    return total_of([v if s > 0 else -v for s, v in zip(STEP[i], speed) if s])


def relax(fields, rate):
    density = total_of(fields)
    momentum = [
        total_of([fields[i] for i in range(27) if STEP[i][axis] == 1])
        - total_of([fields[i] for i in range(27) if STEP[i][axis] == -1])
        for axis in range(3)
    ]
    inverse = 1.0 / density
    speed = [m * inverse for m in momentum]
    base = 1.0 - 1.5 * total_of([v * v for v in speed])
    departure = [None] * 27
    for i in range(13, 27):
        scale = WEIGHT[i] * density
        if i == 13:
            departure[i] = fields[i] - scale * base
            continue
        dot = along(speed, i)
        even, odd = scale * (base + 4.5 * dot * dot), scale * (3.0 * dot)
        departure[i] = fields[i] - (even + odd)
        departure[26 - i] = fields[26 - i] - (even - odd)
    moments = list(departure)
    for stride in (1, 3, 9):
        for i in range(27):
            if i // stride % 3 == 0:
                low, mid, high = moments[i], moments[i + stride], moments[i + 2 * stride]
                both = low + high
                moments[i], moments[i + stride], moments[i + 2 * stride] = both + mid, high - low, both
    moments = [rate[a] * moments[a] for a in range(27)]
    for stride in (9, 3, 1):
        for i in range(27):
            if i // stride % 3 == 0:
                m0, m1, m2 = moments[i], moments[i + stride], moments[i + 2 * stride]
                half1, half2 = 0.5 * m1, 0.5 * m2
                moments[i], moments[i + stride], moments[i + 2 * stride] = half2 - half1, m0 - m2, half2 + half1
    kept = [fields[i] - moments[i] for i in range(27)]
    swapped = [departure[26 - i] - kept[i] for i in range(27)]
    return density, momentum, kept, swapped


def exchange(density, momentum, kept, swapped, solid, carried):
    inverse = 1.0 / (1.0 + solid)
    share = solid * inverse
    speed = [c * inverse for c in carried]
    base = 1.0 - 1.5 * total_of([v * v for v in speed])
    push = [(density * v - m) * inverse for v, m in zip(speed, momentum)]
    post = [None] * 27
    for i in range(13, 27):
        scale = WEIGHT[i] * density
        if i == 13:
            post[i] = kept[i] + share * (swapped[i] + scale * base)
            continue
        dot = along(speed, i)
        even, odd = scale * (base + 4.5 * dot * dot), scale * (3.0 * dot)
        post[i] = kept[i] + share * (swapped[i] + (even + odd))
        post[26 - i] = kept[26 - i] + share * (swapped[26 - i] + (even - odd))
    return post, push


def grains_at(held_ref, z, depth, length):
    lines = depth * length
    first = [held_ref[k * lines + z * length : k * lines + (z + 1) * length, :] for k in range(4)]
    return first[0], first[1:]


def even_place(axis):
    return lax.axis_index(axis) % 2 == 0


def store_faces(post_ref, near_ref, far_ref):
    top = post_ref.shape[1] - 1
    for n in range(9):
        up, down = post_ref[n + 18, top], post_ref[n, 0]
        near_ref[n] = jnp.where(even_place("gz"), up, down)
        far_ref[n] = jnp.where(even_place("gz"), down, up)


def end_row(i, z, depth):
    return ((STEP[i][0] + 1) * 3 + STEP[i][2] + 1) * depth + z


def store_ends(post_ref, inner_ref, outer_ref):
    depth, length = post_ref.shape[1], post_ref.shape[2]
    for i in range(27):
        if STEP[i][1] == 1:
            for z in range(depth):
                n = end_row(i, z, depth)
                right, left = post_ref[i, z, length - 1 : length], post_ref[i - 6, z, 0:1]
                inner_ref[n : n + 1] = jnp.where(even_place("gx"), right, left)
                outer_ref[n : n + 1] = jnp.where(even_place("gx"), left, right)


def end_from(i, outer, inner):
    if STEP[i][1] > 0:
        return jnp.where(even_place("gx"), outer, inner)
    return jnp.where(even_place("gx"), inner, outer)


def moved_along_x(field, i, end):
    cx, length = STEP[i][1], field.shape[0]
    place = 0 if cx > 0 else length - 1
    return jnp.where(iota(field.shape, 0) == place, end, pltpu.roll(field, cx % length, 0))


def across(near, far, i):
    if STEP[i][0] > 0:
        return jnp.where(even_place("gz"), far, near)
    return jnp.where(even_place("gz"), near, far)


def first_kernel(
    devices, capacity, recv_ref, fields_ref, rates_ref,
    post_ref, outer_ref, inner_ref, far_ref, near_ref, push_ref, held_ref, line_ref, slot_ref, wide_ref,
):
    width = recv_ref.shape[1]
    block, slots = capacity + 2, devices * capacity
    depth, length = fields_ref.shape[1], fields_ref.shape[2]
    lines = depth * length
    rate = [rates_ref[:, a : a + 1] for a in range(27)]
    wide_ref[...] = recv_ref[...].astype(f32)
    slot_rows = jnp.concatenate(
        [wide_ref[j * block : j * block + capacity] for j in range(devices)], axis=0
    ).astype(bf16)
    slot_ref[...] = slot_rows
    tiles, shared = slots // LANES, LANES // capacity
    group = iota((tiles, width), 1) // capacity
    rows = [wide_ref[pl.ds(capacity + a * block, tiles, stride=shared * block), :] for a in range(shared)]
    fact = []
    for m in range(4):
        mixed = total_of([jnp.where(group == (a + m) % shared, rows[a], 0.0) for a in range(shared)])
        fact.append(pltpu.roll(mixed, LANES - m * capacity, 1) if m else mixed)
    line_ref[...] = fact[3].astype(i32)
    gather = []
    for t in range(tiles):
        on_line = iota((lines, LANES), 0) == fact[3][t : t + 1].astype(i32)
        gather.append(
            jnp.concatenate(
                [jnp.where(on_line, 1.0, 0.0)]
                + [jnp.where(on_line, fact[k][t : t + 1], 0.0) for k in range(3)],
                axis=0,
            ).astype(bf16)
        )
    held_ref[...] = jnp.dot(jnp.concatenate(gather, axis=1), slot_rows, preferred_element_type=f32)
    for z in range(depth):
        relaxed = relax([fields_ref[i, z] for i in range(27)], rate)
        post, push = exchange(*relaxed, *grains_at(held_ref, z, depth, length))
        for i in range(27):
            post_ref[i, z] = post[i]
        for k in range(3):
            push_ref[k, z] = push[k]
    store_ends(post_ref, inner_ref, outer_ref)
    store_faces(post_ref, near_ref, far_ref)


def turn_kernel(slot_ref, dest_ref, rank_ref, turned_ref, hot_ref, at_rank_ref):
    turned_ref[...] = slot_ref[...].astype(f32).T.astype(bf16)
    devices = hot_ref.shape[0] // 2
    hot_ref[...] = jnp.where(iota(hot_ref.shape, 0) % devices == dest_ref[...], 1.0, 0.0).astype(bf16)
    at_rank_ref[...] = jnp.where(iota(at_rank_ref.shape, 0) == rank_ref[...], 1.0, 0.0)


def corners_kernel(depth, outer_ref, inner_ref, far_ref, near_ref):
    for i in range(9):
        if STEP[i][1]:
            up, down = [
                end_from(i, outer_ref[n : n + 1], inner_ref[n : n + 1])
                for n in (end_row(18 + i, depth - 1, depth), end_row(i, 0, depth))
            ]
            n = corner_row(i)
            near_ref[n : n + 1] = jnp.where(even_place("gz"), up, down)
            far_ref[n : n + 1] = jnp.where(even_place("gz"), down, up)


def corner_row(i):
    return (3 if STEP[i][1] > 0 else 0) + STEP[i][2] + 1


def streamed(post_ref, outer_ref, inner_ref, far_ref, near_ref, z, corner):
    depth, width = post_ref.shape[1], post_ref.shape[3]
    moved_list = []
    for i in range(27):
        cz, cx, cy = STEP[i]
        source = z - cz
        inside = 0 <= source < depth
        moved = post_ref[i, source] if inside else across(near_ref[i % 9], far_ref[i % 9], i)
        if cx and inside:
            n = end_row(i, source, depth)
            moved = moved_along_x(moved, i, end_from(i, outer_ref[n : n + 1], inner_ref[n : n + 1]))
        elif cx:
            moved = moved_along_x(moved, i, corner(i))
        if cy:
            moved = pltpu.roll(moved, cy % width, 1)
        if not inside:
            wall = 0 if cz > 0 else lax.axis_size("gz") - 1
            moved = jnp.where(lax.axis_index("gz") == wall, post_ref[26 - i, z], moved)
        moved_list.append(moved)
    return moved_list


def second_kernel(
    capacity, rates_ref, post_ref, outer_ref, inner_ref, far_ref, near_ref, far_rows_ref, near_rows_ref,
    held_ref, push_ref, line_ref, turned_ref,
    next_ref, next_near_ref, next_far_ref, next_inner_ref, next_outer_ref, back_ref,
):
    depth, length, width = post_ref.shape[1:]
    lines = depth * length
    slots = turned_ref.shape[1]
    halo = (outer_ref, inner_ref, far_ref, near_ref)
    rate = [rates_ref[:, a : a + 1] for a in range(27)]

    def corner(i):
        n = corner_row(i)
        return across(near_rows_ref[n : n + 1], far_rows_ref[n : n + 1], i)

    pushes = []
    for z in range(depth):
        relaxed = relax(streamed(post_ref, *halo, z, corner), rate)
        post, push = exchange(*relaxed, *grains_at(held_ref, z, depth, length))
        for i in range(27):
            next_ref[i, z] = post[i]
        pushes.append(push)
    store_faces(next_ref, next_near_ref, next_far_ref)
    store_ends(next_ref, next_inner_ref, next_outer_ref)
    back_ref[...] = jnp.zeros(back_ref.shape, f32)
    for i in range(27):
        cz, cx, cy = STEP[i]
        if cz and cx:
            z, x = depth - 1 if cz > 0 else 0, length - 1 if cx > 0 else 0
            back_ref[pl.ds(4 * device_at(cz, cx) + 2 + cy, 1)] = next_ref[i, z, x : x + 1]
    total = jnp.concatenate(
        [push_ref[k, z] + pushes[z][k] for k in range(3) for z in range(depth)], axis=0
    )
    along_y = jnp.dot(
        jnp.concatenate(split2(total), axis=0), turned_ref[...], preferred_element_type=f32
    )
    along_y = along_y[: 3 * lines] + along_y[3 * lines :]
    tiles, per_tile = slots // LANES, LANES // capacity
    group = iota((tiles, LANES), 1) // capacity
    force = [[], [], []]
    for t in range(tiles):
        on_line = iota((lines, LANES), 0) == line_ref[t : t + 1]
        for k in range(3):
            part = along_y[k * lines : (k + 1) * lines, t * LANES : (t + 1) * LANES]
            force[k].append(-jnp.sum(jnp.where(on_line, part, 0.0), axis=0, keepdims=True))
    force = [jnp.concatenate(parts, axis=0) for parts in force]
    for a in range(per_tile):
        block = jnp.zeros((tiles, LANES), f32)
        for k in range(3):
            shift = (k - a) * capacity % LANES
            turned = pltpu.roll(force[k], shift, 1) if shift else force[k]
            block = jnp.where(group == k, turned, block)
        back_ref[pl.ds(4 * a, tiles, stride=4 * per_tile), :] = block


def scale_kernel(post_ref, near_ref, far_ref, outer_ref, inner_ref, staged_ref):
    none = jnp.zeros((1, post_ref.shape[3]), f32)
    for z in range(post_ref.shape[1]):
        fields = streamed(post_ref, outer_ref, inner_ref, far_ref, near_ref, z, lambda i: none)
        for i in range(27):
            staged_ref[i, z] = fields[i] * (1.0 / WEIGHT[i])


def last_kernel(capacity, staged_ref, back_ref, hot_ref, at_rank_ref, scaled_ref, force_ref):
    depth, length, width = staged_ref.shape[1:]
    for z in range(depth):
        for i in range(27):
            cz, cx, cy = STEP[i]
            value = staged_ref[i, z]
            if cx and not 0 <= z - cz < depth:
                row = back_ref[pl.ds(4 * device_at(-cz, -cx) + 2 + cy, 1)] * (1.0 / WEIGHT[i])
                row = pltpu.roll(row, cy % width, 1) if cy else row
                wall = 0 if cz > 0 else lax.axis_size("gz") - 1
                place = jnp.where(lax.axis_index("gz") == wall, -1, 0 if cx > 0 else length - 1)
                value = jnp.where(iota(value.shape, 0) == place, row, value)
            scaled_ref[i, z] = value
    back = back_ref[pl.ds(0, hot_ref.shape[0] // 2, stride=4), :]
    picked = lax.dot_general(
        jnp.concatenate(split2(back), axis=0),
        hot_ref[...],
        (((0,), (0,)), ((), ())),
        preferred_element_type=f32,
    )
    for k in range(3):
        mine = at_rank_ref[...] * picked[k * capacity : (k + 1) * capacity]
        force_ref[k : k + 1] = jnp.sum(mine, axis=0, keepdims=True)


def swap_faces(near, far):
    depth, length = lax.axis_size("gz"), lax.axis_size("gx")
    received = []
    for face, odd in ((far, 1), (near, 0)):
        pairs = []
        for z in range(depth):
            other = z + 1 if z % 2 == odd else z - 1
            for x in range(length):
                to = other * length + x if 0 <= other < depth else z * length + (x ^ 1)
                pairs.append((z * length + x, to))
        received.append(lax.ppermute(face, ("gz", "gx"), pairs))
    return received[1], received[0]


def swap_inner(inner):
    return lax.ppermute(inner, "gx", [(i, i ^ 1) for i in range(lax.axis_size("gx"))])


def swap_outer(outer):
    length = lax.axis_size("gx")
    pairs = [(i, (i + 1) % length if i % 2 else (i - 1) % length) for i in range(length)]
    return lax.ppermute(outer, "gx", pairs)


def per_device(populations, rates, grain_fraction, grain_velocity, grain_dest, grain_line):
    _, depth, length, width = populations.shape
    lines = depth * length
    devices = lax.axis_size("gz") * lax.axis_size("gx")
    grains = grain_fraction.shape[0]
    capacity = 2 * grains // devices
    slots = devices * capacity
    shape, both = jax.ShapeDtypeStruct, ("gz", "gx")
    dest, line = grain_dest.reshape(1, grains), grain_line.reshape(1, grains)
    rows = devices * (capacity + 2)
    (earlier,) = call(tables_kernel, [shape((LANES, LANES), bf16)], flops=10**9)
    rank, facts, rates = call(
        functools.partial(rank_kernel, devices),
        [shape((1, grains), i32), shape((LANES // capacity, grains), f32), shape((1, 27), f32)],
        dest, line, grain_velocity, rates.reshape(1, 27), earlier,
    )
    (send,) = call(
        functools.partial(pack_kernel, devices, capacity),
        [shape((rows, width), bf16)],
        dest, rank, facts, grain_fraction,
        scratch=[pltpu.VMEM((rows, width), f32)],
    )
    recv = lax.all_to_all(
        send.reshape(devices, capacity // 2 + 1, 2, width), both, split_axis=0, concat_axis=0, tiled=True
    ).reshape(rows, width)
    state = shape(populations.shape, f32)
    face, ends = shape((9, length, width), f32), shape((9 * depth, width), f32)
    post, outer, inner, far, near, push, held, slot_line, slot_rows = call(
        functools.partial(first_kernel, devices, capacity),
        [
            state, ends, ends, face, face, shape((3, depth, length, width), f32),
            shape((4 * lines, width), f32), shape((slots // LANES, LANES), i32), shape((slots, width), bf16),
        ],
        recv, populations, rates, scratch=[pltpu.VMEM((rows, width), f32)],
    )
    outer, inner = swap_outer(outer), swap_inner(inner)
    near, far = swap_faces(near, far)
    turned, hot, at_rank = call(
        turn_kernel,
        [shape((width, slots), bf16), shape((2 * devices, grains), bf16), shape((capacity, grains), f32)],
        slot_rows, dest, rank,
    )
    corners = shape((6, width), f32)
    far_rows, near_rows = call(
        functools.partial(corners_kernel, depth), [corners, corners], outer, inner, flops=10**10
    )
    near_rows, far_rows = swap_faces(near_rows, far_rows)
    post, next_near, next_far, inner, outer, back = call(
        functools.partial(second_kernel, capacity),
        [state, face, face, ends, ends, shape((4 * devices, LANES), f32)],
        rates, post, outer, inner, far, near, far_rows, near_rows, held, push, slot_line, turned,
    )
    back = lax.all_to_all(
        back.reshape(devices, 4, LANES), both, split_axis=0, concat_axis=0, tiled=True
    ).reshape(4 * devices, LANES)
    outer = swap_outer(outer)
    near, far = swap_faces(next_near, next_far)
    inner = swap_inner(inner)
    (staged,) = call(scale_kernel, [state], post, near, far, outer, inner)
    scaled, grain_force = call(
        functools.partial(last_kernel, capacity),
        [state, shape((3, grains), f32)],
        staged, back, hot, at_rank,
    )
    return (scaled, grain_force)


def solution(mesh):
    in_specs = (
        P(None, "gz", "gx", None),
        P(),
        P(("gz", "gx"), None),
        P(None, ("gz", "gx")),
        P(("gz", "gx"), None),
        P(("gz", "gx")),
    )
    out_specs = (P(None, "gz", "gx", None), P(None, ("gz", "gx")))
    return jax.shard_map(
        per_device, mesh=mesh, in_specs=in_specs, out_specs=out_specs, check_vma=False
    )
```

```python
import functools

import jax
import jax.numpy as jnp
import numpy as np
from jax import lax
from jax.experimental import pallas as pl
from jax.experimental.pallas import tpu as pltpu
from jax.sharding import PartitionSpec as P

STEPS = 2
LANES = 128
f32, bf16, i32 = jnp.float32, jnp.bfloat16, jnp.int32
DIGITS = [(i // 9, i // 3 % 3, i % 3) for i in range(27)]
STEP = [tuple(d - 1 for d in digits) for digits in DIGITS]
WEIGHT = [(8.0 / 27, 2.0 / 27, 1.0 / 54, 1.0 / 216)[sum(abs(s) for s in step)] for step in STEP]


def iota(shape, dim):
    return lax.broadcasted_iota(i32, shape, dim)


def call(kernel, outs, *operands, scratch=(), flops=0):
    size = sum(o.size * o.dtype.itemsize for o in operands) + sum(
        int(np.prod(o.shape)) * o.dtype.itemsize for o in outs
    )
    return pl.pallas_call(
        kernel,
        out_shape=list(outs),
        in_specs=[pl.BlockSpec(memory_space=pltpu.VMEM)] * len(operands),
        out_specs=[pl.BlockSpec(memory_space=pltpu.VMEM)] * len(outs),
        scratch_shapes=list(scratch),
        compiler_params=pltpu.CompilerParams(vmem_limit_bytes=24 * 1024 * 1024),
        cost_estimate=pl.CostEstimate(flops=flops, bytes_accessed=size, transcendentals=0),
    )(*operands)


def device_at(step_z, step_x):
    depth, length = lax.axis_size("gz"), lax.axis_size("gx")
    z = lax.rem(lax.axis_index("gz") + step_z + depth, depth)
    x = lax.rem(lax.axis_index("gx") + step_x + length, length)
    return z * length + x


def split2(x):
    high = x.astype(bf16)
    return high, (x - high.astype(f32)).astype(bf16)


def tables_kernel(earlier_ref):
    row, column = iota(earlier_ref.shape, 0), iota(earlier_ref.shape, 1)
    earlier_ref[...] = jnp.where(row < column, 1.0, 0.0).astype(bf16)


def ranks(hot, earlier):
    devices, grains = hot.shape
    total = jnp.zeros((devices, 1), f32)
    parts = []
    for start in range(0, grains, LANES):
        part = hot[:, start : start + LANES]
        before = jnp.dot(part.astype(bf16), earlier, preferred_element_type=f32) + total
        parts.append(jnp.sum(part * before, axis=0, keepdims=True))
        total = total + jnp.sum(part, axis=1, keepdims=True)
    return jnp.concatenate(parts, axis=1)


def rank_kernel(
    devices, dest_ref, line_ref, speed_ref, rates_ref, earlier_ref, rank_ref, facts_ref, rates_out_ref
):
    hot = jnp.where(iota((devices, dest_ref.shape[1]), 0) == dest_ref[...], 1.0, 0.0)
    rank_ref[...] = ranks(hot, earlier_ref[...]).astype(i32)
    shared = facts_ref.shape[0]
    place = device_at(0, 0) % shared
    speed = speed_ref[...].astype(f32)
    values = [speed[0:1], speed[1:2], speed[2:3], line_ref[...].astype(f32)]
    for group in range(shared):
        row = jnp.zeros(values[3].shape, f32)
        for m, value in enumerate(values):
            row = jnp.where(place == (group - m) % shared, value, row)
        facts_ref[group : group + 1] = row
    rates_out_ref[...] = rates_ref[...]


def pack_kernel(devices, capacity, dest_ref, rank_ref, facts_ref, fraction_ref, send_ref, rows_ref):
    grains, width = fraction_ref.shape
    dest, rank = dest_ref[...], rank_ref[...]
    chosen = jnp.where(iota((rows_ref.shape[0], grains), 0) == dest * (capacity + 2) + rank, 1.0, 0.0)
    rows_ref[...] = jnp.dot(chosen.astype(bf16), fraction_ref[...], preferred_element_type=f32)
    at_rank = iota((capacity, grains), 0) == rank
    facts = [jnp.where(at_rank, facts_ref[m : m + 1], 0.0) for m in range(facts_ref.shape[0])]
    rows_ref[pl.ds(capacity, devices, stride=capacity + 2), :] = lax.dot_general(
        jnp.where(iota((devices, grains), 0) == dest, 1.0, 0.0).astype(bf16),
        jnp.concatenate(facts, axis=0).astype(bf16),
        (((1,), (1,)), ((), ())),
        preferred_element_type=f32,
    )
    send_ref[...] = rows_ref[...].astype(bf16)


def total_of(values):
    return functools.reduce(lambda a, b: a + b, values)


def along(speed, i):
    return total_of([v if s > 0 else -v for s, v in zip(STEP[i], speed) if s])


def relax(fields, rate):
    density = total_of(fields)
    momentum = [
        total_of([fields[i] for i in range(27) if STEP[i][axis] == 1])
        - total_of([fields[i] for i in range(27) if STEP[i][axis] == -1])
        for axis in range(3)
    ]
    inverse = 1.0 / density
    speed = [m * inverse for m in momentum]
    base = 1.0 - 1.5 * total_of([v * v for v in speed])
    departure = [None] * 27
    for i in range(13, 27):
        scale = WEIGHT[i] * density
        if i == 13:
            departure[i] = fields[i] - scale * base
            continue
        dot = along(speed, i)
        even, odd = scale * (base + 4.5 * dot * dot), scale * (3.0 * dot)
        departure[i] = fields[i] - (even + odd)
        departure[26 - i] = fields[26 - i] - (even - odd)
    moments = list(departure)
    for stride in (1, 3, 9):
        for i in range(27):
            if i // stride % 3 == 0:
                low, mid, high = moments[i], moments[i + stride], moments[i + 2 * stride]
                both = low + high
                moments[i], moments[i + stride], moments[i + 2 * stride] = both + mid, high - low, both
    moments = [rate[a] * moments[a] for a in range(27)]
    for stride in (9, 3, 1):
        for i in range(27):
            if i // stride % 3 == 0:
                m0, m1, m2 = moments[i], moments[i + stride], moments[i + 2 * stride]
                half1, half2 = 0.5 * m1, 0.5 * m2
                moments[i], moments[i + stride], moments[i + 2 * stride] = half2 - half1, m0 - m2, half2 + half1
    kept = [fields[i] - moments[i] for i in range(27)]
    swapped = [departure[26 - i] - kept[i] for i in range(27)]
    return density, momentum, kept, swapped


def pull(solid, carried):
    inverse = 1.0 / (1.0 + solid)
    share = solid * inverse
    speed = [c * inverse for c in carried]
    base = 1.0 - 1.5 * total_of([v * v for v in speed])
    pulled = [None] * 27
    for i in range(13, 27):
        scale = WEIGHT[i] * share
        if i == 13:
            pulled[i] = scale * base
            continue
        dot = along(speed, i)
        even, odd = scale * (base + 4.5 * dot * dot), scale * (3.0 * dot)
        pulled[i], pulled[26 - i] = even + odd, even - odd
    return share, inverse, [v * inverse for v in speed], pulled


def exchange(density, momentum, kept, swapped, share, inverse, drag, pulled):
    push = [density * d - m * inverse for d, m in zip(drag, momentum)]
    post = [kept[i] + (share * swapped[i] + density * pulled[i]) for i in range(27)]
    return post, push


def grains_at(held_ref, z, depth, length):
    lines = depth * length
    first = [held_ref[k * lines + z * length : k * lines + (z + 1) * length, :] for k in range(4)]
    return first[0], first[1:]


def even_place(axis):
    return lax.axis_index(axis) % 2 == 0


def store_faces(post_ref, near_ref, far_ref):
    top = post_ref.shape[1] - 1
    for n in range(9):
        up, down = post_ref[n + 18, top], post_ref[n, 0]
        near_ref[n] = jnp.where(even_place("gz"), up, down)
        far_ref[n] = jnp.where(even_place("gz"), down, up)


def end_row(i, z, depth):
    return ((STEP[i][0] + 1) * 3 + STEP[i][2] + 1) * depth + z


def store_ends(post_ref, inner_ref, outer_ref):
    depth, length = post_ref.shape[1], post_ref.shape[2]
    for i in range(27):
        if STEP[i][1] == 1:
            for z in range(depth):
                n = end_row(i, z, depth)
                right, left = post_ref[i, z, length - 1 : length], post_ref[i - 6, z, 0:1]
                inner_ref[n : n + 1] = jnp.where(even_place("gx"), right, left)
                outer_ref[n : n + 1] = jnp.where(even_place("gx"), left, right)


def end_from(i, outer, inner):
    if STEP[i][1] > 0:
        return jnp.where(even_place("gx"), outer, inner)
    return jnp.where(even_place("gx"), inner, outer)


def moved_along_x(field, i, end):
    cx, length = STEP[i][1], field.shape[0]
    place = 0 if cx > 0 else length - 1
    return jnp.where(iota(field.shape, 0) == place, end, pltpu.roll(field, cx % length, 0))


def across(near, far, i):
    if STEP[i][0] > 0:
        return jnp.where(even_place("gz"), far, near)
    return jnp.where(even_place("gz"), near, far)


def first_kernel(
    devices, capacity, recv_ref, fields_ref, rates_ref,
    post_ref, outer_ref, inner_ref, far_ref, near_ref, push_ref, held_ref, line_ref, slot_ref, wide_ref,
):
    width = recv_ref.shape[1]
    block, slots = capacity + 2, devices * capacity
    depth, length = fields_ref.shape[1], fields_ref.shape[2]
    lines = depth * length
    rate = [rates_ref[:, a : a + 1] for a in range(27)]
    wide_ref[...] = recv_ref[...].astype(f32)
    slot_rows = jnp.concatenate(
        [wide_ref[j * block : j * block + capacity] for j in range(devices)], axis=0
    ).astype(bf16)
    slot_ref[...] = slot_rows
    tiles, shared = slots // LANES, LANES // capacity
    group = iota((tiles, width), 1) // capacity
    rows = [wide_ref[pl.ds(capacity + a * block, tiles, stride=shared * block), :] for a in range(shared)]
    fact = []
    for m in range(4):
        mixed = total_of([jnp.where(group == (a + m) % shared, rows[a], 0.0) for a in range(shared)])
        fact.append(pltpu.roll(mixed, LANES - m * capacity, 1) if m else mixed)
    line_ref[...] = fact[3].astype(i32)
    gather = []
    for t in range(tiles):
        on_line = iota((lines, LANES), 0) == fact[3][t : t + 1].astype(i32)
        gather.append(
            jnp.concatenate(
                [jnp.where(on_line, 1.0, 0.0)]
                + [jnp.where(on_line, fact[k][t : t + 1], 0.0) for k in range(3)],
                axis=0,
            ).astype(bf16)
        )
    held_ref[...] = jnp.dot(jnp.concatenate(gather, axis=1), slot_rows, preferred_element_type=f32)
    for z in range(depth):
        relaxed = relax([fields_ref[i, z] for i in range(27)], rate)
        post, push = exchange(*relaxed, *pull(*grains_at(held_ref, z, depth, length)))
        for i in range(27):
            post_ref[i, z] = post[i]
        for k in range(3):
            push_ref[k, z] = push[k]
    store_ends(post_ref, inner_ref, outer_ref)
    store_faces(post_ref, near_ref, far_ref)


def turn_kernel(slot_ref, dest_ref, rank_ref, held_ref, turned_ref, hot_ref, at_rank_ref, pulled_ref):
    _, depth, length, _ = pulled_ref.shape
    for z in range(depth):
        share, inverse, drag, pulled = pull(*grains_at(held_ref, z, depth, length))
        for n, value in enumerate(pulled + [share, inverse] + drag):
            pulled_ref[n, z] = value
    turned_ref[...] = slot_ref[...].astype(f32).T.astype(bf16)
    devices = hot_ref.shape[0] // 2
    hot_ref[...] = jnp.where(iota(hot_ref.shape, 0) % devices == dest_ref[...], 1.0, 0.0).astype(bf16)
    at_rank_ref[...] = jnp.where(iota(at_rank_ref.shape, 0) == rank_ref[...], 1.0, 0.0)


def corners_kernel(depth, outer_ref, inner_ref, far_ref, near_ref):
    for i in range(9):
        if STEP[i][1]:
            up, down = [
                end_from(i, outer_ref[n : n + 1], inner_ref[n : n + 1])
                for n in (end_row(18 + i, depth - 1, depth), end_row(i, 0, depth))
            ]
            n = corner_row(i)
            near_ref[n : n + 1] = jnp.where(even_place("gz"), up, down)
            far_ref[n : n + 1] = jnp.where(even_place("gz"), down, up)


def corner_row(i):
    return (3 if STEP[i][1] > 0 else 0) + STEP[i][2] + 1


def streamed(post_ref, outer_ref, inner_ref, far_ref, near_ref, z, corner):
    depth, width = post_ref.shape[1], post_ref.shape[3]
    moved_list = []
    for i in range(27):
        cz, cx, cy = STEP[i]
        source = z - cz
        inside = 0 <= source < depth
        moved = post_ref[i, source] if inside else across(near_ref[i % 9], far_ref[i % 9], i)
        if cx and inside:
            n = end_row(i, source, depth)
            moved = moved_along_x(moved, i, end_from(i, outer_ref[n : n + 1], inner_ref[n : n + 1]))
        elif cx:
            moved = moved_along_x(moved, i, corner(i))
        if cy:
            moved = pltpu.roll(moved, cy % width, 1)
        if not inside:
            wall = 0 if cz > 0 else lax.axis_size("gz") - 1
            moved = jnp.where(lax.axis_index("gz") == wall, post_ref[26 - i, z], moved)
        moved_list.append(moved)
    return moved_list


def second_kernel(
    capacity, rates_ref, post_ref, outer_ref, inner_ref, far_ref, near_ref, far_rows_ref, near_rows_ref,
    pulled_ref, push_ref, line_ref, turned_ref,
    next_ref, next_near_ref, next_far_ref, next_inner_ref, next_outer_ref, back_ref,
):
    depth, length, width = post_ref.shape[1:]
    lines = depth * length
    slots = turned_ref.shape[1]
    halo = (outer_ref, inner_ref, far_ref, near_ref)
    rate = [rates_ref[:, a : a + 1] for a in range(27)]

    def corner(i):
        n = corner_row(i)
        return across(near_rows_ref[n : n + 1], far_rows_ref[n : n + 1], i)

    pushes = []
    for z in range(depth):
        relaxed = relax(streamed(post_ref, *halo, z, corner), rate)
        post, push = exchange(
            *relaxed,
            pulled_ref[27, z],
            pulled_ref[28, z],
            [pulled_ref[29 + k, z] for k in range(3)],
            [pulled_ref[i, z] for i in range(27)],
        )
        for i in range(27):
            next_ref[i, z] = post[i]
        pushes.append(push)
    store_faces(next_ref, next_near_ref, next_far_ref)
    store_ends(next_ref, next_inner_ref, next_outer_ref)
    back_ref[...] = jnp.zeros(back_ref.shape, f32)
    for i in range(27):
        cz, cx, cy = STEP[i]
        if cz and cx:
            z, x = depth - 1 if cz > 0 else 0, length - 1 if cx > 0 else 0
            back_ref[pl.ds(4 * device_at(cz, cx) + 2 + cy, 1)] = next_ref[i, z, x : x + 1]
    total = jnp.concatenate(
        [push_ref[k, z] + pushes[z][k] for k in range(3) for z in range(depth)], axis=0
    )
    along_y = jnp.dot(
        jnp.concatenate(split2(total), axis=0), turned_ref[...], preferred_element_type=f32
    )
    along_y = along_y[: 3 * lines] + along_y[3 * lines :]
    tiles, per_tile = slots // LANES, LANES // capacity
    group = iota((tiles, LANES), 1) // capacity
    force = [[], [], []]
    for t in range(tiles):
        on_line = iota((lines, LANES), 0) == line_ref[t : t + 1]
        for k in range(3):
            part = along_y[k * lines : (k + 1) * lines, t * LANES : (t + 1) * LANES]
            force[k].append(-jnp.sum(jnp.where(on_line, part, 0.0), axis=0, keepdims=True))
    force = [jnp.concatenate(parts, axis=0) for parts in force]
    for a in range(per_tile):
        block = jnp.zeros((tiles, LANES), f32)
        for k in range(3):
            shift = (k - a) * capacity % LANES
            turned = pltpu.roll(force[k], shift, 1) if shift else force[k]
            block = jnp.where(group == k, turned, block)
        back_ref[pl.ds(4 * a, tiles, stride=4 * per_tile), :] = block


def scale_kernel(post_ref, near_ref, far_ref, outer_ref, inner_ref, staged_ref):
    none = jnp.zeros((1, post_ref.shape[3]), f32)
    for z in range(post_ref.shape[1]):
        fields = streamed(post_ref, outer_ref, inner_ref, far_ref, near_ref, z, lambda i: none)
        for i in range(27):
            staged_ref[i, z] = fields[i] * (1.0 / WEIGHT[i])


def last_kernel(capacity, staged_ref, back_ref, hot_ref, at_rank_ref, scaled_ref, force_ref):
    depth, length, width = staged_ref.shape[1:]
    for z in range(depth):
        for i in range(27):
            cz, cx, cy = STEP[i]
            value = staged_ref[i, z]
            if cx and not 0 <= z - cz < depth:
                row = back_ref[pl.ds(4 * device_at(-cz, -cx) + 2 + cy, 1)] * (1.0 / WEIGHT[i])
                row = pltpu.roll(row, cy % width, 1) if cy else row
                wall = 0 if cz > 0 else lax.axis_size("gz") - 1
                place = jnp.where(lax.axis_index("gz") == wall, -1, 0 if cx > 0 else length - 1)
                value = jnp.where(iota(value.shape, 0) == place, row, value)
            scaled_ref[i, z] = value
    back = back_ref[pl.ds(0, hot_ref.shape[0] // 2, stride=4), :]
    picked = lax.dot_general(
        jnp.concatenate(split2(back), axis=0),
        hot_ref[...],
        (((0,), (0,)), ((), ())),
        preferred_element_type=f32,
    )
    for k in range(3):
        mine = at_rank_ref[...] * picked[k * capacity : (k + 1) * capacity]
        force_ref[k : k + 1] = jnp.sum(mine, axis=0, keepdims=True)


def swap_faces(near, far):
    depth, length = lax.axis_size("gz"), lax.axis_size("gx")
    received = []
    for face, odd in ((far, 1), (near, 0)):
        pairs = []
        for z in range(depth):
            other = z + 1 if z % 2 == odd else z - 1
            for x in range(length):
                to = other * length + x if 0 <= other < depth else z * length + (x ^ 1)
                pairs.append((z * length + x, to))
        received.append(lax.ppermute(face, ("gz", "gx"), pairs))
    return received[1], received[0]


def swap_inner(inner):
    return lax.ppermute(inner, "gx", [(i, i ^ 1) for i in range(lax.axis_size("gx"))])


def swap_outer(outer):
    length = lax.axis_size("gx")
    pairs = [(i, (i + 1) % length if i % 2 else (i - 1) % length) for i in range(length)]
    return lax.ppermute(outer, "gx", pairs)


def per_device(populations, rates, grain_fraction, grain_velocity, grain_dest, grain_line):
    _, depth, length, width = populations.shape
    lines = depth * length
    devices = lax.axis_size("gz") * lax.axis_size("gx")
    grains = grain_fraction.shape[0]
    capacity = 2 * grains // devices
    slots = devices * capacity
    shape, both = jax.ShapeDtypeStruct, ("gz", "gx")
    dest, line = grain_dest.reshape(1, grains), grain_line.reshape(1, grains)
    rows = devices * (capacity + 2)
    (earlier,) = call(tables_kernel, [shape((LANES, LANES), bf16)], flops=10**9)
    rank, facts, rates = call(
        functools.partial(rank_kernel, devices),
        [shape((1, grains), i32), shape((LANES // capacity, grains), f32), shape((1, 27), f32)],
        dest, line, grain_velocity, rates.reshape(1, 27), earlier,
    )
    (send,) = call(
        functools.partial(pack_kernel, devices, capacity),
        [shape((rows, width), bf16)],
        dest, rank, facts, grain_fraction,
        scratch=[pltpu.VMEM((rows, width), f32)],
    )
    recv = lax.all_to_all(
        send.reshape(devices, capacity // 2 + 1, 2, width), both, split_axis=0, concat_axis=0, tiled=True
    ).reshape(rows, width)
    state = shape(populations.shape, f32)
    face, ends = shape((9, length, width), f32), shape((9 * depth, width), f32)
    post, outer, inner, far, near, push, held, slot_line, slot_rows = call(
        functools.partial(first_kernel, devices, capacity),
        [
            state, ends, ends, face, face, shape((3, depth, length, width), f32),
            shape((4 * lines, width), f32), shape((slots // LANES, LANES), i32), shape((slots, width), bf16),
        ],
        recv, populations, rates, scratch=[pltpu.VMEM((rows, width), f32)],
    )
    outer, inner = swap_outer(outer), swap_inner(inner)
    near, far = swap_faces(near, far)
    turned, hot, at_rank, pulled = call(
        turn_kernel,
        [shape((width, slots), bf16), shape((2 * devices, grains), bf16), shape((capacity, grains), f32), shape((32, depth, length, width), f32)],
        slot_rows, dest, rank, held,
    )
    corners = shape((6, width), f32)
    far_rows, near_rows = call(
        functools.partial(corners_kernel, depth), [corners, corners], outer, inner, flops=10**10
    )
    near_rows, far_rows = swap_faces(near_rows, far_rows)
    post, next_near, next_far, inner, outer, back = call(
        functools.partial(second_kernel, capacity),
        [state, face, face, ends, ends, shape((4 * devices, LANES), f32)],
        rates, post, outer, inner, far, near, far_rows, near_rows, pulled, push, slot_line, turned,
    )
    back = lax.all_to_all(
        back.reshape(devices, 4, LANES), both, split_axis=0, concat_axis=0, tiled=True
    ).reshape(4 * devices, LANES)
    outer = swap_outer(outer)
    near, far = swap_faces(next_near, next_far)
    inner = swap_inner(inner)
    (staged,) = call(scale_kernel, [state], post, near, far, outer, inner)
    scaled, grain_force = call(
        functools.partial(last_kernel, capacity),
        [state, shape((3, grains), f32)],
        staged, back, hot, at_rank,
    )
    return (scaled, grain_force)


def solution(mesh):
    in_specs = (
        P(None, "gz", "gx", None),
        P(),
        P(("gz", "gx"), None),
        P(None, ("gz", "gx")),
        P(("gz", "gx"), None),
        P(("gz", "gx")),
    )
    out_specs = (P(None, "gz", "gx", None), P(None, ("gz", "gx")))
    return jax.shard_map(
        per_device, mesh=mesh, in_specs=in_specs, out_specs=out_specs, check_vma=False
    )
```
